256 devices in a mesh: ctx: 32 (over x_hi, z, core), head: 8 (over y, x_lo).
Axes of the slice: x: 4 (x_hi: 2, x_lo: 2; x = x_hi * 2 + x_lo), y: 4, z: 8, core: 2. Of those that a mesh axis runs over, the one named last changes fastest.
Arguments:
- queries: bfloat16 [8192, 8192], P(('ctx', 'head')), may hold values from -5 to 5
- keys: bfloat16 [8192, 1024], P(('ctx', 'head')), may hold values from -5 to 5
- values: bfloat16 [8192, 1024], P(('ctx', 'head')), may hold values from -6 to 6
- output_gradient: bfloat16 [8192, 8192], P(('ctx', 'head')), may hold values from -6 to 6
- doc_lengths: int32 [4], replicated, may hold values from 1 to 4096, 8192 in all
- span_of: int32 [32], replicated, may hold values from 0 to 31, each once
Outputs:
- attended: bfloat16 [8192, 8192], P(('ctx', 'head'))
- query_grad: bfloat16 [8192, 8192], P(('ctx', 'head'))
- key_gradient: bfloat16 [8192, 1024], P(('ctx', 'head'))
- value_gradient: bfloat16 [8192, 1024], P(('ctx', 'head'))
The draws below stay inside these ranges and needn't reach their ends.
Inputs may be any that keep to these rules, and one draw needn't show every extreme that they name: `doc_lengths`: the lengths sum to 8192 and the longest is exactly 4096. `span_of`: every span number appears once.
All inputs are finite; a program needn't handle non-finite values.
Results may differ from the reference program's by a relative error of at most 0.024.
Values may be sent and summed in bfloat16 or wider, within the bound.
A program may use at most 64 MiB of HBM per device.

```python
import math
import jax
import jax.numpy as jnp
import numpy as np
from jax import lax

QUERY_HEADS = 64
KEY_VALUE_HEADS = 8
HEAD_WIDTH = 128
TOK_DEV = 256
PACK_TOKENS = 8192
LONGEST_DOC_LEN = 4096
DOCS = 4
N_CTX = 32


def draw_queries(key, part):
    key = jax.random.fold_in(key, 1)
    random_jitter = jax.random.normal(key, (PACK_TOKENS, KEY_VALUE_HEADS, QUERY_HEADS // KEY_VALUE_HEADS, HEAD_WIDTH), jnp.float32)
    random_jitter = jnp.clip(random_jitter, -4.0, 4.0)
    return random_jitter.reshape(PACK_TOKENS, QUERY_HEADS * HEAD_WIDTH).astype(jnp.bfloat16)


def draw_keys(key, part):
    key = jax.random.fold_in(key, 2)
    random_jitter = jax.random.normal(key, (PACK_TOKENS, KEY_VALUE_HEADS, HEAD_WIDTH), jnp.float32)
    random_jitter = jnp.clip(random_jitter, -4.0, 4.0)
    return random_jitter.reshape(PACK_TOKENS, KEY_VALUE_HEADS * HEAD_WIDTH).astype(jnp.bfloat16)


def steps_of(stream_key, dims, shards, smallest, largest):
    gain, own = 1.0, jax.random.fold_in(stream_key, 6)
    for axis_at, parts in shards:
        steps = jnp.exp(jax.random.uniform(jax.random.fold_in(own, axis_at), (parts,), jnp.float32, smallest / len(shards), largest / len(shards)))
        gain = gain * jnp.repeat(steps, dims[axis_at] // parts).reshape([-1 if axis == axis_at else 1 for axis in range(len(dims))])
    return gain


def profile(amount, total, reach, skew):
    portions = [(1 << 20) // math.isqrt(rank ** skew) + 1 for rank in range(2, amount + 1)]
    surplus, counts = total - reach - (amount - 1), [1] * (amount - 1)
    while surplus > 0:
        candidates = [i for i in range(amount - 1) if counts[i] < reach]
        whole, budget = sum([portions[i] for i in candidates]), surplus
        for i in candidates:
            more = min(reach - counts[i], max(1, budget * portions[i] // whole), surplus)
            counts[i] = counts[i] + more
            surplus = surplus - more
    return np.array([reach] + counts)


def uneven(rng, number_of, total, limit, lean):
    if number_of == 2:
        one = jax.random.randint(rng, (), max(1, total - limit), min(limit, total - 1) + 1)
        return jnp.stack([one, total - one])
    sizes = jnp.asarray(profile(number_of, total, limit, lean), jnp.int32)
    pairs = (number_of - 1) // 2
    source_of, receiver = sizes[1:1 + 2 * pairs:2], sizes[2:2 + 2 * pairs:2]
    room = jnp.minimum(source_of - 1, limit - receiver)
    moved = jax.random.randint(jax.random.fold_in(rng, 1), (pairs,), 0, 1 << 20) % (room + 1)
    sizes = sizes.at[1:1 + 2 * pairs:2].set(source_of - moved).at[2:2 + 2 * pairs:2].set(receiver + moved)
    return sizes[jax.random.permutation(jax.random.fold_in(rng, 2), number_of)]


def noise(key, dims, spread, limit, split=(), kind=jnp.bfloat16):
    array = spread * jax.random.normal(key, dims, jnp.float32)
    if split:
        array = array * steps_of(key, dims, split, -0.22, 0.18)
    return jnp.clip(array, -limit, limit).astype(kind)


def setup_inputs(seed: int = 0) -> dict:
    key_list = jax.random.split(jax.random.key(seed), 7)
    queries = draw_queries(jax.random.fold_in(key_list[6], 71), 0)
    keys = draw_keys(jax.random.fold_in(key_list[6], 71), 0)
    values = noise(key_list[2], (PACK_TOKENS, KEY_VALUE_HEADS * HEAD_WIDTH), 1.0, 6.0, ((0, 256),))
    output_gradient = noise(key_list[3], (PACK_TOKENS, QUERY_HEADS * HEAD_WIDTH), 1.0, 6.0, ((0, 256),))
    doc_lengths = uneven(key_list[4], DOCS, PACK_TOKENS, LONGEST_DOC_LEN, 2).astype(jnp.int32)
    span_of = jax.random.permutation(key_list[5], N_CTX).astype(jnp.int32)
    return dict(queries=queries, keys=keys, values=values, output_gradient=output_gradient, doc_lengths=doc_lengths, span_of=span_of)


NEG = -1.0e30


def doc_index(positions, doc_ends):
    return jnp.sum((positions[:, None] >= doc_ends[None, :]).astype(jnp.int32), axis=1)


def reference(queries, keys, values, output_gradient, doc_lengths, span_of):
    heads_per_group = QUERY_HEADS // KEY_VALUE_HEADS
    score_scale = HEAD_WIDTH ** -0.5
    row_ids = jnp.arange(PACK_TOKENS, dtype=jnp.int32)
    holder = jnp.zeros((N_CTX,), jnp.int32).at[span_of].set(jnp.arange(N_CTX, dtype=jnp.int32))
    sequence_rows = holder[row_ids // TOK_DEV] * TOK_DEV + row_ids % TOK_DEV
    row_location = span_of[row_ids // TOK_DEV] * TOK_DEV + row_ids % TOK_DEV
    doc_ends = jnp.cumsum(doc_lengths).astype(jnp.int32)
    doc_of = doc_index(row_ids, doc_ends)
    doc_padded = jnp.concatenate([jnp.full((LONGEST_DOC_LEN,), -1, jnp.int32), doc_of])
    query_sequence = jnp.transpose(queries[sequence_rows].reshape(PACK_TOKENS, KEY_VALUE_HEADS, heads_per_group, HEAD_WIDTH), (1, 0, 2, 3))
    gradient_sequence = jnp.transpose(output_gradient[sequence_rows].reshape(PACK_TOKENS, KEY_VALUE_HEADS, heads_per_group, HEAD_WIDTH), (1, 0, 2, 3))
    padding_rows = jnp.zeros((LONGEST_DOC_LEN, KEY_VALUE_HEADS, HEAD_WIDTH), keys.dtype)
    key_sequence = jnp.transpose(jnp.concatenate([padding_rows, keys[sequence_rows].reshape(PACK_TOKENS, KEY_VALUE_HEADS, HEAD_WIDTH)]), (1, 0, 2))
    value_sequence = jnp.transpose(jnp.concatenate([padding_rows, values[sequence_rows].reshape(PACK_TOKENS, KEY_VALUE_HEADS, HEAD_WIDTH)]), (1, 0, 2))
    window = TOK_DEV + LONGEST_DOC_LEN
    offsets = jnp.arange(TOK_DEV, dtype=jnp.int32)
    window_offsets = jnp.arange(window, dtype=jnp.int32)

    def one_group(arrays):
        query_g, key_g, value_g, grad_g = arrays

        def block_step(carried, block_index):
            key_acc, value_acc = carried
            row_start = (block_index * TOK_DEV).astype(jnp.int32)
            query_b = lax.dynamic_slice_in_dim(query_g, row_start, TOK_DEV, 0).astype(jnp.float32)
            grad_b = lax.dynamic_slice_in_dim(grad_g, row_start, TOK_DEV, 0).astype(jnp.float32)
            key_w = lax.dynamic_slice_in_dim(key_g, row_start, window, 0).astype(jnp.float32)
            value_w = lax.dynamic_slice_in_dim(value_g, row_start, window, 0).astype(jnp.float32)
            query_pos = row_start + offsets
            query_doc = lax.dynamic_slice_in_dim(doc_of, row_start, TOK_DEV, 0)
            key_pos = row_start - LONGEST_DOC_LEN + window_offsets
            key_doc = lax.dynamic_slice_in_dim(doc_padded, row_start, window, 0)
            allowed = (key_pos[None, :] <= query_pos[:, None]) & (key_doc[None, :] == query_doc[:, None])
            scores = jnp.einsum("qhd,kd->hqk", query_b, key_w) * score_scale
            scores = jnp.where(allowed, scores, NEG)
            row_max = jnp.max(scores, axis=2, keepdims=True)
            row_total = jnp.sum(jnp.where(allowed, jnp.exp(scores - row_max), 0.0), axis=2, keepdims=True)
            log_total = row_max + jnp.log(row_total)
            weights = jnp.where(allowed, jnp.exp(scores - log_total), 0.0).astype(jnp.bfloat16)
            weights_f = lax.optimization_barrier(weights).astype(jnp.float32)
            attended_b = jnp.einsum("hqk,kd->qhd", weights_f, value_w).astype(jnp.bfloat16)
            row_delta = jnp.sum(grad_b * attended_b.astype(jnp.float32), axis=2)
            prob_grad = jnp.einsum("qhd,kd->hqk", grad_b, value_w)
            score_grad = (weights_f * (prob_grad - jnp.transpose(row_delta)[:, :, None])).astype(jnp.bfloat16)
            score_grad_f = lax.optimization_barrier(score_grad).astype(jnp.float32)
            query_part = (score_scale * jnp.einsum("hqk,kd->qhd", score_grad_f, key_w)).astype(jnp.bfloat16)
            key_part = score_scale * jnp.einsum("hqk,qhd->kd", score_grad_f, query_b)
            value_part = jnp.einsum("hqk,qhd->kd", weights_f, grad_b)
            key_acc = lax.dynamic_update_slice_in_dim(key_acc, lax.dynamic_slice_in_dim(key_acc, row_start, window, 0) + key_part, row_start, 0)
            value_acc = lax.dynamic_update_slice_in_dim(value_acc, lax.dynamic_slice_in_dim(value_acc, row_start, window, 0) + value_part, row_start, 0)
            return (key_acc, value_acc), (attended_b, query_part)

        zeros_kv = jnp.zeros((LONGEST_DOC_LEN + PACK_TOKENS, HEAD_WIDTH), jnp.float32)
        (key_acc, value_acc), (attended_g, query_grad_g) = lax.scan(block_step, (zeros_kv, zeros_kv), jnp.arange(PACK_TOKENS // TOK_DEV, dtype=jnp.int32))
        attended_g = attended_g.reshape(PACK_TOKENS, heads_per_group, HEAD_WIDTH)
        query_grad_g = query_grad_g.reshape(PACK_TOKENS, heads_per_group, HEAD_WIDTH)
        return attended_g, query_grad_g, key_acc[LONGEST_DOC_LEN:], value_acc[LONGEST_DOC_LEN:]

    attended_s, query_grad_s, key_gradient_sorted, value_gradient_sorted = lax.map(one_group, (query_sequence, key_sequence, value_sequence, gradient_sequence))
    attended = jnp.transpose(attended_s, (1, 0, 2, 3)).reshape(PACK_TOKENS, QUERY_HEADS * HEAD_WIDTH)[row_location]
    query_grad = jnp.transpose(query_grad_s, (1, 0, 2, 3)).reshape(PACK_TOKENS, QUERY_HEADS * HEAD_WIDTH)[row_location]
    key_gradient = jnp.transpose(key_gradient_sorted, (1, 0, 2)).reshape(PACK_TOKENS, KEY_VALUE_HEADS * HEAD_WIDTH)[row_location].astype(jnp.bfloat16)
    value_gradient = jnp.transpose(value_gradient_sorted, (1, 0, 2)).reshape(PACK_TOKENS, KEY_VALUE_HEADS * HEAD_WIDTH)[row_location].astype(jnp.bfloat16)
    return (attended, query_grad, key_gradient, value_gradient)
```

```python
import functools
import math

import jax
import jax.numpy as jnp
from jax import lax
from jax.experimental import pallas as pl
from jax.experimental.pallas import tpu as pltpu
from jax.sharding import PartitionSpec as P

N_CTX = 32
SPAN = 256
WIDTH = 128
UNIT_HEADS = 4
UNITS = 2
MAX_BLOCKS = 17
SCALE = WIDTH**-0.5
LOG2_SCALE = SCALE * math.log2(math.e)
NEG = -1e30


def attention_kernel(
    span_ref, len_ref, unit_ref, q_hbm, do_hbm, kv_hbm,
    o_hbm, dq_hbm, dkv_hbm,
    holder, q_v, do_v, kv_v, o_v, dq_v, acc, dkv_v, scores, probs,
    q_t, do_t, do_s, o_t, dq_t, top, total, sem, out_sem,
):
    load_q = pltpu.make_async_copy(q_hbm, q_v, sem.at[0])
    load_do = pltpu.make_async_copy(do_hbm, do_v, sem.at[1])
    load_kv = pltpu.make_async_copy(kv_hbm, kv_v, sem.at[2])
    load_q.start()
    load_kv.start()
    load_do.start()

    def note(c, _):
        holder[span_ref[c]] = c
        return 0

    lax.fori_loop(0, N_CTX, note, 0)

    def clear(c, _):
        acc[c] = jnp.zeros((2, SPAN, WIDTH), jnp.float32)
        return 0

    lax.fori_loop(0, N_CTX, clear, 0)
    load_q.wait()
    load_do.wait()
    load_kv.wait()

    ends = []
    running = jnp.int32(0)
    for j in range(4):
        running = running + len_ref[j]
        ends.append(running)

    def doc_start(pos):
        start = jnp.zeros_like(pos)
        for end in ends:
            start = jnp.where(pos >= end, end, start)
        return start

    def unit(u, _):
        span = span_ref[unit_ref[u]]
        first_pos = span * SPAN
        first_block = doc_start(first_pos) // SPAN
        last_start = doc_start(first_pos + (SPAN - 1))
        blocks = span - first_block + 1
        q_pos = first_pos + lax.broadcasted_iota(jnp.int32, (1, SPAN), 1)
        q_start = doc_start(q_pos)

        for h in range(UNIT_HEADS):
            cols = pl.ds(h * WIDTH, WIDTH)
            q_t[h] = q_v[u, :, cols].T
            do_t[h] = do_v[u, :, cols].T
            top[h] = jnp.full((8, SPAN), NEG, jnp.float32)
            total[h] = jnp.zeros((8, SPAN), jnp.float32)
            o_t[h] = jnp.zeros((WIDTH, SPAN), jnp.float32)
            dq_t[h] = jnp.zeros((WIDTH, SPAN), jnp.float32)

        def score_block(i, masked):
            t = first_block + i
            k = kv_v[holder[t], 0]
            if masked:
                k_pos = t * SPAN + lax.broadcasted_iota(jnp.int32, (SPAN, SPAN), 0)
                allowed = (k_pos <= q_pos) & (k_pos >= q_start)
            for h in range(UNIT_HEADS):
                s = jnp.dot(k, q_t[h], preferred_element_type=jnp.float32)
                if masked:
                    s = jnp.where(allowed, s, NEG)
                scores[i, h] = s
                top[h] = jnp.maximum(top[h], jnp.max(s.reshape(SPAN // 8, 8, SPAN), axis=0))

        def score_step(i, _):
            t = first_block + i
            edge = (t == span) | (t * SPAN < last_start)

            @pl.when(edge)
            def _():
                score_block(i, True)

            @pl.when(jnp.logical_not(edge))
            def _():
                score_block(i, False)

            return 0

        lax.fori_loop(0, blocks, score_step, 0)
        for h in range(UNIT_HEADS):
            top[h] = jnp.broadcast_to(jnp.max(top[h], axis=0, keepdims=True), (8, SPAN))

        def weight_step(i, _):
            v_t = kv_v[holder[first_block + i], 1].T
            for h in range(UNIT_HEADS):
                p = jnp.exp2((scores[i, h] - top[h, 0:1]) * LOG2_SCALE)
                total[h] += jnp.sum(p.reshape(SPAN // 8, 8, SPAN), axis=0)
                p = p.astype(jnp.bfloat16)
                probs[i, h] = p
                o_t[h] += jnp.dot(v_t, p, preferred_element_type=jnp.float32)
            return 0

        lax.fori_loop(0, blocks, weight_step, 0)

        for h in range(UNIT_HEADS):
            cols = pl.ds(h * WIDTH, WIDTH)
            inverse = 1.0 / jnp.sum(total[h], axis=0, keepdims=True)
            out = (o_t[h] * inverse).astype(jnp.bfloat16)
            o_v[u, :, cols] = out.T
            scaled = (do_t[h].astype(jnp.float32) * inverse).astype(jnp.bfloat16)
            do_t[h] = scaled
            do_s[h] = scaled.T
            delta = jnp.sum(scaled.astype(jnp.float32) * out.astype(jnp.float32), axis=0, keepdims=True)
            total[h] = jnp.broadcast_to(delta, (8, SPAN))

        def grad_step(i, _):
            c = holder[first_block + i]
            k = kv_v[c, 0]
            v = kv_v[c, 1]
            k_t = k.T
            dk = jnp.zeros((SPAN, WIDTH), jnp.float32)
            dv = jnp.zeros((SPAN, WIDTH), jnp.float32)
            for h in range(UNIT_HEADS):
                p = probs[i, h]
                dp = jnp.dot(v, do_t[h], preferred_element_type=jnp.float32)
                dv += jnp.dot(p, do_s[h], preferred_element_type=jnp.float32)
                ds = (p.astype(jnp.float32) * (dp - total[h, 0:1])).astype(jnp.bfloat16)
                dk += jnp.dot(ds, q_v[u, :, pl.ds(h * WIDTH, WIDTH)], preferred_element_type=jnp.float32)
                dq_t[h] += jnp.dot(k_t, ds, preferred_element_type=jnp.float32)
            acc[c, 0] += dk * SCALE
            acc[c, 1] += dv
            return 0

        lax.fori_loop(0, blocks, grad_step, 0)
        for h in range(UNIT_HEADS):
            dq_v[u, :, pl.ds(h * WIDTH, WIDTH)] = (dq_t[h] * SCALE).astype(jnp.bfloat16).T
        return 0

    lax.fori_loop(0, UNITS, unit, 0)
    save_o = pltpu.make_async_copy(o_v, o_hbm, out_sem.at[0])
    save_dq = pltpu.make_async_copy(dq_v, dq_hbm, out_sem.at[1])
    save_o.start()
    save_dq.start()

    def pack(c, _):
        dkv_v[c] = acc[c].astype(jnp.bfloat16)
        return 0

    lax.fori_loop(0, N_CTX, pack, 0)
    save_dkv = pltpu.make_async_copy(dkv_v, dkv_hbm, out_sem.at[2])
    save_dkv.start()
    save_o.wait()
    save_dq.wait()
    save_dkv.wait()


def attention(q, do, kv, span_of, doc_lengths, unit_ctx):
    rows = jax.ShapeDtypeStruct((UNITS, SPAN, UNIT_HEADS * WIDTH), jnp.bfloat16)
    blocks = jax.ShapeDtypeStruct((N_CTX, 2, SPAN, WIDTH), jnp.bfloat16)
    smem = pl.BlockSpec(memory_space=pltpu.SMEM)
    hbm = pl.BlockSpec(memory_space=pl.ANY)
    vmem = pltpu.VMEM
    head_t = (UNIT_HEADS, WIDTH, SPAN)
    return pl.pallas_call(
        attention_kernel,
        out_shape=(rows, rows, blocks),
        in_specs=[smem, smem, smem, hbm, hbm, hbm],
        out_specs=(hbm, hbm, hbm),
        scratch_shapes=[
            pltpu.SMEM((N_CTX,), jnp.int32),
            vmem(rows.shape, jnp.bfloat16),
            vmem(rows.shape, jnp.bfloat16),
            vmem(blocks.shape, jnp.bfloat16),
            vmem(rows.shape, jnp.bfloat16),
            vmem(rows.shape, jnp.bfloat16),
            vmem(blocks.shape, jnp.float32),
            vmem(blocks.shape, jnp.bfloat16),
            vmem((MAX_BLOCKS, UNIT_HEADS, SPAN, SPAN), jnp.float32),
            vmem((MAX_BLOCKS, UNIT_HEADS, SPAN, SPAN), jnp.bfloat16),
            vmem(head_t, jnp.bfloat16),
            vmem(head_t, jnp.bfloat16),
            vmem((UNIT_HEADS, SPAN, WIDTH), jnp.bfloat16),
            vmem(head_t, jnp.float32),
            vmem(head_t, jnp.float32),
            vmem((UNIT_HEADS, 8, SPAN), jnp.float32),
            vmem((UNIT_HEADS, 8, SPAN), jnp.float32),
            pltpu.SemaphoreType.DMA((3,)),
            pltpu.SemaphoreType.DMA((3,)),
        ],
        compiler_params=pltpu.CompilerParams(vmem_limit_bytes=60 * 1024 * 1024),
        name="attention",
    )(span_of, doc_lengths, unit_ctx, q, do, kv)


MESH_IDS = pl.DeviceIdType.MESH


def place(z_size):
    ctx, head = lax.axis_index("ctx"), lax.axis_index("head")
    return ctx, head, ctx // (2 * z_size), (ctx // 2) % z_size, ctx % 2


def meet(group, ctx, head, core, heads, others):
    barrier = pltpu.get_barrier_semaphore()
    base = ctx - core

    def greet(step, _):
        peer = (core * heads + head + step) % group
        pl.semaphore_signal(
            barrier, inc=1, device_id=(base + peer // heads, peer % heads), device_id_type=MESH_IDS
        )
        return 0

    lax.fori_loop(1, group, greet, 0)
    for other in others:
        pl.semaphore_signal(barrier, inc=1, device_id=(other, head), device_id_type=MESH_IDS)
    pl.semaphore_wait(barrier, group - 1 + len(others))


def arrived(ref, sem):
    pltpu.make_async_copy(ref, ref, sem).wait()


def send(src, dst, send_sem, recv_sem, ctx, head):
    pltpu.make_async_remote_copy(
        src_ref=src, dst_ref=dst, send_sem=send_sem, recv_sem=recv_sem,
        device_id=(ctx, head), device_id_type=MESH_IDS,
    ).start()


def gather_kernel(
    z_size, heads,
    q_in, do_in, k_in, v_in, q_out, do_out, kv_out,
    row_send, row_recv, piece_send, piece_recv, ring_send, right_recv, left_recv,
    cross_recv, twin_send, twin_recv, local_sem,
):
    ctx, head, x, z, core = place(z_size)
    group = 2 * heads
    base = ctx - core
    mine = core * heads + head
    wide = q_in.shape[1] // group

    def index(x_at, z_at):
        return (x_at * z_size + z_at) * 2 + core

    right, left = index(x, (z + 1) % z_size), index(x, (z + z_size - 1) % z_size)
    cross, twin = index(1 - x, z), base + 1 - core
    meet(group, ctx, head, core, heads, (right, left, cross))

    def piece_cols(at):
        return pl.ds(pl.multiple_of(at * WIDTH, WIDTH), WIDTH)

    def row_cols(at):
        peer_core, peer_head = at // heads, at % heads
        return pl.ds(pl.multiple_of((peer_head * 2 + peer_core) * wide, WIDTH), wide)

    def send_pieces(step, _):
        peer = (head + step) % heads
        for side, ref in enumerate((k_in, v_in)):
            send(
                ref.at[:, piece_cols(peer)], kv_out.at[ctx, side, head],
                piece_send, piece_recv, ctx, peer,
            )
        return 0

    lax.fori_loop(1, heads, send_pieces, 0)
    own = []
    for side, ref in enumerate((k_in, v_in)):
        own.append(
            pltpu.make_async_copy(ref.at[:, piece_cols(head)], kv_out.at[ctx, side, head], local_sem.at[side])
        )
        own[-1].start()

    def send_rows(src, dst, which):
        def step_rows(step, _):
            peer = (mine + step) % group
            send(
                src.at[:, row_cols(peer)], dst.at[mine],
                row_send.at[which], row_recv.at[which], base + peer // heads, peer % heads,
            )
            return 0

        lax.fori_loop(1, group, step_rows, 0)
        copy = pltpu.make_async_copy(src.at[:, row_cols(mine)], dst.at[mine], local_sem.at[2 + which])
        copy.start()
        own.append(copy)

    send_rows(q_in, q_out, 0)
    own[0].wait()
    own[1].wait()
    pieces = kv_out.at[ctx, :, pl.ds(0, heads - 1)]
    arrived(pieces, piece_recv)

    sent = []

    def forward(block, to, recv):
        sem = ring_send.at[len(sent)]
        send(kv_out.at[block], kv_out.at[block], sem, recv, to, head)
        sent.append((block, sem))

    def share(block):
        send(kv_out.at[block], kv_out.at[block], twin_send, twin_recv, twin, head)

    far = z_size // 2
    reach = ((far, far - 1), (far - 1, far))
    forward(ctx, cross, cross_recv)
    forward(ctx, right, right_recv.at[0, 0])
    forward(ctx, left, left_recv.at[0, 0])
    share(ctx)
    send_rows(do_in, do_out, 1)
    arrived(kv_out.at[cross], cross_recv)
    forward(cross, right, right_recv.at[1, 0])
    forward(cross, left, left_recv.at[1, 0])
    share(cross)
    for d in range(1, far + 1):
        for plane in range(2):
            at_x = x if plane == 0 else 1 - x
            for way in range(2):
                if d > reach[plane][way]:
                    continue
                recv, to = ((right_recv, right), (left_recv, left))[way]
                origin = (z + z_size - d) % z_size if way == 0 else (z + d) % z_size
                block = index(at_x, origin)
                arrived(kv_out.at[block], recv.at[plane, d - 1])
                if d < reach[plane][way]:
                    forward(block, to, recv.at[plane, d])
                share(block)

    arrived(pieces, piece_send)
    for block, sem in sent:
        arrived(kv_out.at[block], sem)
    half = kv_out.at[pl.ds(0, 2 * z_size)]
    arrived(half, twin_send)
    arrived(half, twin_recv)
    for which, dst in enumerate((q_out, do_out)):
        own[2 + which].wait()
        rows = dst.at[pl.ds(0, group - 1)]
        arrived(rows, row_send.at[which])
        arrived(rows, row_recv.at[which])


def gather(q, do, k, v, z_size, heads):
    tokens = q.shape[0]
    group = 2 * heads
    far = z_size // 2
    rows = jax.ShapeDtypeStruct((group, tokens, q.shape[1] // group), q.dtype)
    kv = jax.ShapeDtypeStruct((4 * z_size, 2, heads, tokens, WIDTH), q.dtype)
    hbm = pl.BlockSpec(memory_space=pl.ANY)
    dma = pltpu.SemaphoreType.DMA
    return pl.pallas_call(
        functools.partial(gather_kernel, z_size, heads),
        out_shape=(rows, rows, kv),
        in_specs=[hbm] * 4,
        out_specs=(hbm, hbm, hbm),
        scratch_shapes=[
            dma((2,)), dma((2,)), dma, dma, dma((4 * far - 2 + 1,)), dma((2, far)), dma((2, far)),
            dma, dma, dma, dma((4,)),
        ],
        compiler_params=pltpu.CompilerParams(collective_id=0, has_side_effects=True),
        name="gather",
    )(q, do, k, v)


def scatter_kernel(
    z_size, heads,
    o_in, dq_in, dkv_in, o_out, dq_out, dk_out, dv_out,
    part, twin_part, right_part, left_part, cross_part,
    row_send, row_recv, piece_send, piece_recv, ring_send, right_recv, left_recv,
    cross_recv, twin_send, twin_recv, local_sem,
):
    ctx, head, x, z, core = place(z_size)
    group = 2 * heads
    base = ctx - core
    mine = core * heads + head
    wide = o_in.shape[2]

    def index(x_at, z_at):
        return (x_at * z_size + z_at) * 2 + core

    right, left = index(x, (z + 1) % z_size), index(x, (z + z_size - 1) % z_size)
    cross, twin = index(1 - x, z), base + 1 - core
    meet(group, ctx, head, core, heads, (right, left, cross))

    load = pltpu.make_async_copy(dkv_in.at[:, core], part, local_sem.at[0])
    load.start()

    far = z_size // 2
    reach = ((far, far - 1), (far - 1, far))
    steps = []
    for back in range(far):
        for plane, way in ((0, 0), (1, 1), (1, 0), (0, 1)):
            d = reach[plane][way] - back
            if d > 0:
                steps.append((plane, way, d, back))

    def slot(plane, way, d):
        at_x = x if plane == 0 else 1 - x
        at_z = (z + d) % z_size if way == 0 else (z + z_size - d) % z_size
        return at_x * z_size + at_z

    order = [slot(plane, way, d) for plane, way, d, _ in steps]
    order += [slot(1, 0, 0), slot(0, 0, 0)]
    for n, block in enumerate(order):
        send(dkv_in.at[block, 1 - core], twin_part.at[block], twin_send, twin_recv.at[n], twin, head)

    def row_cols(at):
        return pl.ds(pl.multiple_of(((at % heads) * 2 + at // heads) * wide, WIDTH), wide)

    own = []

    def send_rows(src, dst, which):
        def step_rows(step, _):
            peer = (mine + step) % group
            send(
                src.at[peer], dst.at[:, row_cols_mine],
                row_send.at[which], row_recv.at[which], base + peer // heads, peer % heads,
            )
            return 0

        row_cols_mine = row_cols(mine)
        lax.fori_loop(1, group, step_rows, 0)
        copy = pltpu.make_async_copy(src.at[mine], dst.at[:, row_cols_mine], local_sem.at[1 + which])
        copy.start()
        own.append(copy)

    def combine(block, extras):
        def add_half(side, _):
            total = part[block, side].astype(jnp.float32) + twin_part[block, side].astype(jnp.float32)
            for ref, at in extras:
                total = total + ref[at + (side,)].astype(jnp.float32)
            part[block, side] = total.astype(part.dtype)
            return 0

        lax.fori_loop(0, 2, add_half, 0)

    load.wait()
    sent = []
    for n, (plane, way, d, back) in enumerate(steps):
        if n == min(4, len(steps) - 1):
            send_rows(o_in, o_out, 0)
        block = order[n]
        recv, buf, to = ((right_recv, right_part, right), (left_recv, left_part, left))[way]
        arrived(twin_part.at[block], twin_recv.at[n])
        extras = []
        if back > 0:
            arrived(buf.at[plane, back - 1], recv.at[plane, back - 1])
            extras = [(buf, (plane, back - 1))]
        combine(block, extras)
        send(part.at[block], buf.at[plane, back], ring_send.at[n], recv.at[plane, back], to, head)
        sent.append((block, ring_send.at[n]))
        if n == min(7, len(steps) - 1):
            send_rows(dq_in, dq_out, 1)
    for plane in (1, 0):
        n = len(steps) + 1 - plane
        block = order[n]
        arrived(twin_part.at[block], twin_recv.at[n])
        last_right, last_left = reach[plane][0] - 1, reach[plane][1] - 1
        arrived(right_part.at[plane, last_right], right_recv.at[plane, last_right])
        arrived(left_part.at[plane, last_left], left_recv.at[plane, last_left])
        extras = [(right_part, (plane, last_right)), (left_part, (plane, last_left))]
        if plane == 0:
            arrived(cross_part.at[0], cross_recv)
            extras.append((cross_part, (0,)))
        combine(block, extras)
        if plane == 1:
            send(part.at[block], cross_part.at[0], ring_send.at[n], cross_recv, cross, head)
            sent.append((block, ring_send.at[n]))

    final = order[-1]
    my_cols = pl.ds(pl.multiple_of(head * WIDTH, WIDTH), WIDTH)

    def send_pieces(step, _):
        peer = (head + step) % heads
        for side, dst in enumerate((dk_out, dv_out)):
            send(part.at[final, side, peer], dst.at[:, my_cols], piece_send, piece_recv.at[side], ctx, peer)
        return 0

    lax.fori_loop(1, heads, send_pieces, 0)
    for side, dst in enumerate((dk_out, dv_out)):
        copy = pltpu.make_async_copy(part.at[final, side, head], dst.at[:, my_cols], local_sem.at[3 + side])
        copy.start()
        own.append(copy)

    for copy in own:
        copy.wait()
    for block, sem in sent:
        arrived(part.at[block], sem)
    arrived(part.at[pl.ds(0, 2 * z_size)], twin_send)
    for which, dst in enumerate((o_out, dq_out)):
        rows = dst.at[:, pl.ds(0, (group - 1) * wide)]
        arrived(rows, row_send.at[which])
        arrived(rows, row_recv.at[which])
    arrived(part.at[final, :, pl.ds(0, heads - 1)], piece_send)
    for side, dst in enumerate((dk_out, dv_out)):
        arrived(dst.at[:, pl.ds(0, (heads - 1) * WIDTH)], piece_recv.at[side])


def scatter(o, dq, dkv, z_size, heads):
    group, tokens, wide = o.shape
    far = z_size // 2
    rows = jax.ShapeDtypeStruct((tokens, group * wide), o.dtype)
    pieces = jax.ShapeDtypeStruct((tokens, heads * WIDTH), o.dtype)
    block = dkv.shape[2:]
    hbm = pl.BlockSpec(memory_space=pl.ANY)
    dma = pltpu.SemaphoreType.DMA
    return pl.pallas_call(
        functools.partial(scatter_kernel, z_size, heads),
        out_shape=(rows, rows, pieces, pieces),
        in_specs=[hbm] * 3,
        out_specs=(hbm,) * 4,
        scratch_shapes=[
            pltpu.VMEM((2 * z_size,) + block, dkv.dtype),
            pltpu.VMEM((2 * z_size,) + block, dkv.dtype),
            pltpu.VMEM((2, far) + block, dkv.dtype),
            pltpu.VMEM((2, far) + block, dkv.dtype),
            pltpu.VMEM((1,) + block, dkv.dtype),
            dma((2,)), dma((2,)), dma, dma((2,)), dma((4 * far - 2 + 1,)), dma((2, far)), dma((2, far)),
            dma, dma, dma((2 * z_size,)), dma((5,)),
        ],
        compiler_params=pltpu.CompilerParams(
            collective_id=1, has_side_effects=True, vmem_limit_bytes=32 * 1024 * 1024
        ),
        name="scatter",
    )(o, dq, dkv)


def per_device(heads, z_size, queries, keys, values, output_gradient, doc_lengths, span_of):
    q, do, kv = gather(queries, output_gradient, keys, values, z_size, heads)
    mine = lax.axis_index("ctx").astype(jnp.int32)
    first = mine - mine % 2
    rows = (UNITS, SPAN, UNIT_HEADS * WIDTH)
    o, dq, dkv = attention(
        q.reshape(rows), do.reshape(rows), kv.reshape(N_CTX, 2, SPAN, WIDTH),
        span_of, doc_lengths, jnp.stack([first, first + 1]),
    )
    dkv = dkv.reshape((N_CTX // 2, 2) + kv.shape[1:])
    return scatter(o.reshape(q.shape), dq.reshape(q.shape), dkv, z_size, heads)


def solution(mesh):
    shard = P(("ctx", "head"), None)
    return jax.shard_map(
        functools.partial(per_device, mesh.shape["head"], N_CTX // 4),
        mesh=mesh,
        in_specs=(shard, shard, shard, shard, P(), P()),
        out_specs=(shard, shard, shard, shard),
        check_vma=False,
    )
```

```python
import functools
import math

import jax
import jax.numpy as jnp
from jax import lax
from jax.experimental import pallas as pl
from jax.experimental.pallas import tpu as pltpu
from jax.sharding import PartitionSpec as P

N_CTX = 32
SPAN = 256
WIDTH = 128
UNIT_HEADS = 4
UNITS = 2
MAX_BLOCKS = 18
COLS = UNIT_HEADS * SPAN
LIMIT = 2.0**60
SCALE = WIDTH**-0.5
LOG2_SCALE = SCALE * math.log2(math.e)
NEG = -1e30


def attention_kernel(
    span_ref, len_ref, q_hbm, do_hbm, kv_hbm,
    o_hbm, dq_hbm, dkv_hbm,
    holder, q_v, do_v, kv_v, o_v, dq_v, acc, dkv_v, probs, grads,
    q_t, do_t, q_s, do_s, o_t, dq_t, top, total, sem, out_sem,
):
    load_q = pltpu.make_async_copy(q_hbm, q_v, sem.at[0])
    load_do = pltpu.make_async_copy(do_hbm, do_v, sem.at[1])
    load_kv = pltpu.make_async_copy(kv_hbm, kv_v, sem.at[2])
    load_q.start()
    load_kv.start()
    load_do.start()
    ctx = lax.axis_index("ctx")
    first_unit = ctx - ctx % UNITS

    def note(c, _):
        holder[span_ref[c]] = c
        return 0

    lax.fori_loop(0, N_CTX, note, 0)

    def clear(c, _):
        acc[c] = jnp.zeros((2, SPAN, WIDTH), jnp.float32)
        return 0

    lax.fori_loop(0, N_CTX, clear, 0)
    load_q.wait()
    load_do.wait()
    load_kv.wait()

    ends = []
    running = jnp.int32(0)
    for j in range(4):
        running = running + len_ref[j]
        ends.append(running)

    def doc_start(pos):
        start = jnp.zeros_like(pos)
        for end in ends:
            start = jnp.where(pos >= end, end, start)
        return start

    def rows_of(i, count=1):
        return pl.ds(pl.multiple_of(i * SPAN, SPAN), count * SPAN)

    def cols_of(h):
        return pl.ds(h * SPAN, SPAN)

    def unit(u, _):
        span = span_ref[first_unit + u]
        first_pos = span * SPAN
        first_block = doc_start(first_pos) // SPAN
        last_start = doc_start(first_pos + (SPAN - 1))
        blocks = span - first_block + 1
        edges = jnp.maximum(jnp.minimum((last_start + (SPAN - 1)) // SPAN, span) - first_block, 0)
        q_pos = first_pos + lax.broadcasted_iota(jnp.int32, (1, SPAN), 1)
        q_start = doc_start(q_pos)

        for h in range(UNIT_HEADS):
            lanes = pl.ds(h * WIDTH, WIDTH)
            q_h = q_v[u, :, lanes]
            q_s[cols_of(h)] = q_h
            q_t[h] = q_h.T
            do_t[h] = do_v[u, :, lanes].T

        def clear_totals():
            total[...] = jnp.zeros_like(total)
            o_t[...] = jnp.zeros_like(o_t)

        def allowed_at(t):
            k_pos = t * SPAN + lax.broadcasted_iota(jnp.int32, (SPAN, SPAN), 0)
            return (k_pos <= q_pos) & (k_pos >= q_start)

        def fold(x, reduce):
            return reduce(x.reshape(x.shape[0] // 8, 8, SPAN), axis=0)

        def forward(i, count, masked, take_top=False):
            places = [holder[first_block + i + n] for n in range(count)]
            k = jnp.concatenate([kv_v[c, 0] for c in places], axis=0)
            v_t = jnp.concatenate([kv_v[c, 1] for c in places], axis=0).T
            if masked:
                allowed = allowed_at(first_block + i)
            for h in range(UNIT_HEADS):
                s = jnp.dot(k, q_t[h], preferred_element_type=jnp.float32)
                if masked:
                    s = jnp.where(allowed, s, NEG)
                if take_top:
                    level = jnp.max(fold(s, jnp.max), axis=0, keepdims=True)
                    top[h] = jnp.broadcast_to(level, (8, SPAN))
                else:
                    level = top[h, 0:1]
                p = jnp.exp2((s - level) * LOG2_SCALE)
                total[h] += fold(p, jnp.sum)
                p = p.astype(jnp.bfloat16)
                probs[rows_of(i, count), cols_of(h)] = p
                o_t[h] += jnp.dot(v_t, p, preferred_element_type=jnp.float32)

        def masked_step(i, _):
            forward(i, 1, True)
            return 0

        clear_totals()
        forward(blocks - 1, 1, True, take_top=True)
        lax.fori_loop(0, edges, masked_step, 0)
        inner = blocks - 1 - edges

        def pair_step(j, _):
            forward(edges + 2 * j, 2, False)
            return 0

        lax.fori_loop(0, inner // 2, pair_step, 0)

        @pl.when(inner % 2 == 1)
        def _():
            forward(blocks - 2, 1, False)

        worst = jnp.max(jnp.where(total[...] < LIMIT, 0.0, 1.0))

        @pl.when(worst > 0.0)
        def _():
            clear_totals()
            top[...] = jnp.full_like(top, NEG)

            def top_step(i, _):
                k = kv_v[holder[first_block + i], 0]
                allowed = allowed_at(first_block + i)
                for h in range(UNIT_HEADS):
                    s = jnp.dot(k, q_t[h], preferred_element_type=jnp.float32)
                    top[h] = jnp.maximum(top[h], fold(jnp.where(allowed, s, NEG), jnp.max))
                return 0

            lax.fori_loop(0, blocks, top_step, 0)
            for h in range(UNIT_HEADS):
                top[h] = jnp.broadcast_to(jnp.max(top[h], axis=0, keepdims=True), (8, SPAN))
            lax.fori_loop(0, blocks, masked_step, 0)

        for h in range(UNIT_HEADS):
            lanes = pl.ds(h * WIDTH, WIDTH)
            inverse = 1.0 / jnp.sum(total[h], axis=0, keepdims=True)
            out = (o_t[h] * inverse).astype(jnp.bfloat16)
            o_v[u, :, lanes] = out.T
            scaled = (do_t[h].astype(jnp.float32) * inverse).astype(jnp.bfloat16)
            do_t[h] = scaled
            do_s[cols_of(h)] = scaled.T
            delta = jnp.sum(scaled.astype(jnp.float32) * out.astype(jnp.float32), axis=0, keepdims=True)
            total[h] = jnp.broadcast_to(delta, (8, SPAN))
        dq_t[...] = jnp.zeros_like(dq_t)

        def backward(i, count):
            rows = rows_of(i, count)
            here = pl.ds(0, count * SPAN)
            places = [holder[first_block + i + n] for n in range(count)]
            k_t = jnp.concatenate([kv_v[c, 0] for c in places], axis=0).T
            v = jnp.concatenate([kv_v[c, 1] for c in places], axis=0)
            for h in range(UNIT_HEADS):
                dp = jnp.dot(v, do_t[h], preferred_element_type=jnp.float32)
                p = probs[rows, cols_of(h)].astype(jnp.float32)
                ds = (p * (dp - total[h, 0:1])).astype(jnp.bfloat16)
                grads[here, cols_of(h)] = ds
                dq_t[h] += jnp.dot(k_t, ds, preferred_element_type=jnp.float32)
            dv = jnp.dot(probs[rows], do_s[...], preferred_element_type=jnp.float32)
            dk = jnp.dot(grads[here], q_s[...], preferred_element_type=jnp.float32)
            for n, c in enumerate(places):
                part = slice(n * SPAN, (n + 1) * SPAN)
                acc[c, 0] += dk[part]
                acc[c, 1] += dv[part]

        def grad_step(j, _):
            backward(2 * j, 2)
            return 0

        lax.fori_loop(0, blocks // 2, grad_step, 0)

        @pl.when(blocks % 2 == 1)
        def _():
            backward(blocks - 1, 1)

        for h in range(UNIT_HEADS):
            dq_v[u, :, pl.ds(h * WIDTH, WIDTH)] = (dq_t[h] * SCALE).astype(jnp.bfloat16).T
        return 0

    lax.fori_loop(0, UNITS, unit, 0)
    save_o = pltpu.make_async_copy(o_v, o_hbm, out_sem.at[0])
    save_dq = pltpu.make_async_copy(dq_v, dq_hbm, out_sem.at[1])
    save_o.start()
    save_dq.start()

    def pack(c, _):
        dkv_v[c, 0] = (acc[c, 0] * SCALE).astype(jnp.bfloat16)
        dkv_v[c, 1] = acc[c, 1].astype(jnp.bfloat16)
        pltpu.make_async_copy(dkv_v.at[c], dkv_hbm.at[c], out_sem.at[2]).start()
        return 0

    lax.fori_loop(0, N_CTX, pack, 0)
    save_o.wait()
    save_dq.wait()
    pltpu.make_async_copy(dkv_v, dkv_hbm, out_sem.at[2]).wait()


def attention(q, do, kv, span_of, doc_lengths):
    rows = jax.ShapeDtypeStruct((UNITS, SPAN, UNIT_HEADS * WIDTH), jnp.bfloat16)
    blocks = jax.ShapeDtypeStruct((N_CTX, 2, SPAN, WIDTH), jnp.bfloat16)
    smem = pl.BlockSpec(memory_space=pltpu.SMEM)
    hbm = pl.BlockSpec(memory_space=pl.ANY)
    vmem = pltpu.VMEM
    head_t = (UNIT_HEADS, WIDTH, SPAN)
    return pl.pallas_call(
        attention_kernel,
        out_shape=(rows, rows, blocks),
        in_specs=[smem, smem, hbm, hbm, hbm],
        out_specs=(hbm, hbm, hbm),
        scratch_shapes=[
            pltpu.SMEM((N_CTX,), jnp.int32),
            vmem(rows.shape, jnp.bfloat16),
            vmem(rows.shape, jnp.bfloat16),
            vmem(blocks.shape, jnp.bfloat16),
            vmem(rows.shape, jnp.bfloat16),
            vmem(rows.shape, jnp.bfloat16),
            vmem(blocks.shape, jnp.float32),
            vmem(blocks.shape, jnp.bfloat16),
            vmem((MAX_BLOCKS * SPAN, COLS), jnp.bfloat16),
            vmem((2 * SPAN, COLS), jnp.bfloat16),
            vmem(head_t, jnp.bfloat16),
            vmem(head_t, jnp.bfloat16),
            vmem((COLS, WIDTH), jnp.bfloat16),
            vmem((COLS, WIDTH), jnp.bfloat16),
            vmem(head_t, jnp.float32),
            vmem(head_t, jnp.float32),
            vmem((UNIT_HEADS, 8, SPAN), jnp.float32),
            vmem((UNIT_HEADS, 8, SPAN), jnp.float32),
            pltpu.SemaphoreType.DMA((3,)),
            pltpu.SemaphoreType.DMA((3,)),
        ],
        compiler_params=pltpu.CompilerParams(vmem_limit_bytes=60 * 1024 * 1024),
        name="attention",
    )(span_of, doc_lengths, q, do, kv)


MESH_IDS = pl.DeviceIdType.MESH


def place(z_size):
    ctx, head = lax.axis_index("ctx"), lax.axis_index("head")
    return ctx, head, ctx // (2 * z_size), (ctx // 2) % z_size, ctx % 2


def meet(group, ctx, head, core, heads, others):
    barrier = pltpu.get_barrier_semaphore()
    base = ctx - core

    def greet(step, _):
        peer = (core * heads + head + step) % group
        pl.semaphore_signal(
            barrier, inc=1, device_id=(base + peer // heads, peer % heads), device_id_type=MESH_IDS
        )
        return 0

    lax.fori_loop(1, group, greet, 0)
    for other in others:
        pl.semaphore_signal(barrier, inc=1, device_id=(other, head), device_id_type=MESH_IDS)
    pl.semaphore_wait(barrier, group - 1 + len(others))


def arrived(ref, sem):
    pltpu.make_async_copy(ref, ref, sem).wait()


def send(src, dst, send_sem, recv_sem, ctx, head):
    pltpu.make_async_remote_copy(
        src_ref=src, dst_ref=dst, send_sem=send_sem, recv_sem=recv_sem,
        device_id=(ctx, head), device_id_type=MESH_IDS,
    ).start()


def gather_kernel(
    z_size, heads,
    q_in, do_in, k_in, v_in, q_out, do_out, kv_out,
    row_send, row_recv, piece_send, piece_recv, ring_send, right_recv, left_recv,
    cross_recv, twin_send, twin_recv, local_sem,
):
    ctx, head, x, z, core = place(z_size)
    group = 2 * heads
    base = ctx - core
    mine = core * heads + head
    wide = q_in.shape[1] // group

    def index(x_at, z_at):
        return (x_at * z_size + z_at) * 2 + core

    right, left = index(x, (z + 1) % z_size), index(x, (z + z_size - 1) % z_size)
    cross, twin = index(1 - x, z), base + 1 - core
    meet(group, ctx, head, core, heads, (right, left, cross))

    def piece_cols(at):
        return pl.ds(pl.multiple_of(at * WIDTH, WIDTH), WIDTH)

    def row_cols(at):
        peer_core, peer_head = at // heads, at % heads
        return pl.ds(pl.multiple_of((peer_head * 2 + peer_core) * wide, WIDTH), wide)

    def send_pieces(step, _):
        peer = (head + step) % heads
        for side, ref in enumerate((k_in, v_in)):
            send(
                ref.at[:, piece_cols(peer)], kv_out.at[ctx, side, head],
                piece_send, piece_recv, ctx, peer,
            )
        return 0

    lax.fori_loop(1, heads, send_pieces, 0)
    own = []
    for side, ref in enumerate((k_in, v_in)):
        own.append(
            pltpu.make_async_copy(ref.at[:, piece_cols(head)], kv_out.at[ctx, side, head], local_sem.at[side])
        )
        own[-1].start()

    def send_rows(src, dst, which):
        def step_rows(step, _):
            peer = (mine + step) % group
            send(
                src.at[:, row_cols(peer)], dst.at[mine],
                row_send.at[which], row_recv.at[which], base + peer // heads, peer % heads,
            )
            return 0

        lax.fori_loop(1, group, step_rows, 0)
        copy = pltpu.make_async_copy(src.at[:, row_cols(mine)], dst.at[mine], local_sem.at[2 + which])
        copy.start()
        own.append(copy)

    send_rows(q_in, q_out, 0)
    own[0].wait()
    own[1].wait()
    pieces = kv_out.at[ctx, :, pl.ds(0, heads - 1)]
    arrived(pieces, piece_recv)

    sent = []

    def forward(block, to, recv):
        sem = ring_send.at[len(sent)]
        send(kv_out.at[block], kv_out.at[block], sem, recv, to, head)
        sent.append((block, sem))

    def share(block):
        send(kv_out.at[block], kv_out.at[block], twin_send, twin_recv, twin, head)

    far = z_size // 2
    reach = ((far, far - 1), (far - 1, far))
    forward(ctx, cross, cross_recv)
    forward(ctx, right, right_recv.at[0, 0])
    forward(ctx, left, left_recv.at[0, 0])
    share(ctx)
    send_rows(do_in, do_out, 1)
    arrived(kv_out.at[cross], cross_recv)
    forward(cross, right, right_recv.at[1, 0])
    forward(cross, left, left_recv.at[1, 0])
    share(cross)
    for d in range(1, far + 1):
        for plane in range(2):
            at_x = x if plane == 0 else 1 - x
            for way in range(2):
                if d > reach[plane][way]:
                    continue
                recv, to = ((right_recv, right), (left_recv, left))[way]
                origin = (z + z_size - d) % z_size if way == 0 else (z + d) % z_size
                block = index(at_x, origin)
                arrived(kv_out.at[block], recv.at[plane, d - 1])
                if d < reach[plane][way]:
                    forward(block, to, recv.at[plane, d])
                share(block)

    arrived(pieces, piece_send)
    for block, sem in sent:
        arrived(kv_out.at[block], sem)
    half = kv_out.at[pl.ds(0, 2 * z_size)]
    arrived(half, twin_send)
    arrived(half, twin_recv)
    for which, dst in enumerate((q_out, do_out)):
        own[2 + which].wait()
        rows = dst.at[pl.ds(0, group - 1)]
        arrived(rows, row_send.at[which])
        arrived(rows, row_recv.at[which])


def gather(q, do, k, v, z_size, heads):
    tokens = q.shape[0]
    group = 2 * heads
    far = z_size // 2
    rows = jax.ShapeDtypeStruct((group, tokens, q.shape[1] // group), q.dtype)
    kv = jax.ShapeDtypeStruct((4 * z_size, 2, heads, tokens, WIDTH), q.dtype)
    hbm = pl.BlockSpec(memory_space=pl.ANY)
    dma = pltpu.SemaphoreType.DMA
    return pl.pallas_call(
        functools.partial(gather_kernel, z_size, heads),
        out_shape=(rows, rows, kv),
        in_specs=[hbm] * 4,
        out_specs=(hbm, hbm, hbm),
        scratch_shapes=[
            dma((2,)), dma((2,)), dma, dma, dma((4 * far - 2 + 1,)), dma((2, far)), dma((2, far)),
            dma, dma, dma, dma((4,)),
        ],
        compiler_params=pltpu.CompilerParams(collective_id=0, has_side_effects=True, vmem_limit_bytes=60 * 1024 * 1024),
        name="gather",
    )(q, do, k, v)


def scatter_kernel(
    z_size, heads,
    o_in, dq_in, dkv_in, o_out, dq_out, dk_out, dv_out,
    part, twin_part, right_part, left_part, cross_part,
    row_send, row_recv, piece_send, piece_recv, ring_send, right_recv, left_recv,
    cross_recv, twin_send, twin_recv, local_sem,
):
    ctx, head, x, z, core = place(z_size)
    group = 2 * heads
    base = ctx - core
    mine = core * heads + head
    wide = o_in.shape[2]

    def index(x_at, z_at):
        return (x_at * z_size + z_at) * 2 + core

    right, left = index(x, (z + 1) % z_size), index(x, (z + z_size - 1) % z_size)
    cross, twin = index(1 - x, z), base + 1 - core
    meet(group, ctx, head, core, heads, (right, left, cross))

    load = pltpu.make_async_copy(dkv_in.at[:, core], part, local_sem.at[0])
    load.start()

    far = z_size // 2
    reach = ((far, far - 1), (far - 1, far))
    steps = []
    for back in range(far):
        for plane, way in ((0, 0), (1, 1), (1, 0), (0, 1)):
            d = reach[plane][way] - back
            if d > 0:
                steps.append((plane, way, d, back))

    def slot(plane, way, d):
        at_x = x if plane == 0 else 1 - x
        at_z = (z + d) % z_size if way == 0 else (z + z_size - d) % z_size
        return at_x * z_size + at_z

    order = [slot(plane, way, d) for plane, way, d, _ in steps]
    order += [slot(1, 0, 0), slot(0, 0, 0)]
    for n, block in enumerate(order):
        send(dkv_in.at[block, 1 - core], twin_part.at[block], twin_send, twin_recv.at[n], twin, head)

    def row_cols(at):
        return pl.ds(pl.multiple_of(((at % heads) * 2 + at // heads) * wide, WIDTH), wide)

    own = []

    def send_rows(src, dst, which):
        def step_rows(step, _):
            peer = (mine + step) % group
            send(
                src.at[peer], dst.at[:, row_cols_mine],
                row_send.at[which], row_recv.at[which], base + peer // heads, peer % heads,
            )
            return 0

        row_cols_mine = row_cols(mine)
        lax.fori_loop(1, group, step_rows, 0)
        copy = pltpu.make_async_copy(src.at[mine], dst.at[:, row_cols_mine], local_sem.at[1 + which])
        copy.start()
        own.append(copy)

    def combine(block, extras):
        def add_half(side, _):
            total = part[block, side].astype(jnp.float32) + twin_part[block, side].astype(jnp.float32)
            for ref, at in extras:
                total = total + ref[at + (side,)].astype(jnp.float32)
            part[block, side] = total.astype(part.dtype)
            return 0

        lax.fori_loop(0, 2, add_half, 0)

    load.wait()
    sent = []
    for n, (plane, way, d, back) in enumerate(steps):
        if n == min(4, len(steps) - 1):
            send_rows(o_in, o_out, 0)
        block = order[n]
        recv, buf, to = ((right_recv, right_part, right), (left_recv, left_part, left))[way]
        arrived(twin_part.at[block], twin_recv.at[n])
        extras = []
        if back > 0:
            arrived(buf.at[plane, back - 1], recv.at[plane, back - 1])
            extras = [(buf, (plane, back - 1))]
        combine(block, extras)
        send(part.at[block], buf.at[plane, back], ring_send.at[n], recv.at[plane, back], to, head)
        sent.append((block, ring_send.at[n]))
        if n == min(7, len(steps) - 1):
            send_rows(dq_in, dq_out, 1)
    for plane in (1, 0):
        n = len(steps) + 1 - plane
        block = order[n]
        arrived(twin_part.at[block], twin_recv.at[n])
        last_right, last_left = reach[plane][0] - 1, reach[plane][1] - 1
        arrived(right_part.at[plane, last_right], right_recv.at[plane, last_right])
        arrived(left_part.at[plane, last_left], left_recv.at[plane, last_left])
        extras = [(right_part, (plane, last_right)), (left_part, (plane, last_left))]
        if plane == 0:
            arrived(cross_part.at[0], cross_recv)
            extras.append((cross_part, (0,)))
        combine(block, extras)
        if plane == 1:
            send(part.at[block], cross_part.at[0], ring_send.at[n], cross_recv, cross, head)
            sent.append((block, ring_send.at[n]))

    final = order[-1]
    my_cols = pl.ds(pl.multiple_of(head * WIDTH, WIDTH), WIDTH)

    def send_pieces(step, _):
        peer = (head + step) % heads
        for side, dst in enumerate((dk_out, dv_out)):
            send(part.at[final, side, peer], dst.at[:, my_cols], piece_send, piece_recv.at[side], ctx, peer)
        return 0

    lax.fori_loop(1, heads, send_pieces, 0)
    for side, dst in enumerate((dk_out, dv_out)):
        copy = pltpu.make_async_copy(part.at[final, side, head], dst.at[:, my_cols], local_sem.at[3 + side])
        copy.start()
        own.append(copy)

    for copy in own:
        copy.wait()
    for block, sem in sent:
        arrived(part.at[block], sem)
    arrived(part.at[pl.ds(0, 2 * z_size)], twin_send)
    for which, dst in enumerate((o_out, dq_out)):
        rows = dst.at[:, pl.ds(0, (group - 1) * wide)]
        arrived(rows, row_send.at[which])
        arrived(rows, row_recv.at[which])
    arrived(part.at[final, :, pl.ds(0, heads - 1)], piece_send)
    for side, dst in enumerate((dk_out, dv_out)):
        arrived(dst.at[:, pl.ds(0, (heads - 1) * WIDTH)], piece_recv.at[side])


def scatter(o, dq, dkv, z_size, heads):
    group, tokens, wide = o.shape
    far = z_size // 2
    rows = jax.ShapeDtypeStruct((tokens, group * wide), o.dtype)
    pieces = jax.ShapeDtypeStruct((tokens, heads * WIDTH), o.dtype)
    block = dkv.shape[2:]
    hbm = pl.BlockSpec(memory_space=pl.ANY)
    dma = pltpu.SemaphoreType.DMA
    return pl.pallas_call(
        functools.partial(scatter_kernel, z_size, heads),
        out_shape=(rows, rows, pieces, pieces),
        in_specs=[hbm] * 3,
        out_specs=(hbm,) * 4,
        scratch_shapes=[
            pltpu.VMEM((2 * z_size,) + block, dkv.dtype),
            pltpu.VMEM((2 * z_size,) + block, dkv.dtype),
            pltpu.VMEM((2, far) + block, dkv.dtype),
            pltpu.VMEM((2, far) + block, dkv.dtype),
            pltpu.VMEM((1,) + block, dkv.dtype),
            dma((2,)), dma((2,)), dma, dma((2,)), dma((4 * far - 2 + 1,)), dma((2, far)), dma((2, far)),
            dma, dma, dma((2 * z_size,)), dma((5,)),
        ],
        compiler_params=pltpu.CompilerParams(
            collective_id=1, has_side_effects=True, vmem_limit_bytes=60 * 1024 * 1024
        ),
        name="scatter",
    )(o, dq, dkv)


def settle_kernel(*refs):
    count = len(refs) // 2
    sem = refs[-1]
    copies = [pltpu.make_async_copy(refs[i], refs[count + i], sem.at[i]) for i in range(count)]
    for copy in copies:
        copy.start()
    for copy in copies:
        copy.wait()


def settle(arrays):
    hbm = pl.BlockSpec(memory_space=pl.ANY)
    return pl.pallas_call(
        settle_kernel,
        out_shape=tuple(jax.ShapeDtypeStruct(a.shape, a.dtype) for a in arrays),
        in_specs=[hbm] * len(arrays),
        out_specs=(hbm,) * len(arrays),
        scratch_shapes=[pltpu.SemaphoreType.DMA((len(arrays),))],
        compiler_params=pltpu.CompilerParams(vmem_limit_bytes=60 * 1024 * 1024),
        name="settle",
    )(*arrays)


def per_device(heads, z_size, queries, keys, values, output_gradient, doc_lengths, span_of):
    q, do, kv = gather(queries, output_gradient, keys, values, z_size, heads)
    rows = (UNITS, SPAN, UNIT_HEADS * WIDTH)
    o, dq, dkv = attention(
        q.reshape(rows), do.reshape(rows), kv.reshape(N_CTX, 2, SPAN, WIDTH), span_of, doc_lengths
    )
    dkv = dkv.reshape((N_CTX // 2, 2) + kv.shape[1:])
    return settle(scatter(o.reshape(q.shape), dq.reshape(q.shape), dkv, z_size, heads))


def solution(mesh):
    shard = P(("ctx", "head"), None)
    return jax.shard_map(
        functools.partial(per_device, mesh.shape["head"], N_CTX // 4),
        mesh=mesh,
        in_specs=(shard, shard, shard, shard, P(), P()),
        out_specs=(shard, shard, shard, shard),
        check_vma=False,
    )
```

```python
import functools
import math

import jax
import jax.numpy as jnp
from jax import lax
from jax.experimental import pallas as pl
from jax.experimental.pallas import tpu as pltpu
from jax.sharding import PartitionSpec as P

N_CTX = 32
SPAN = 256
WIDTH = 128
UNIT_HEADS = 4
UNITS = 2
MAX_BLOCKS = 18
COLS = UNIT_HEADS * SPAN
LIMIT = 2.0**60
SCALE = WIDTH**-0.5
LOG2_SCALE = SCALE * math.log2(math.e)
NEG = -1e30


NT = (((1,), (1,)), ((), ()))


def attention_kernel(
    span_ref, len_ref, q_v, do_v, kv_v,
    o_v, dq_v, dkv_v,
    holder, acc, probs, grads, wide_buf,
    q_t, do_t, q_s, do_s, o_acc, dq_acc, level_b, delta_b, starts,
):
    ctx = lax.axis_index("ctx")
    first_unit = ctx - ctx % UNITS

    def note(c, _):
        holder[span_ref[c]] = c
        return 0

    lax.fori_loop(0, N_CTX, note, 0)

    def clear(c, _):
        acc[c] = jnp.zeros((2, WIDTH, SPAN), jnp.float32)
        return 0

    lax.fori_loop(0, N_CTX, clear, 0)

    ends = []
    running = jnp.int32(0)
    for j in range(4):
        running = running + len_ref[j]
        ends.append(running)

    def doc_start(pos):
        start = jnp.zeros_like(pos)
        for end in ends:
            start = jnp.where(pos >= end, end, start)
        return start

    def rows_of(h):
        return pl.ds(h * SPAN, SPAN)

    def lanes_of(h):
        return pl.ds(h * WIDTH, WIDTH)

    def both(x):
        return jnp.concatenate([x, x], axis=1)

    def beside(parts):
        return parts[0] if len(parts) == 1 else jnp.concatenate(parts, axis=1)

    def below(parts):
        return parts[0] if len(parts) == 1 else jnp.concatenate(parts, axis=0)

    ones = jnp.ones((SPAN, WIDTH), jnp.bfloat16)

    def unit(u, _):
        span = span_ref[first_unit + u]
        first_pos = span * SPAN
        first_block = doc_start(first_pos) // SPAN
        last_start = doc_start(first_pos + (SPAN - 1))
        blocks = span - first_block + 1
        edges = jnp.maximum(jnp.minimum((last_start + (SPAN - 1)) // SPAN, span) - first_block, 0)
        starts[...] = doc_start(first_pos + lax.broadcasted_iota(jnp.int32, (SPAN, WIDTH), 0))

        for h in range(UNIT_HEADS):
            q_h = q_v[u, :, lanes_of(h)]
            q_s[rows_of(h)] = q_h
            q_t[:, rows_of(h)] = q_h.T

        def allowed_at(t):
            k_pos = t * SPAN + lax.broadcasted_iota(jnp.int32, (SPAN, SPAN), 1)
            q_pos = first_pos + lax.broadcasted_iota(jnp.int32, (SPAN, SPAN), 0)
            return (k_pos <= q_pos) & (k_pos >= both(starts[...]))

        def halves_max(s):
            return jnp.maximum(s[:, :WIDTH], s[:, WIDTH:])

        def row_max(x):
            return jnp.broadcast_to(jnp.max(x, axis=1, keepdims=True), x.shape)

        def forward(i, count, masked, take_top=False):
            places = [holder[first_block + i + n] for n in range(count)]
            for n, c in enumerate(places):
                wide_buf[n] = lax.dot_general(
                    q_s[...], kv_v[c, 0], NT, preferred_element_type=jnp.float32
                )
            if masked:
                allowed = allowed_at(first_block + i)
            for n in range(count):
                for h in range(UNIT_HEADS):
                    s = wide_buf[n, rows_of(h)]
                    if masked:
                        s = jnp.where(allowed, s, NEG)
                    if take_top:
                        level = row_max(halves_max(s))
                        level_b[rows_of(h)] = level
                    else:
                        level = level_b[rows_of(h)]
                    p = jnp.exp2((s - both(level)) * LOG2_SCALE)
                    probs[i + n, rows_of(h)] = p.astype(jnp.bfloat16)
            values = below([beside([kv_v[c, 1], ones]) for c in places])
            o_acc[...] += jnp.dot(
                beside([probs[i + n] for n in range(count)]), values, preferred_element_type=jnp.float32
            )

        def masked_step(i, _):
            forward(i, 1, True)
            return 0

        o_acc[...] = jnp.zeros_like(o_acc)
        forward(blocks - 1, 1, True, take_top=True)
        lax.fori_loop(0, edges, masked_step, 0)
        inner = blocks - 1 - edges

        def pair_step(j, _):
            forward(edges + 2 * j, 2, False)
            return 0

        lax.fori_loop(0, inner // 2, pair_step, 0)

        @pl.when(inner % 2 == 1)
        def _():
            forward(blocks - 2, 1, False)

        worst = jnp.max(jnp.where(o_acc[:, WIDTH:] < LIMIT, 0.0, 1.0))

        @pl.when(worst > 0.0)
        def _():
            o_acc[...] = jnp.zeros_like(o_acc)
            level_b[...] = jnp.full_like(level_b, NEG)

            def top_step(i, _):
                k = kv_v[holder[first_block + i], 0]
                allowed = allowed_at(first_block + i)
                for h in range(UNIT_HEADS):
                    s = lax.dot_general(q_s[rows_of(h)], k, NT, preferred_element_type=jnp.float32)
                    s = jnp.where(allowed, s, NEG)
                    level_b[rows_of(h)] = jnp.maximum(level_b[rows_of(h)], halves_max(s))
                return 0

            lax.fori_loop(0, blocks, top_step, 0)
            for h in range(UNIT_HEADS):
                level_b[rows_of(h)] = row_max(level_b[rows_of(h)])
            lax.fori_loop(0, blocks, masked_step, 0)

        for h in range(UNIT_HEADS):
            inverse = 1.0 / o_acc[rows_of(h), WIDTH:]
            out = (o_acc[rows_of(h), :WIDTH] * inverse).astype(jnp.bfloat16)
            o_v[u, :, lanes_of(h)] = out
            scaled = (do_v[u, :, lanes_of(h)].astype(jnp.float32) * inverse).astype(jnp.bfloat16)
            do_s[rows_of(h)] = scaled
            do_t[:, rows_of(h)] = scaled.T
            delta = jnp.sum(scaled.astype(jnp.float32) * out.astype(jnp.float32), axis=1, keepdims=True)
            delta_b[rows_of(h)] = jnp.broadcast_to(delta, (SPAN, WIDTH))
        dq_acc[...] = jnp.zeros_like(dq_acc)

        def backward(i, count):
            places = [holder[first_block + i + n] for n in range(count)]
            for n, c in enumerate(places):
                wide_buf[n] = lax.dot_general(
                    do_s[...], kv_v[c, 1], NT, preferred_element_type=jnp.float32
                )
            for n in range(count):
                for h in range(UNIT_HEADS):
                    p = probs[i + n, rows_of(h)].astype(jnp.float32)
                    ds = p * (wide_buf[n, rows_of(h)] - both(delta_b[rows_of(h)]))
                    grads[n, rows_of(h)] = ds.astype(jnp.bfloat16)
            dv = jnp.dot(
                do_t[...], beside([probs[i + n] for n in range(count)]), preferred_element_type=jnp.float32
            )
            ds = beside([grads[n] for n in range(count)])
            dk = jnp.dot(q_t[...], ds, preferred_element_type=jnp.float32)
            dq_acc[...] += jnp.dot(
                ds, below([kv_v[c, 0] for c in places]), preferred_element_type=jnp.float32
            )
            for n, c in enumerate(places):
                part = slice(n * SPAN, (n + 1) * SPAN)
                acc[c, 0] += dk[:, part]
                acc[c, 1] += dv[:, part]

        def grad_step(j, _):
            backward(2 * j, 2)
            return 0

        lax.fori_loop(0, blocks // 2, grad_step, 0)

        @pl.when(blocks % 2 == 1)
        def _():
            backward(blocks - 1, 1)

        for h in range(UNIT_HEADS):
            dq_v[u, :, lanes_of(h)] = (dq_acc[rows_of(h)] * SCALE).astype(jnp.bfloat16)
        return 0

    lax.fori_loop(0, UNITS, unit, 0)

    def pack(c, _):
        dkv_v[c, 0] = (acc[c, 0] * SCALE).astype(jnp.bfloat16)
        dkv_v[c, 1] = acc[c, 1].astype(jnp.bfloat16)
        return 0

    lax.fori_loop(0, N_CTX, pack, 0)


def attention(q, do, kv, span_of, doc_lengths):
    rows = jax.ShapeDtypeStruct((UNITS, SPAN, UNIT_HEADS * WIDTH), jnp.bfloat16)
    blocks = jax.ShapeDtypeStruct((N_CTX, 2, WIDTH, SPAN), jnp.bfloat16)
    smem = pl.BlockSpec(memory_space=pltpu.SMEM)
    here = pl.BlockSpec(memory_space=pltpu.VMEM)
    vmem = pltpu.VMEM
    return pl.pallas_call(
        attention_kernel,
        out_shape=(rows, rows, blocks),
        in_specs=[smem, smem, here, here, here],
        out_specs=(here, here, here),
        scratch_shapes=[
            pltpu.SMEM((N_CTX,), jnp.int32),
            vmem(blocks.shape, jnp.float32),
            vmem((MAX_BLOCKS, COLS, SPAN), jnp.bfloat16),
            vmem((2, COLS, SPAN), jnp.bfloat16),
            vmem((2, COLS, SPAN), jnp.float32),
            vmem((WIDTH, COLS), jnp.bfloat16),
            vmem((WIDTH, COLS), jnp.bfloat16),
            vmem((COLS, WIDTH), jnp.bfloat16),
            vmem((COLS, WIDTH), jnp.bfloat16),
            vmem((COLS, 2 * WIDTH), jnp.float32),
            vmem((COLS, WIDTH), jnp.float32),
            vmem((COLS, WIDTH), jnp.float32),
            vmem((COLS, WIDTH), jnp.float32),
            vmem((SPAN, WIDTH), jnp.int32),
        ],
        compiler_params=pltpu.CompilerParams(vmem_limit_bytes=40 * 1024 * 1024),
        name="attention",
    )(span_of, doc_lengths, q, do, kv)


MESH_IDS = pl.DeviceIdType.MESH


def place(z_size):
    ctx, head = lax.axis_index("ctx"), lax.axis_index("head")
    return ctx, head, ctx // (2 * z_size), (ctx // 2) % z_size, ctx % 2


def meet(group, ctx, head, core, heads, others):
    barrier = pltpu.get_barrier_semaphore()
    base = ctx - core

    def greet(step, _):
        peer = (core * heads + head + step) % group
        pl.semaphore_signal(
            barrier, inc=1, device_id=(base + peer // heads, peer % heads), device_id_type=MESH_IDS
        )
        return 0

    lax.fori_loop(1, group, greet, 0)
    for other in others:
        pl.semaphore_signal(barrier, inc=1, device_id=(other, head), device_id_type=MESH_IDS)
    pl.semaphore_wait(barrier, group - 1 + len(others))


def arrived(ref, sem):
    pltpu.make_async_copy(ref, ref, sem).wait()


def send(src, dst, send_sem, recv_sem, ctx, head):
    pltpu.make_async_remote_copy(
        src_ref=src, dst_ref=dst, send_sem=send_sem, recv_sem=recv_sem,
        device_id=(ctx, head), device_id_type=MESH_IDS,
    ).start()


def gather_kernel(
    z_size, heads,
    q_hbm, do_hbm, k_hbm, v_hbm, q_out, do_out, kv_out, q_in, do_in, k_in, v_in,
    row_send, row_recv, piece_send, piece_recv, ring_send, right_recv, left_recv,
    cross_recv, twin_send, twin_recv, local_sem, load_sem,
):
    loads = []
    for n, (src, dst) in enumerate(((k_hbm, k_in), (v_hbm, v_in), (q_hbm, q_in), (do_hbm, do_in))):
        loads.append(pltpu.make_async_copy(src, dst, load_sem.at[n]))
        loads[-1].start()
    ctx, head, x, z, core = place(z_size)
    group = 2 * heads
    base = ctx - core
    mine = core * heads + head
    wide = q_in.shape[1] // group

    def index(x_at, z_at):
        return (x_at * z_size + z_at) * 2 + core

    right, left = index(x, (z + 1) % z_size), index(x, (z + z_size - 1) % z_size)
    cross, twin = index(1 - x, z), base + 1 - core
    meet(group, ctx, head, core, heads, (right, left, cross))

    def piece_cols(at):
        return pl.ds(pl.multiple_of(at * WIDTH, WIDTH), WIDTH)

    def row_cols(at):
        peer_core, peer_head = at // heads, at % heads
        return pl.ds(pl.multiple_of((peer_head * 2 + peer_core) * wide, WIDTH), wide)

    def send_pieces(step, _):
        peer = (head + step) % heads
        for side, ref in enumerate((k_in, v_in)):
            send(
                ref.at[:, piece_cols(peer)], kv_out.at[ctx, side, head],
                piece_send, piece_recv, ctx, peer,
            )
        return 0

    loads[0].wait()
    loads[1].wait()
    lax.fori_loop(1, heads, send_pieces, 0)
    own = []
    for side, ref in enumerate((k_in, v_in)):
        own.append(
            pltpu.make_async_copy(ref.at[:, piece_cols(head)], kv_out.at[ctx, side, head], local_sem.at[side])
        )
        own[-1].start()

    def send_rows(src, dst, which):
        def step_rows(step, _):
            peer = (mine + step) % group
            send(
                src.at[:, row_cols(peer)], dst.at[mine],
                row_send.at[which], row_recv.at[which], base + peer // heads, peer % heads,
            )
            return 0

        lax.fori_loop(1, group, step_rows, 0)
        copy = pltpu.make_async_copy(src.at[:, row_cols(mine)], dst.at[mine], local_sem.at[2 + which])
        copy.start()
        own.append(copy)

    loads[2].wait()
    send_rows(q_in, q_out, 0)
    own[0].wait()
    own[1].wait()
    pieces = kv_out.at[ctx, :, pl.ds(0, heads - 1)]
    arrived(pieces, piece_recv)

    sent = []

    def forward(block, to, recv):
        sem = ring_send.at[len(sent)]
        send(kv_out.at[block], kv_out.at[block], sem, recv, to, head)
        sent.append((block, sem))

    def share(block):
        send(kv_out.at[block], kv_out.at[block], twin_send, twin_recv, twin, head)

    far = z_size // 2
    reach = ((far, far - 1), (far - 1, far))
    forward(ctx, cross, cross_recv)
    forward(ctx, right, right_recv.at[0, 0])
    forward(ctx, left, left_recv.at[0, 0])
    share(ctx)
    loads[3].wait()
    send_rows(do_in, do_out, 1)
    arrived(kv_out.at[cross], cross_recv)
    forward(cross, right, right_recv.at[1, 0])
    forward(cross, left, left_recv.at[1, 0])
    share(cross)
    for d in range(1, far + 1):
        for plane in range(2):
            at_x = x if plane == 0 else 1 - x
            for way in range(2):
                if d > reach[plane][way]:
                    continue
                recv, to = ((right_recv, right), (left_recv, left))[way]
                origin = (z + z_size - d) % z_size if way == 0 else (z + d) % z_size
                block = index(at_x, origin)
                arrived(kv_out.at[block], recv.at[plane, d - 1])
                if d < reach[plane][way]:
                    forward(block, to, recv.at[plane, d])
                share(block)

    arrived(pieces, piece_send)
    for block, sem in sent:
        arrived(kv_out.at[block], sem)
    half = kv_out.at[pl.ds(0, 2 * z_size)]
    arrived(half, twin_send)
    arrived(half, twin_recv)
    for which, dst in enumerate((q_out, do_out)):
        own[2 + which].wait()
        rows = dst.at[pl.ds(0, group - 1)]
        arrived(rows, row_send.at[which])
        arrived(rows, row_recv.at[which])


def gather(q, do, k, v, z_size, heads):
    tokens = q.shape[0]
    group = 2 * heads
    far = z_size // 2
    rows = jax.ShapeDtypeStruct((group, tokens, q.shape[1] // group), q.dtype)
    kv = jax.ShapeDtypeStruct((4 * z_size, 2, heads, tokens, WIDTH), q.dtype)
    hbm = pl.BlockSpec(memory_space=pl.ANY)
    here = pl.BlockSpec(memory_space=pltpu.VMEM)
    dma = pltpu.SemaphoreType.DMA
    return pl.pallas_call(
        functools.partial(gather_kernel, z_size, heads),
        out_shape=(rows, rows, kv),
        in_specs=[hbm] * 4,
        out_specs=(here, here, here),
        scratch_shapes=[pltpu.VMEM(a.shape, a.dtype) for a in (q, do, k, v)] + [
            dma((2,)), dma((2,)), dma, dma, dma((4 * far - 2 + 1,)), dma((2, far)), dma((2, far)),
            dma, dma, dma, dma((4,)), dma((4,)),
        ],
        compiler_params=pltpu.CompilerParams(collective_id=0, has_side_effects=True, vmem_limit_bytes=58 * 1024 * 1024),
        name="gather",
    )(q, do, k, v)


def scatter_kernel(
    z_size, heads,
    o_in, dq_in, dkv_in, o_out, dq_out, dk_out, dv_out,
    part, twin_part, right_part, left_part, cross_part, final,
    row_send, row_recv, piece_send, piece_recv, ring_send, right_recv, left_recv,
    cross_recv, twin_send, twin_recv, local_sem,
):
    ctx, head, x, z, core = place(z_size)
    group = 2 * heads
    base = ctx - core
    mine = core * heads + head
    wide = o_in.shape[2]

    def index(x_at, z_at):
        return (x_at * z_size + z_at) * 2 + core

    right, left = index(x, (z + 1) % z_size), index(x, (z + z_size - 1) % z_size)
    cross, twin = index(1 - x, z), base + 1 - core
    meet(group, ctx, head, core, heads, (right, left, cross))

    load = pltpu.make_async_copy(dkv_in.at[:, core], part, local_sem.at[0])
    load.start()

    far = z_size // 2
    reach = ((far, far - 1), (far - 1, far))
    steps = []
    for back in range(far):
        for plane, way in ((0, 0), (1, 1), (1, 0), (0, 1)):
            d = reach[plane][way] - back
            if d > 0:
                steps.append((plane, way, d, back))

    def slot(plane, way, d):
        at_x = x if plane == 0 else 1 - x
        at_z = (z + d) % z_size if way == 0 else (z + z_size - d) % z_size
        return at_x * z_size + at_z

    order = [slot(plane, way, d) for plane, way, d, _ in steps]
    order += [slot(1, 0, 0), slot(0, 0, 0)]
    for n, block in enumerate(order):
        send(dkv_in.at[block, 1 - core], twin_part.at[block], twin_send, twin_recv.at[n], twin, head)

    def row_cols(at):
        return pl.ds(pl.multiple_of(((at % heads) * 2 + at // heads) * wide, WIDTH), wide)

    own = []

    def send_rows(src, dst, which):
        def step_rows(step, _):
            peer = (mine + step) % group
            send(
                src.at[peer], dst.at[:, row_cols_mine],
                row_send.at[which], row_recv.at[which], base + peer // heads, peer % heads,
            )
            return 0

        row_cols_mine = row_cols(mine)
        lax.fori_loop(1, group, step_rows, 0)
        copy = pltpu.make_async_copy(src.at[mine], dst.at[:, row_cols_mine], local_sem.at[1 + which])
        copy.start()
        own.append(copy)

    def combine(block, extras, last=False):
        def add_half(side, _):
            total = part[block, side].astype(jnp.float32) + twin_part[block, side].astype(jnp.float32)
            for ref, at in extras:
                total = total + ref[at + (side,)].astype(jnp.float32)
            if last:
                final[side] = total.T.astype(final.dtype).reshape(final.shape[1:])
            else:
                part[block, side] = total.astype(part.dtype)
            return 0

        lax.fori_loop(0, 2, add_half, 0)

    load.wait()
    sent = []
    for n, (plane, way, d, back) in enumerate(steps):
        if n == min(4, len(steps) - 1):
            send_rows(o_in, o_out, 0)
        block = order[n]
        recv, buf, to = ((right_recv, right_part, right), (left_recv, left_part, left))[way]
        arrived(twin_part.at[block], twin_recv.at[n])
        extras = []
        if back > 0:
            arrived(buf.at[plane, back - 1], recv.at[plane, back - 1])
            extras = [(buf, (plane, back - 1))]
        combine(block, extras)
        send(part.at[block], buf.at[plane, back], ring_send.at[n], recv.at[plane, back], to, head)
        sent.append((block, ring_send.at[n]))
        if n == min(7, len(steps) - 1):
            send_rows(dq_in, dq_out, 1)
    for plane in (1, 0):
        n = len(steps) + 1 - plane
        block = order[n]
        arrived(twin_part.at[block], twin_recv.at[n])
        last_right, last_left = reach[plane][0] - 1, reach[plane][1] - 1
        arrived(right_part.at[plane, last_right], right_recv.at[plane, last_right])
        arrived(left_part.at[plane, last_left], left_recv.at[plane, last_left])
        extras = [(right_part, (plane, last_right)), (left_part, (plane, last_left))]
        if plane == 0:
            arrived(cross_part.at[0], cross_recv)
            extras.append((cross_part, (0,)))
        combine(block, extras, last=plane == 0)
        if plane == 1:
            send(part.at[block], cross_part.at[0], ring_send.at[n], cross_recv, cross, head)
            sent.append((block, ring_send.at[n]))

    my_cols = pl.ds(pl.multiple_of(head * WIDTH, WIDTH), WIDTH)

    def send_pieces(step, _):
        peer = (head + step) % heads
        for side, dst in enumerate((dk_out, dv_out)):
            send(final.at[side, peer], dst.at[:, my_cols], piece_send, piece_recv.at[side], ctx, peer)
        return 0

    lax.fori_loop(1, heads, send_pieces, 0)
    for side, dst in enumerate((dk_out, dv_out)):
        copy = pltpu.make_async_copy(final.at[side, head], dst.at[:, my_cols], local_sem.at[3 + side])
        copy.start()
        own.append(copy)

    for copy in own:
        copy.wait()
    for block, sem in sent:
        arrived(part.at[block], sem)
    arrived(part.at[pl.ds(0, 2 * z_size)], twin_send)
    for which, dst in enumerate((o_out, dq_out)):
        rows = dst.at[:, pl.ds(0, (group - 1) * wide)]
        arrived(rows, row_send.at[which])
        arrived(rows, row_recv.at[which])
    arrived(final.at[:, pl.ds(0, heads - 1)], piece_send)
    for side, dst in enumerate((dk_out, dv_out)):
        arrived(dst.at[:, pl.ds(0, (heads - 1) * WIDTH)], piece_recv.at[side])


def scatter(o, dq, dkv, z_size, heads):
    group, tokens, wide = o.shape
    far = z_size // 2
    rows = jax.ShapeDtypeStruct((tokens, group * wide), o.dtype)
    pieces = jax.ShapeDtypeStruct((tokens, heads * WIDTH), o.dtype)
    block = dkv.shape[2:]
    here = pl.BlockSpec(memory_space=pltpu.VMEM)
    dma = pltpu.SemaphoreType.DMA
    return pl.pallas_call(
        functools.partial(scatter_kernel, z_size, heads),
        out_shape=(rows, rows, pieces, pieces),
        in_specs=[here] * 3,
        out_specs=(here,) * 4,
        scratch_shapes=[
            pltpu.VMEM((2 * z_size,) + block, dkv.dtype),
            pltpu.VMEM((2 * z_size,) + block, dkv.dtype),
            pltpu.VMEM((2, far) + block, dkv.dtype),
            pltpu.VMEM((2, far) + block, dkv.dtype),
            pltpu.VMEM((1,) + block, dkv.dtype),
            pltpu.VMEM((2, heads, tokens, WIDTH), dkv.dtype),
            dma((2,)), dma((2,)), dma, dma((2,)), dma((4 * far - 2 + 1,)), dma((2, far)), dma((2, far)),
            dma, dma, dma((2 * z_size,)), dma((5,)),
        ],
        compiler_params=pltpu.CompilerParams(
            collective_id=1, has_side_effects=True, vmem_limit_bytes=24 * 1024 * 1024
        ),
        name="scatter",
    )(o, dq, dkv)


def settle_kernel(*refs):
    count = len(refs) // 2
    sem = refs[-1]
    copies = [pltpu.make_async_copy(refs[i], refs[count + i], sem.at[i]) for i in range(count)]
    for copy in copies:
        copy.start()
    for copy in copies:
        copy.wait()


def settle(arrays):
    hbm = pl.BlockSpec(memory_space=pl.ANY)
    here = pl.BlockSpec(memory_space=pltpu.VMEM)
    return pl.pallas_call(
        settle_kernel,
        out_shape=tuple(jax.ShapeDtypeStruct(a.shape, a.dtype) for a in arrays),
        in_specs=[here] * len(arrays),
        out_specs=(hbm,) * len(arrays),
        scratch_shapes=[pltpu.SemaphoreType.DMA((len(arrays),))],
        compiler_params=pltpu.CompilerParams(vmem_limit_bytes=32 * 1024 * 1024),
        name="settle",
    )(*arrays)


def per_device(heads, z_size, queries, keys, values, output_gradient, doc_lengths, span_of):
    q, do, kv = gather(queries, output_gradient, keys, values, z_size, heads)
    rows = (UNITS, SPAN, UNIT_HEADS * WIDTH)
    o, dq, dkv = attention(
        q.reshape(rows), do.reshape(rows), kv.reshape(N_CTX, 2, SPAN, WIDTH), span_of, doc_lengths
    )
    dkv = dkv.reshape((N_CTX // 2, 2) + dkv.shape[1:])
    return settle(scatter(o.reshape(q.shape), dq.reshape(q.shape), dkv, z_size, heads))


def solution(mesh):
    shard = P(("ctx", "head"), None)
    return jax.shard_map(
        functools.partial(per_device, mesh.shape["head"], N_CTX // 4),
        mesh=mesh,
        in_specs=(shard, shard, shard, shard, P(), P()),
        out_specs=(shard, shard, shard, shard),
        check_vma=False,
    )
```

```python
import functools
import math

import jax
import jax.numpy as jnp
from jax import lax
from jax.experimental import pallas as pl
from jax.experimental.pallas import tpu as pltpu
from jax.sharding import PartitionSpec as P

N_CTX = 32
SPAN = 256
WIDTH = 128
UNIT_HEADS = 4
UNITS = 2
MAX_BLOCKS = 18
COLS = UNIT_HEADS * SPAN
LIMIT = 2.0**60
SCALE = WIDTH**-0.5
LOG2_SCALE = SCALE * math.log2(math.e)
NEG = -1e30


NT = (((1,), (1,)), ((), ()))


def attention_kernel(
    span_hbm, len_hbm, q_v, do_v, kv_v,
    o_v, dq_v, dkv_v,
    holder, acc, probs, grads, wide_buf,
    q_t, do_t, q_s, do_s, o_acc, dq_acc, level_b, delta_b, starts,
    span_ref, len_ref, table_sem,
):
    load_span = pltpu.make_async_copy(span_hbm, span_ref, table_sem.at[0])
    load_len = pltpu.make_async_copy(len_hbm, len_ref, table_sem.at[1])
    load_span.start()
    load_len.start()
    ctx = lax.axis_index("ctx")
    first_unit = ctx - ctx % UNITS

    def clear(c, _):
        acc[c] = jnp.zeros((2, WIDTH, SPAN), jnp.float32)
        return 0

    lax.fori_loop(0, N_CTX, clear, 0)

    load_span.wait()
    load_len.wait()

    def note(c, _):
        holder[span_ref[c]] = c
        return 0

    lax.fori_loop(0, N_CTX, note, 0)

    ends = []
    running = jnp.int32(0)
    for j in range(4):
        running = running + len_ref[j]
        ends.append(running)

    def doc_start(pos):
        start = jnp.zeros_like(pos)
        for end in ends:
            start = jnp.where(pos >= end, end, start)
        return start

    def rows_of(h):
        return pl.ds(h * SPAN, SPAN)

    def lanes_of(h):
        return pl.ds(h * WIDTH, WIDTH)

    def both(x):
        return jnp.concatenate([x, x], axis=1)

    def beside(parts):
        return parts[0] if len(parts) == 1 else jnp.concatenate(parts, axis=1)

    def below(parts):
        return parts[0] if len(parts) == 1 else jnp.concatenate(parts, axis=0)

    ones = jnp.ones((SPAN, WIDTH), jnp.bfloat16)

    def unit(u, _):
        span = span_ref[first_unit + u]
        first_pos = span * SPAN
        first_block = doc_start(first_pos) // SPAN
        last_start = doc_start(first_pos + (SPAN - 1))
        blocks = span - first_block + 1
        edges = jnp.maximum(jnp.minimum((last_start + (SPAN - 1)) // SPAN, span) - first_block, 0)
        starts[...] = doc_start(first_pos + lax.broadcasted_iota(jnp.int32, (SPAN, WIDTH), 0))

        for h in range(UNIT_HEADS):
            q_h = q_v[u, :, lanes_of(h)]
            q_s[rows_of(h)] = q_h
            q_t[:, rows_of(h)] = q_h.T

        def allowed_at(t):
            k_pos = t * SPAN + lax.broadcasted_iota(jnp.int32, (SPAN, SPAN), 1)
            q_pos = first_pos + lax.broadcasted_iota(jnp.int32, (SPAN, SPAN), 0)
            return (k_pos <= q_pos) & (k_pos >= both(starts[...]))

        def halves_max(s):
            return jnp.maximum(s[:, :WIDTH], s[:, WIDTH:])

        def row_max(x):
            return jnp.broadcast_to(jnp.max(x, axis=1, keepdims=True), x.shape)

        def forward(i, count, masked, take_top=False):
            places = [holder[first_block + i + n] for n in range(count)]
            for n, c in enumerate(places):
                wide_buf[n] = lax.dot_general(
                    q_s[...], kv_v[c, 0], NT, preferred_element_type=jnp.float32
                )
            if masked:
                allowed = allowed_at(first_block + i)
            for n in range(count):
                for h in range(UNIT_HEADS):
                    s = wide_buf[n, rows_of(h)]
                    if masked:
                        s = jnp.where(allowed, s, NEG)
                    if take_top:
                        level = row_max(halves_max(s))
                        level_b[rows_of(h)] = level
                    else:
                        level = level_b[rows_of(h)]
                    p = jnp.exp2((s - both(level)) * LOG2_SCALE)
                    probs[i + n, rows_of(h)] = p.astype(jnp.bfloat16)
            values = below([beside([kv_v[c, 1], ones]) for c in places])
            o_acc[...] += jnp.dot(
                beside([probs[i + n] for n in range(count)]), values, preferred_element_type=jnp.float32
            )

        def masked_step(i, _):
            forward(i, 1, True)
            return 0

        o_acc[...] = jnp.zeros_like(o_acc)
        forward(blocks - 1, 1, True, take_top=True)
        lax.fori_loop(0, edges, masked_step, 0)
        inner = blocks - 1 - edges

        def pair_step(j, _):
            forward(edges + 2 * j, 2, False)
            return 0

        lax.fori_loop(0, inner // 2, pair_step, 0)

        @pl.when(inner % 2 == 1)
        def _():
            forward(blocks - 2, 1, False)

        worst = jnp.max(jnp.where(o_acc[:, WIDTH:] < LIMIT, 0.0, 1.0))

        @pl.when(worst > 0.0)
        def _():
            o_acc[...] = jnp.zeros_like(o_acc)
            level_b[...] = jnp.full_like(level_b, NEG)

            def top_step(i, _):
                k = kv_v[holder[first_block + i], 0]
                allowed = allowed_at(first_block + i)
                for h in range(UNIT_HEADS):
                    s = lax.dot_general(q_s[rows_of(h)], k, NT, preferred_element_type=jnp.float32)
                    s = jnp.where(allowed, s, NEG)
                    level_b[rows_of(h)] = jnp.maximum(level_b[rows_of(h)], halves_max(s))
                return 0

            lax.fori_loop(0, blocks, top_step, 0)
            for h in range(UNIT_HEADS):
                level_b[rows_of(h)] = row_max(level_b[rows_of(h)])
            lax.fori_loop(0, blocks, masked_step, 0)

        for h in range(UNIT_HEADS):
            inverse = 1.0 / o_acc[rows_of(h), WIDTH:]
            out = (o_acc[rows_of(h), :WIDTH] * inverse).astype(jnp.bfloat16)
            o_v[u, :, lanes_of(h)] = out
            scaled = (do_v[u, :, lanes_of(h)].astype(jnp.float32) * inverse).astype(jnp.bfloat16)
            do_s[rows_of(h)] = scaled
            do_t[:, rows_of(h)] = scaled.T
            delta = jnp.sum(scaled.astype(jnp.float32) * out.astype(jnp.float32), axis=1, keepdims=True)
            delta_b[rows_of(h)] = jnp.broadcast_to(delta, (SPAN, WIDTH))
        dq_acc[...] = jnp.zeros_like(dq_acc)

        def backward(i, count):
            places = [holder[first_block + i + n] for n in range(count)]
            for n, c in enumerate(places):
                wide_buf[n] = lax.dot_general(
                    do_s[...], kv_v[c, 1], NT, preferred_element_type=jnp.float32
                )
            for n in range(count):
                for h in range(UNIT_HEADS):
                    p = probs[i + n, rows_of(h)].astype(jnp.float32)
                    ds = p * (wide_buf[n, rows_of(h)] - both(delta_b[rows_of(h)]))
                    grads[n, rows_of(h)] = ds.astype(jnp.bfloat16)
            dv = jnp.dot(
                do_t[...], beside([probs[i + n] for n in range(count)]), preferred_element_type=jnp.float32
            )
            ds = beside([grads[n] for n in range(count)])
            dk = jnp.dot(q_t[...], ds, preferred_element_type=jnp.float32)
            dq_acc[...] += jnp.dot(
                ds, below([kv_v[c, 0] for c in places]), preferred_element_type=jnp.float32
            )
            for n, c in enumerate(places):
                part = slice(n * SPAN, (n + 1) * SPAN)
                acc[c, 0] += dk[:, part]
                acc[c, 1] += dv[:, part]

        def grad_step(j, _):
            backward(2 * j, 2)
            return 0

        lax.fori_loop(0, blocks // 2, grad_step, 0)

        @pl.when(blocks % 2 == 1)
        def _():
            backward(blocks - 1, 1)

        for h in range(UNIT_HEADS):
            dq_v[u, :, lanes_of(h)] = (dq_acc[rows_of(h)] * SCALE).astype(jnp.bfloat16)
        return 0

    lax.fori_loop(0, UNITS, unit, 0)

    def pack(c, _):
        dkv_v[c, 0] = (acc[c, 0] * SCALE).astype(jnp.bfloat16)
        dkv_v[c, 1] = acc[c, 1].astype(jnp.bfloat16)
        return 0

    lax.fori_loop(0, N_CTX, pack, 0)


def attention(q, do, kv, span_of, doc_lengths):
    rows = jax.ShapeDtypeStruct((UNITS, SPAN, UNIT_HEADS * WIDTH), jnp.bfloat16)
    blocks = jax.ShapeDtypeStruct((N_CTX, 2, WIDTH, SPAN), jnp.bfloat16)
    table = pl.BlockSpec(memory_space=pltpu.HBM)
    here = pl.BlockSpec(memory_space=pltpu.VMEM)
    vmem = pltpu.VMEM
    return pl.pallas_call(
        attention_kernel,
        out_shape=(rows, rows, blocks),
        in_specs=[table, table, here, here, here],
        out_specs=(here, here, here),
        scratch_shapes=[
            pltpu.SMEM((N_CTX,), jnp.int32),
            vmem(blocks.shape, jnp.float32),
            vmem((MAX_BLOCKS, COLS, SPAN), jnp.bfloat16),
            vmem((2, COLS, SPAN), jnp.bfloat16),
            vmem((2, COLS, SPAN), jnp.float32),
            vmem((WIDTH, COLS), jnp.bfloat16),
            vmem((WIDTH, COLS), jnp.bfloat16),
            vmem((COLS, WIDTH), jnp.bfloat16),
            vmem((COLS, WIDTH), jnp.bfloat16),
            vmem((COLS, 2 * WIDTH), jnp.float32),
            vmem((COLS, WIDTH), jnp.float32),
            vmem((COLS, WIDTH), jnp.float32),
            vmem((COLS, WIDTH), jnp.float32),
            vmem((SPAN, WIDTH), jnp.int32),
            pltpu.SMEM((N_CTX,), jnp.int32),
            pltpu.SMEM((4,), jnp.int32),
            pltpu.SemaphoreType.DMA((2,)),
        ],
        compiler_params=pltpu.CompilerParams(vmem_limit_bytes=40 * 1024 * 1024),
        name="attention",
    )(span_of, doc_lengths, q, do, kv)


MESH_IDS = pl.DeviceIdType.MESH


def place(z_size):
    ctx, head = lax.axis_index("ctx"), lax.axis_index("head")
    return ctx, head, ctx // (2 * z_size), (ctx // 2) % z_size, ctx % 2


def meet(group, ctx, head, core, heads, others):
    barrier = pltpu.get_barrier_semaphore()
    base = ctx - core

    def greet(step, _):
        peer = (core * heads + head + step) % group
        pl.semaphore_signal(
            barrier, inc=1, device_id=(base + peer // heads, peer % heads), device_id_type=MESH_IDS
        )
        return 0

    lax.fori_loop(1, group, greet, 0)
    for other in others:
        pl.semaphore_signal(barrier, inc=1, device_id=(other, head), device_id_type=MESH_IDS)
    pl.semaphore_wait(barrier, group - 1 + len(others))


def arrived(ref, sem):
    pltpu.make_async_copy(ref, ref, sem).wait()


def send(src, dst, send_sem, recv_sem, ctx, head):
    pltpu.make_async_remote_copy(
        src_ref=src, dst_ref=dst, send_sem=send_sem, recv_sem=recv_sem,
        device_id=(ctx, head), device_id_type=MESH_IDS,
    ).start()


def gather_kernel(
    z_size, heads,
    q_hbm, do_hbm, k_hbm, v_hbm, q_out, do_out, kv_out, q_in, do_in, k_in, v_in,
    row_send, row_recv, piece_send, piece_recv, ring_send, right_recv, left_recv,
    cross_recv, twin_send, twin_recv, local_sem, load_sem,
):
    loads = []
    for n, (src, dst) in enumerate(((k_hbm, k_in), (v_hbm, v_in), (q_hbm, q_in), (do_hbm, do_in))):
        loads.append(pltpu.make_async_copy(src, dst, load_sem.at[n]))
        loads[-1].start()
    ctx, head, x, z, core = place(z_size)
    group = 2 * heads
    base = ctx - core
    mine = core * heads + head
    wide = q_in.shape[1] // group

    def index(x_at, z_at):
        return (x_at * z_size + z_at) * 2 + core

    right, left = index(x, (z + 1) % z_size), index(x, (z + z_size - 1) % z_size)
    cross, twin = index(1 - x, z), base + 1 - core
    meet(group, ctx, head, core, heads, (right, left, cross))

    def piece_cols(at):
        return pl.ds(pl.multiple_of(at * WIDTH, WIDTH), WIDTH)

    def row_cols(at):
        peer_core, peer_head = at // heads, at % heads
        return pl.ds(pl.multiple_of((peer_head * 2 + peer_core) * wide, WIDTH), wide)

    def send_pieces(step, _):
        peer = (head + step) % heads
        for side, ref in enumerate((k_in, v_in)):
            send(
                ref.at[:, piece_cols(peer)], kv_out.at[ctx, side, head],
                piece_send, piece_recv, ctx, peer,
            )
        return 0

    loads[0].wait()
    loads[1].wait()
    lax.fori_loop(1, heads, send_pieces, 0)
    own = []
    for side, ref in enumerate((k_in, v_in)):
        own.append(
            pltpu.make_async_copy(ref.at[:, piece_cols(head)], kv_out.at[ctx, side, head], local_sem.at[side])
        )
        own[-1].start()

    rows_left = []

    def start_rows(src, dst, which):
        def step_rows(step, _):
            peer = (mine + step) % group
            send(
                src.at[:, row_cols(peer)], dst.at[mine],
                row_send.at[which], row_recv.at[which], base + peer // heads, peer % heads,
            )
            return 0

        rows_left.extend((step, step_rows) for step in range(1, group))
        copy = pltpu.make_async_copy(src.at[:, row_cols(mine)], dst.at[mine], local_sem.at[2 + which])
        copy.start()
        own.append(copy)

    def send_some(count):
        while rows_left and count > 0:
            first, which = rows_left[0]
            run = 0
            while rows_left and run < count and rows_left[0][1] is which:
                rows_left.pop(0)
                run += 1
            lax.fori_loop(first, first + run, which, 0)
            count -= run

    loads[2].wait()
    start_rows(q_in, q_out, 0)
    loads[3].wait()
    start_rows(do_in, do_out, 1)
    send_some(3)
    own[0].wait()
    own[1].wait()
    pieces = kv_out.at[ctx, :, pl.ds(0, heads - 1)]
    arrived(pieces, piece_recv)

    sent = []

    def forward(block, to, recv):
        sem = ring_send.at[len(sent)]
        send(kv_out.at[block], kv_out.at[block], sem, recv, to, head)
        sent.append((block, sem))

    def share(block):
        send(kv_out.at[block], kv_out.at[block], twin_send, twin_recv, twin, head)

    far = z_size // 2
    reach = ((far, far - 1), (far - 1, far))
    forward(ctx, cross, cross_recv)
    forward(ctx, right, right_recv.at[0, 0])
    forward(ctx, left, left_recv.at[0, 0])
    share(ctx)
    send_some(4)
    arrived(kv_out.at[cross], cross_recv)
    forward(cross, right, right_recv.at[1, 0])
    forward(cross, left, left_recv.at[1, 0])
    share(cross)
    for d in range(1, far + 1):
        for plane in range(2):
            at_x = x if plane == 0 else 1 - x
            for way in range(2):
                if d > reach[plane][way]:
                    continue
                recv, to = ((right_recv, right), (left_recv, left))[way]
                origin = (z + z_size - d) % z_size if way == 0 else (z + d) % z_size
                block = index(at_x, origin)
                arrived(kv_out.at[block], recv.at[plane, d - 1])
                if d < reach[plane][way]:
                    forward(block, to, recv.at[plane, d])
                share(block)
                send_some(2)

    send_some(len(rows_left))
    arrived(pieces, piece_send)
    for block, sem in sent:
        arrived(kv_out.at[block], sem)
    half = kv_out.at[pl.ds(0, 2 * z_size)]
    arrived(half, twin_send)
    arrived(half, twin_recv)
    for which, dst in enumerate((q_out, do_out)):
        own[2 + which].wait()
        rows = dst.at[pl.ds(0, group - 1)]
        arrived(rows, row_send.at[which])
        arrived(rows, row_recv.at[which])


def gather(q, do, k, v, z_size, heads):
    tokens = q.shape[0]
    group = 2 * heads
    far = z_size // 2
    rows = jax.ShapeDtypeStruct((group, tokens, q.shape[1] // group), q.dtype)
    kv = jax.ShapeDtypeStruct((4 * z_size, 2, heads, tokens, WIDTH), q.dtype)
    hbm = pl.BlockSpec(memory_space=pltpu.HBM)
    here = pl.BlockSpec(memory_space=pltpu.VMEM)
    dma = pltpu.SemaphoreType.DMA
    return pl.pallas_call(
        functools.partial(gather_kernel, z_size, heads),
        out_shape=(rows, rows, kv),
        in_specs=[hbm] * 4,
        out_specs=(here, here, here),
        scratch_shapes=[pltpu.VMEM(a.shape, a.dtype) for a in (q, do, k, v)] + [
            dma((2,)), dma((2,)), dma, dma, dma((4 * far - 2 + 1,)), dma((2, far)), dma((2, far)),
            dma, dma, dma, dma((4,)), dma((4,)),
        ],
        compiler_params=pltpu.CompilerParams(collective_id=0, has_side_effects=True, vmem_limit_bytes=32 * 1024 * 1024),
        name="gather",
    )(q, do, k, v)


def scatter_kernel(
    z_size, heads,
    o_in, dq_in, dkv_in, o_out, dq_out, dk_out, dv_out,
    part, twin_part, right_part, left_part, cross_part, final,
    row_send, row_recv, piece_send, piece_recv, ring_send, right_recv, left_recv,
    cross_recv, twin_send, twin_recv, local_sem,
):
    ctx, head, x, z, core = place(z_size)
    group = 2 * heads
    base = ctx - core
    mine = core * heads + head
    wide = o_in.shape[2]

    def index(x_at, z_at):
        return (x_at * z_size + z_at) * 2 + core

    right, left = index(x, (z + 1) % z_size), index(x, (z + z_size - 1) % z_size)
    cross, twin = index(1 - x, z), base + 1 - core
    meet(group, ctx, head, core, heads, (right, left, cross))

    load = pltpu.make_async_copy(dkv_in.at[:, core], part, local_sem.at[0])
    load.start()

    far = z_size // 2
    reach = ((far, far - 1), (far - 1, far))
    steps = []
    for back in range(far):
        for plane, way in ((0, 0), (1, 1), (1, 0), (0, 1)):
            d = reach[plane][way] - back
            if d > 0:
                steps.append((plane, way, d, back))

    def slot(plane, way, d):
        at_x = x if plane == 0 else 1 - x
        at_z = (z + d) % z_size if way == 0 else (z + z_size - d) % z_size
        return at_x * z_size + at_z

    order = [slot(plane, way, d) for plane, way, d, _ in steps]
    order += [slot(1, 0, 0), slot(0, 0, 0)]
    for n, block in enumerate(order):
        send(dkv_in.at[block, 1 - core], twin_part.at[block], twin_send, twin_recv.at[n], twin, head)

    def row_cols(at):
        return pl.ds(pl.multiple_of(((at % heads) * 2 + at // heads) * wide, WIDTH), wide)

    own = []

    rows_left = []

    def start_rows(src, dst, which):
        def step_rows(step, _):
            peer = (mine + step) % group
            send(
                src.at[peer], dst.at[:, row_cols(mine)],
                row_send.at[which], row_recv.at[which], base + peer // heads, peer % heads,
            )
            return 0

        rows_left.extend((step, step_rows) for step in range(1, group))
        copy = pltpu.make_async_copy(src.at[mine], dst.at[:, row_cols(mine)], local_sem.at[1 + which])
        copy.start()
        own.append(copy)

    def send_some(count):
        while rows_left and count > 0:
            first, which = rows_left[0]
            run = 0
            while rows_left and run < count and rows_left[0][1] is which:
                rows_left.pop(0)
                run += 1
            lax.fori_loop(first, first + run, which, 0)
            count -= run

    def combine(block, extras, last=False):
        def add_half(side, _):
            total = part[block, side].astype(jnp.float32) + twin_part[block, side].astype(jnp.float32)
            for ref, at in extras:
                total = total + ref[at + (side,)].astype(jnp.float32)
            if last:
                final[side] = total.T.astype(final.dtype).reshape(final.shape[1:])
            else:
                part[block, side] = total.astype(part.dtype)
            return 0

        lax.fori_loop(0, 2, add_half, 0)

    start_rows(o_in, o_out, 0)
    start_rows(dq_in, dq_out, 1)
    load.wait()
    sent = []
    for n, (plane, way, d, back) in enumerate(steps):
        block = order[n]
        recv, buf, to = ((right_recv, right_part, right), (left_recv, left_part, left))[way]
        arrived(twin_part.at[block], twin_recv.at[n])
        extras = []
        if back > 0:
            arrived(buf.at[plane, back - 1], recv.at[plane, back - 1])
            extras = [(buf, (plane, back - 1))]
        combine(block, extras)
        send(part.at[block], buf.at[plane, back], ring_send.at[n], recv.at[plane, back], to, head)
        sent.append((block, ring_send.at[n]))
        send_some(3)
    send_some(len(rows_left))
    for plane in (1, 0):
        n = len(steps) + 1 - plane
        block = order[n]
        arrived(twin_part.at[block], twin_recv.at[n])
        last_right, last_left = reach[plane][0] - 1, reach[plane][1] - 1
        arrived(right_part.at[plane, last_right], right_recv.at[plane, last_right])
        arrived(left_part.at[plane, last_left], left_recv.at[plane, last_left])
        extras = [(right_part, (plane, last_right)), (left_part, (plane, last_left))]
        if plane == 0:
            arrived(cross_part.at[0], cross_recv)
            extras.append((cross_part, (0,)))
        combine(block, extras, last=plane == 0)
        if plane == 1:
            send(part.at[block], cross_part.at[0], ring_send.at[n], cross_recv, cross, head)
            sent.append((block, ring_send.at[n]))

    my_cols = pl.ds(pl.multiple_of(head * WIDTH, WIDTH), WIDTH)

    def send_pieces(step, _):
        peer = (head + step) % heads
        for side, dst in enumerate((dk_out, dv_out)):
            send(final.at[side, peer], dst.at[:, my_cols], piece_send, piece_recv.at[side], ctx, peer)
        return 0

    lax.fori_loop(1, heads, send_pieces, 0)
    for side, dst in enumerate((dk_out, dv_out)):
        copy = pltpu.make_async_copy(final.at[side, head], dst.at[:, my_cols], local_sem.at[3 + side])
        copy.start()
        own.append(copy)

    for copy in own:
        copy.wait()
    for block, sem in sent:
        arrived(part.at[block], sem)
    arrived(part.at[pl.ds(0, 2 * z_size)], twin_send)
    for which, dst in enumerate((o_out, dq_out)):
        rows = dst.at[:, pl.ds(0, (group - 1) * wide)]
        arrived(rows, row_send.at[which])
        arrived(rows, row_recv.at[which])
    arrived(final.at[:, pl.ds(0, heads - 1)], piece_send)
    for side, dst in enumerate((dk_out, dv_out)):
        arrived(dst.at[:, pl.ds(0, (heads - 1) * WIDTH)], piece_recv.at[side])


def scatter(o, dq, dkv, z_size, heads):
    group, tokens, wide = o.shape
    far = z_size // 2
    rows = jax.ShapeDtypeStruct((tokens, group * wide), o.dtype)
    pieces = jax.ShapeDtypeStruct((tokens, heads * WIDTH), o.dtype)
    block = dkv.shape[2:]
    here = pl.BlockSpec(memory_space=pltpu.VMEM)
    dma = pltpu.SemaphoreType.DMA
    return pl.pallas_call(
        functools.partial(scatter_kernel, z_size, heads),
        out_shape=(rows, rows, pieces, pieces),
        in_specs=[here] * 3,
        out_specs=(here,) * 4,
        scratch_shapes=[
            pltpu.VMEM((2 * z_size,) + block, dkv.dtype),
            pltpu.VMEM((2 * z_size,) + block, dkv.dtype),
            pltpu.VMEM((2, far) + block, dkv.dtype),
            pltpu.VMEM((2, far) + block, dkv.dtype),
            pltpu.VMEM((1,) + block, dkv.dtype),
            pltpu.VMEM((2, heads, tokens, WIDTH), dkv.dtype),
            dma((2,)), dma((2,)), dma, dma((2,)), dma((4 * far - 2 + 1,)), dma((2, far)), dma((2, far)),
            dma, dma, dma((2 * z_size,)), dma((5,)),
        ],
        compiler_params=pltpu.CompilerParams(
            collective_id=1, has_side_effects=True, vmem_limit_bytes=24 * 1024 * 1024
        ),
        name="scatter",
    )(o, dq, dkv)


def settle_kernel(*refs):
    count = len(refs) // 2
    sem = refs[-1]
    copies = [pltpu.make_async_copy(refs[i], refs[count + i], sem.at[i]) for i in range(count)]
    for copy in copies:
        copy.start()
    for copy in copies:
        copy.wait()


def settle(arrays):
    hbm = pl.BlockSpec(memory_space=pl.ANY)
    here = pl.BlockSpec(memory_space=pltpu.VMEM)
    return pl.pallas_call(
        settle_kernel,
        out_shape=tuple(jax.ShapeDtypeStruct(a.shape, a.dtype) for a in arrays),
        in_specs=[here] * len(arrays),
        out_specs=(hbm,) * len(arrays),
        scratch_shapes=[pltpu.SemaphoreType.DMA((len(arrays),))],
        compiler_params=pltpu.CompilerParams(vmem_limit_bytes=32 * 1024 * 1024),
        name="settle",
    )(*arrays)


def per_device(heads, z_size, queries, keys, values, output_gradient, doc_lengths, span_of):
    queries, output_gradient, keys, values, doc_lengths, span_of = (
        pltpu.with_memory_space_constraint(a, pltpu.HBM)
        for a in (queries, output_gradient, keys, values, doc_lengths, span_of)
    )
    q, do, kv = gather(queries, output_gradient, keys, values, z_size, heads)
    rows = (UNITS, SPAN, UNIT_HEADS * WIDTH)
    o, dq, dkv = attention(
        q.reshape(rows), do.reshape(rows), kv.reshape(N_CTX, 2, SPAN, WIDTH), span_of, doc_lengths
    )
    dkv = dkv.reshape((N_CTX // 2, 2) + dkv.shape[1:])
    return settle(scatter(o.reshape(q.shape), dq.reshape(q.shape), dkv, z_size, heads))


def solution(mesh):
    shard = P(("ctx", "head"), None)
    return jax.shard_map(
        functools.partial(per_device, mesh.shape["head"], N_CTX // 4),
        mesh=mesh,
        in_specs=(shard, shard, shard, shard, P(), P()),
        out_specs=(shard, shard, shard, shard),
        check_vma=False,
    )
```

```python
import functools
import math

import jax
import jax.numpy as jnp
from jax import lax
from jax.experimental import pallas as pl
from jax.experimental.pallas import tpu as pltpu
from jax.sharding import PartitionSpec as P

N_CTX = 32
SPAN = 256
WIDTH = 128
UNIT_HEADS = 4
UNITS = 2
MAX_BLOCKS = 18
COLS = UNIT_HEADS * SPAN
LIMIT = 2.0**60
SCALE = WIDTH**-0.5
LOG2_SCALE = SCALE * math.log2(math.e)
NEG = -1e30


NT = (((1,), (1,)), ((), ()))


def attention_kernel(
    span_hbm, len_hbm, q_v, do_v, kv_v,
    o_v, dq_v, dkv_v,
    holder, slots, acc, probs, grads, wide_buf,
    q_t, do_t, q_s, do_s, o_acc, dq_acc, level_b, delta_b, starts,
    span_ref, len_ref, table_sem,
):
    load_span = pltpu.make_async_copy(span_hbm, span_ref, table_sem.at[0])
    load_len = pltpu.make_async_copy(len_hbm, len_ref, table_sem.at[1])
    load_span.start()
    load_len.start()
    ctx = lax.axis_index("ctx")
    first_unit = ctx - ctx % UNITS

    def clear(c, _):
        acc[c] = jnp.zeros((2, WIDTH, SPAN), jnp.float32)
        return 0

    lax.fori_loop(0, N_CTX, clear, 0)

    load_span.wait()
    load_len.wait()

    def note(c, _):
        holder[span_ref[c]] = c
        return 0

    lax.fori_loop(0, N_CTX, note, 0)

    ends = []
    running = jnp.int32(0)
    for j in range(4):
        running = running + len_ref[j]
        ends.append(running)

    def doc_start(pos):
        start = jnp.zeros_like(pos)
        for end in ends:
            start = jnp.where(pos >= end, end, start)
        return start

    def rows_of(h):
        return pl.ds(h * SPAN, SPAN)

    def lanes_of(h):
        return pl.ds(h * WIDTH, WIDTH)

    def both(x):
        return jnp.concatenate([x, x], axis=1)

    def beside(parts):
        return parts[0] if len(parts) == 1 else jnp.concatenate(parts, axis=1)

    def below(parts):
        return parts[0] if len(parts) == 1 else jnp.concatenate(parts, axis=0)

    ones = jnp.ones((SPAN, WIDTH), jnp.bfloat16)

    def unit(u, _):
        span = span_ref[first_unit + u]
        first_pos = span * SPAN
        first_block = doc_start(first_pos) // SPAN
        last_start = doc_start(first_pos + (SPAN - 1))
        blocks = span - first_block + 1
        edges = jnp.maximum(jnp.minimum((last_start + (SPAN - 1)) // SPAN, span) - first_block, 0)
        starts[...] = doc_start(first_pos + lax.broadcasted_iota(jnp.int32, (SPAN, WIDTH), 0))

        for h in range(UNIT_HEADS):
            q_h = q_v[u, :, lanes_of(h)]
            q_s[rows_of(h)] = q_h
            q_t[:, rows_of(h)] = q_h.T

        def allowed_at(t):
            k_pos = t * SPAN + lax.broadcasted_iota(jnp.int32, (SPAN, SPAN), 1)
            q_pos = first_pos + lax.broadcasted_iota(jnp.int32, (SPAN, SPAN), 0)
            return (k_pos <= q_pos) & (k_pos >= both(starts[...]))

        def halves_max(s):
            return jnp.maximum(s[:, :WIDTH], s[:, WIDTH:])

        def row_max(x):
            return jnp.broadcast_to(jnp.max(x, axis=1, keepdims=True), x.shape)

        def score(slot, count):
            for n in range(count):
                wide_buf[n] = lax.dot_general(
                    q_s[...], kv_v[slots[slot + n], 0], NT, preferred_element_type=jnp.float32
                )

        def weigh(slot, count, allowed=None, take_top=False):
            for n in range(count):
                for h in range(UNIT_HEADS):
                    s = wide_buf[n, rows_of(h)]
                    if allowed is not None:
                        s = jnp.where(allowed, s, NEG)
                    if take_top:
                        level = row_max(halves_max(s))
                        level_b[rows_of(h)] = level
                    else:
                        level = level_b[rows_of(h)]
                    p = jnp.exp2((s - both(level)) * LOG2_SCALE)
                    probs[slot + n, rows_of(h)] = p.astype(jnp.bfloat16)

        def attend(slot, count):
            values = below([beside([kv_v[slots[slot + n], 1], ones]) for n in range(count)])
            o_acc[...] += jnp.dot(
                beside([probs[slot + n] for n in range(count)]), values, preferred_element_type=jnp.float32
            )

        def masked_step(i, _):
            score(i, 1)
            weigh(i, 1, allowed_at(first_block + i - 2))
            return 0

        def attend_step(i, _):
            attend(i, 1)
            return 0

        inner_from = edges + 2
        inner = blocks - 1 - edges
        slots[0] = first_unit
        slots[1] = holder[span]

        def place_slot(i, _):
            slots[i + 2] = holder[first_block + i]
            return 0

        lax.fori_loop(0, blocks - 1, place_slot, 0)
        probs[0] = jnp.zeros((COLS, SPAN), jnp.bfloat16)
        o_acc[...] = jnp.zeros_like(o_acc)
        score(1, 1)
        weigh(1, 1, allowed_at(span), take_top=True)
        lax.fori_loop(2, inner_from, masked_step, 0)
        lax.fori_loop(1, edges, attend_step, 0)

        def pair_step(j, _):
            slot = inner_from + 2 * j
            score(slot, 2)
            attend(slot - 2, 2)
            weigh(slot, 2)
            return 0

        lax.fori_loop(0, inner // 2, pair_step, 0)
        last = inner_from + inner - inner % 2

        @pl.when(inner % 2 == 1)
        def _():
            score(last, 1)
            attend(last - 2, 2)
            weigh(last, 1)
            attend(last, 1)

        @pl.when(inner % 2 == 0)
        def _():
            attend(last - 2, 2)

        worst = jnp.max(jnp.where(o_acc[:, WIDTH:] < LIMIT, 0.0, 1.0))

        @pl.when(worst > 0.0)
        def _():
            o_acc[...] = jnp.zeros_like(o_acc)
            level_b[...] = jnp.full_like(level_b, NEG)

            def top_step(i, _):
                k = kv_v[slots[i], 0]
                allowed = allowed_at(jnp.where(i == 1, span, first_block + i - 2))
                for h in range(UNIT_HEADS):
                    s = lax.dot_general(q_s[rows_of(h)], k, NT, preferred_element_type=jnp.float32)
                    s = jnp.where(allowed, s, NEG)
                    level_b[rows_of(h)] = jnp.maximum(level_b[rows_of(h)], halves_max(s))
                return 0

            lax.fori_loop(1, blocks + 1, top_step, 0)
            for h in range(UNIT_HEADS):
                level_b[rows_of(h)] = row_max(level_b[rows_of(h)])
            score(1, 1)
            weigh(1, 1, allowed_at(span))
            lax.fori_loop(2, blocks + 1, masked_step, 0)
            lax.fori_loop(1, blocks + 1, attend_step, 0)

        for h in range(UNIT_HEADS):
            inverse = 1.0 / o_acc[rows_of(h), WIDTH:]
            out = (o_acc[rows_of(h), :WIDTH] * inverse).astype(jnp.bfloat16)
            o_v[u, :, lanes_of(h)] = out
            scaled = (do_v[u, :, lanes_of(h)].astype(jnp.float32) * inverse).astype(jnp.bfloat16)
            do_s[rows_of(h)] = scaled
            do_t[:, rows_of(h)] = scaled.T
            delta = jnp.sum(scaled.astype(jnp.float32) * out.astype(jnp.float32), axis=1, keepdims=True)
            delta_b[rows_of(h)] = jnp.broadcast_to(delta, (SPAN, WIDTH))
        dq_acc[...] = jnp.zeros_like(dq_acc)

        def backward(i, count):
            places = [slots[i + n] for n in range(count)]
            for n, c in enumerate(places):
                wide_buf[n] = lax.dot_general(
                    do_s[...], kv_v[c, 1], NT, preferred_element_type=jnp.float32
                )
            for n in range(count):
                for h in range(UNIT_HEADS):
                    p = probs[i + n, rows_of(h)].astype(jnp.float32)
                    ds = p * (wide_buf[n, rows_of(h)] - both(delta_b[rows_of(h)]))
                    grads[n, rows_of(h)] = ds.astype(jnp.bfloat16)
            dv = jnp.dot(
                do_t[...], beside([probs[i + n] for n in range(count)]), preferred_element_type=jnp.float32
            )
            ds = beside([grads[n] for n in range(count)])
            dk = jnp.dot(q_t[...], ds, preferred_element_type=jnp.float32)
            dq_acc[...] += jnp.dot(
                ds, below([kv_v[c, 0] for c in places]), preferred_element_type=jnp.float32
            )
            for n, c in enumerate(places):
                part = slice(n * SPAN, (n + 1) * SPAN)
                acc[c, 0] += dk[:, part]
                acc[c, 1] += dv[:, part]

        def grad_step(j, _):
            backward(2 * j + 1, 2)
            return 0

        lax.fori_loop(0, blocks // 2, grad_step, 0)

        @pl.when(blocks % 2 == 1)
        def _():
            backward(blocks, 1)

        for h in range(UNIT_HEADS):
            dq_v[u, :, lanes_of(h)] = (dq_acc[rows_of(h)] * SCALE).astype(jnp.bfloat16)
        return 0

    lax.fori_loop(0, UNITS, unit, 0)

    def pack(c, _):
        dkv_v[c, 0] = (acc[c, 0] * SCALE).astype(jnp.bfloat16)
        dkv_v[c, 1] = acc[c, 1].astype(jnp.bfloat16)
        return 0

    lax.fori_loop(0, N_CTX, pack, 0)


def attention(q, do, kv, span_of, doc_lengths):
    rows = jax.ShapeDtypeStruct((UNITS, SPAN, UNIT_HEADS * WIDTH), jnp.bfloat16)
    blocks = jax.ShapeDtypeStruct((N_CTX, 2, WIDTH, SPAN), jnp.bfloat16)
    table = pl.BlockSpec(memory_space=pltpu.HBM)
    here = pl.BlockSpec(memory_space=pltpu.VMEM)
    vmem = pltpu.VMEM
    return pl.pallas_call(
        attention_kernel,
        out_shape=(rows, rows, blocks),
        in_specs=[table, table, here, here, here],
        out_specs=(here, here, here),
        scratch_shapes=[
            pltpu.SMEM((N_CTX,), jnp.int32),
            pltpu.SMEM((MAX_BLOCKS,), jnp.int32),
            vmem(blocks.shape, jnp.float32),
            vmem((MAX_BLOCKS, COLS, SPAN), jnp.bfloat16),
            vmem((2, COLS, SPAN), jnp.bfloat16),
            vmem((2, COLS, SPAN), jnp.float32),
            vmem((WIDTH, COLS), jnp.bfloat16),
            vmem((WIDTH, COLS), jnp.bfloat16),
            vmem((COLS, WIDTH), jnp.bfloat16),
            vmem((COLS, WIDTH), jnp.bfloat16),
            vmem((COLS, 2 * WIDTH), jnp.float32),
            vmem((COLS, WIDTH), jnp.float32),
            vmem((COLS, WIDTH), jnp.float32),
            vmem((COLS, WIDTH), jnp.float32),
            vmem((SPAN, WIDTH), jnp.int32),
            pltpu.SMEM((N_CTX,), jnp.int32),
            pltpu.SMEM((4,), jnp.int32),
            pltpu.SemaphoreType.DMA((2,)),
        ],
        compiler_params=pltpu.CompilerParams(vmem_limit_bytes=40 * 1024 * 1024),
        name="attention",
    )(span_of, doc_lengths, q, do, kv)


MESH_IDS = pl.DeviceIdType.MESH


def place(z_size):
    ctx, head = lax.axis_index("ctx"), lax.axis_index("head")
    return ctx, head, ctx // (2 * z_size), (ctx // 2) % z_size, ctx % 2


def meet(group, ctx, head, core, heads, others):
    barrier = pltpu.get_barrier_semaphore()
    base = ctx - core

    def greet(step, _):
        peer = (core * heads + head + step) % group
        pl.semaphore_signal(
            barrier, inc=1, device_id=(base + peer // heads, peer % heads), device_id_type=MESH_IDS
        )
        return 0

    lax.fori_loop(1, group, greet, 0)
    for other in others:
        pl.semaphore_signal(barrier, inc=1, device_id=(other, head), device_id_type=MESH_IDS)
    pl.semaphore_wait(barrier, group - 1 + len(others))


def arrived(ref, sem):
    pltpu.make_async_copy(ref, ref, sem).wait()


def send(src, dst, send_sem, recv_sem, ctx, head):
    pltpu.make_async_remote_copy(
        src_ref=src, dst_ref=dst, send_sem=send_sem, recv_sem=recv_sem,
        device_id=(ctx, head), device_id_type=MESH_IDS,
    ).start()


def gather_kernel(
    z_size, heads,
    q_hbm, do_hbm, k_hbm, v_hbm, q_out, do_out, kv_out, q_in, do_in, k_in, v_in,
    row_send, row_recv, piece_send, piece_recv, ring_send, right_recv, left_recv,
    cross_recv, twin_send, twin_recv, local_sem, load_sem,
):
    loads = []
    for n, (src, dst) in enumerate(((k_hbm, k_in), (v_hbm, v_in), (q_hbm, q_in), (do_hbm, do_in))):
        loads.append(pltpu.make_async_copy(src, dst, load_sem.at[n]))
        loads[-1].start()
    ctx, head, x, z, core = place(z_size)
    group = 2 * heads
    base = ctx - core
    mine = core * heads + head
    wide = q_in.shape[1] // group

    def index(x_at, z_at):
        return (x_at * z_size + z_at) * 2 + core

    right, left = index(x, (z + 1) % z_size), index(x, (z + z_size - 1) % z_size)
    cross, twin = index(1 - x, z), base + 1 - core
    meet(group, ctx, head, core, heads, (right, left, cross))

    def piece_cols(at):
        return pl.ds(pl.multiple_of(at * WIDTH, WIDTH), WIDTH)

    def row_cols(at):
        peer_core, peer_head = at // heads, at % heads
        return pl.ds(pl.multiple_of((peer_head * 2 + peer_core) * wide, WIDTH), wide)

    def send_pieces(step, _):
        peer = (head + step) % heads
        for side, ref in enumerate((k_in, v_in)):
            send(
                ref.at[:, piece_cols(peer)], kv_out.at[ctx, side, head],
                piece_send, piece_recv, ctx, peer,
            )
        return 0

    loads[0].wait()
    loads[1].wait()
    lax.fori_loop(1, heads, send_pieces, 0)
    own = []
    for side, ref in enumerate((k_in, v_in)):
        own.append(
            pltpu.make_async_copy(ref.at[:, piece_cols(head)], kv_out.at[ctx, side, head], local_sem.at[side])
        )
        own[-1].start()

    rows_left = []

    def start_rows(src, dst, which):
        def step_rows(step, _):
            peer = (mine + step) % group
            send(
                src.at[:, row_cols(peer)], dst.at[mine],
                row_send.at[which], row_recv.at[which], base + peer // heads, peer % heads,
            )
            return 0

        rows_left.extend((step, step_rows) for step in range(1, group))
        copy = pltpu.make_async_copy(src.at[:, row_cols(mine)], dst.at[mine], local_sem.at[2 + which])
        copy.start()
        own.append(copy)

    def send_some(count):
        while rows_left and count > 0:
            first, which = rows_left[0]
            run = 0
            while rows_left and run < count and rows_left[0][1] is which:
                rows_left.pop(0)
                run += 1
            lax.fori_loop(first, first + run, which, 0)
            count -= run

    loads[2].wait()
    start_rows(q_in, q_out, 0)
    loads[3].wait()
    start_rows(do_in, do_out, 1)
    send_some(3)
    own[0].wait()
    own[1].wait()
    pieces = kv_out.at[ctx, :, pl.ds(0, heads - 1)]
    arrived(pieces, piece_recv)

    sent = []

    def forward(block, to, recv):
        sem = ring_send.at[len(sent)]
        send(kv_out.at[block], kv_out.at[block], sem, recv, to, head)
        sent.append((block, sem))

    def share(block):
        send(kv_out.at[block], kv_out.at[block], twin_send, twin_recv, twin, head)

    far = z_size // 2
    reach = ((far, far - 1), (far - 1, far))
    forward(ctx, cross, cross_recv)
    forward(ctx, right, right_recv.at[0, 0])
    forward(ctx, left, left_recv.at[0, 0])
    share(ctx)
    send_some(4)
    arrived(kv_out.at[cross], cross_recv)
    forward(cross, right, right_recv.at[1, 0])
    forward(cross, left, left_recv.at[1, 0])
    share(cross)
    for d in range(1, far + 1):
        for plane in range(2):
            at_x = x if plane == 0 else 1 - x
            for way in range(2):
                if d > reach[plane][way]:
                    continue
                recv, to = ((right_recv, right), (left_recv, left))[way]
                origin = (z + z_size - d) % z_size if way == 0 else (z + d) % z_size
                block = index(at_x, origin)
                arrived(kv_out.at[block], recv.at[plane, d - 1])
                if d < reach[plane][way]:
                    forward(block, to, recv.at[plane, d])
                share(block)
                send_some(2)

    send_some(len(rows_left))
    arrived(pieces, piece_send)
    for block, sem in sent:
        arrived(kv_out.at[block], sem)
    half = kv_out.at[pl.ds(0, 2 * z_size)]
    arrived(half, twin_send)
    arrived(half, twin_recv)
    for which, dst in enumerate((q_out, do_out)):
        own[2 + which].wait()
        rows = dst.at[pl.ds(0, group - 1)]
        arrived(rows, row_send.at[which])
        arrived(rows, row_recv.at[which])


def gather(q, do, k, v, z_size, heads):
    tokens = q.shape[0]
    group = 2 * heads
    far = z_size // 2
    rows = jax.ShapeDtypeStruct((group, tokens, q.shape[1] // group), q.dtype)
    kv = jax.ShapeDtypeStruct((4 * z_size, 2, heads, tokens, WIDTH), q.dtype)
    hbm = pl.BlockSpec(memory_space=pltpu.HBM)
    here = pl.BlockSpec(memory_space=pltpu.VMEM)
    dma = pltpu.SemaphoreType.DMA
    return pl.pallas_call(
        functools.partial(gather_kernel, z_size, heads),
        out_shape=(rows, rows, kv),
        in_specs=[hbm] * 4,
        out_specs=(here, here, here),
        scratch_shapes=[pltpu.VMEM(a.shape, a.dtype) for a in (q, do, k, v)] + [
            dma((2,)), dma((2,)), dma, dma, dma((4 * far - 2 + 1,)), dma((2, far)), dma((2, far)),
            dma, dma, dma, dma((4,)), dma((4,)),
        ],
        compiler_params=pltpu.CompilerParams(collective_id=0, has_side_effects=True, vmem_limit_bytes=32 * 1024 * 1024),
        name="gather",
    )(q, do, k, v)


def scatter_kernel(
    z_size, heads,
    o_in, dq_in, dkv_in, o_out, dq_out, dk_out, dv_out,
    part, twin_part, right_part, left_part, cross_part, final,
    row_send, row_recv, piece_send, piece_recv, ring_send, right_recv, left_recv,
    cross_recv, twin_send, twin_recv, local_sem,
):
    ctx, head, x, z, core = place(z_size)
    group = 2 * heads
    base = ctx - core
    mine = core * heads + head
    wide = o_in.shape[2]

    def index(x_at, z_at):
        return (x_at * z_size + z_at) * 2 + core

    right, left = index(x, (z + 1) % z_size), index(x, (z + z_size - 1) % z_size)
    cross, twin = index(1 - x, z), base + 1 - core
    meet(group, ctx, head, core, heads, (right, left, cross))

    far = z_size // 2
    reach = ((far, far - 1), (far - 1, far))
    steps = []
    for back in range(far):
        for plane, way in ((0, 0), (1, 1), (1, 0), (0, 1)):
            d = reach[plane][way] - back
            if d > 0:
                steps.append((plane, way, d, back))

    def slot(plane, way, d):
        at_x = x if plane == 0 else 1 - x
        at_z = (z + d) % z_size if way == 0 else (z + z_size - d) % z_size
        return at_x * z_size + at_z

    order = [slot(plane, way, d) for plane, way, d, _ in steps]
    order += [slot(1, 0, 0), slot(0, 0, 0)]
    to_twin = list(enumerate(order))

    def feed_twin(count):
        for n, block in to_twin[:count]:
            send(dkv_in.at[block, 1 - core], twin_part.at[block], twin_send, twin_recv.at[n], twin, head)
        del to_twin[:count]

    feed_twin(6)

    def row_cols(at):
        return pl.ds(pl.multiple_of(((at % heads) * 2 + at // heads) * wide, WIDTH), wide)

    own = []

    rows_left = []

    def start_rows(src, dst, which):
        def step_rows(step, _):
            peer = (mine + step) % group
            send(
                src.at[peer], dst.at[:, row_cols(mine)],
                row_send.at[which], row_recv.at[which], base + peer // heads, peer % heads,
            )
            return 0

        rows_left.extend((step, step_rows) for step in range(1, group))
        copy = pltpu.make_async_copy(src.at[mine], dst.at[:, row_cols(mine)], local_sem.at[1 + which])
        copy.start()
        own.append(copy)

    def send_some(count):
        while rows_left and count > 0:
            first, which = rows_left[0]
            run = 0
            while rows_left and run < count and rows_left[0][1] is which:
                rows_left.pop(0)
                run += 1
            lax.fori_loop(first, first + run, which, 0)
            count -= run

    def combine(block, extras, last=False):
        def add_half(side, _):
            total = dkv_in[block, core, side].astype(jnp.float32) + twin_part[block, side].astype(jnp.float32)
            for ref, at in extras:
                total = total + ref[at + (side,)].astype(jnp.float32)
            if last:
                final[side] = total.T.astype(final.dtype).reshape(final.shape[1:])
            else:
                part[block, side] = total.astype(part.dtype)
            return 0

        lax.fori_loop(0, 2, add_half, 0)

    start_rows(o_in, o_out, 0)
    start_rows(dq_in, dq_out, 1)
    sent = []
    for n, (plane, way, d, back) in enumerate(steps):
        block = order[n]
        recv, buf, to = ((right_recv, right_part, right), (left_recv, left_part, left))[way]
        arrived(twin_part.at[block], twin_recv.at[n])
        extras = []
        if back > 0:
            arrived(buf.at[plane, back - 1], recv.at[plane, back - 1])
            extras = [(buf, (plane, back - 1))]
        combine(block, extras)
        send(part.at[block], buf.at[plane, back], ring_send.at[n], recv.at[plane, back], to, head)
        sent.append((block, ring_send.at[n]))
        feed_twin(1)
        send_some(3)
    feed_twin(len(to_twin))
    send_some(len(rows_left))
    for plane in (1, 0):
        n = len(steps) + 1 - plane
        block = order[n]
        arrived(twin_part.at[block], twin_recv.at[n])
        last_right, last_left = reach[plane][0] - 1, reach[plane][1] - 1
        arrived(right_part.at[plane, last_right], right_recv.at[plane, last_right])
        arrived(left_part.at[plane, last_left], left_recv.at[plane, last_left])
        extras = [(right_part, (plane, last_right)), (left_part, (plane, last_left))]
        if plane == 0:
            arrived(cross_part.at[0], cross_recv)
            extras.append((cross_part, (0,)))
        combine(block, extras, last=plane == 0)
        if plane == 1:
            send(part.at[block], cross_part.at[0], ring_send.at[n], cross_recv, cross, head)
            sent.append((block, ring_send.at[n]))

    my_cols = pl.ds(pl.multiple_of(head * WIDTH, WIDTH), WIDTH)

    def send_pieces(step, _):
        peer = (head + step) % heads
        for side, dst in enumerate((dk_out, dv_out)):
            send(final.at[side, peer], dst.at[:, my_cols], piece_send, piece_recv.at[side], ctx, peer)
        return 0

    lax.fori_loop(1, heads, send_pieces, 0)
    for side, dst in enumerate((dk_out, dv_out)):
        copy = pltpu.make_async_copy(final.at[side, head], dst.at[:, my_cols], local_sem.at[3 + side])
        copy.start()
        own.append(copy)

    for copy in own:
        copy.wait()
    for block, sem in sent:
        arrived(part.at[block], sem)
    arrived(part.at[pl.ds(0, 2 * z_size)], twin_send)
    for which, dst in enumerate((o_out, dq_out)):
        rows = dst.at[:, pl.ds(0, (group - 1) * wide)]
        arrived(rows, row_send.at[which])
        arrived(rows, row_recv.at[which])
    arrived(final.at[:, pl.ds(0, heads - 1)], piece_send)
    for side, dst in enumerate((dk_out, dv_out)):
        arrived(dst.at[:, pl.ds(0, (heads - 1) * WIDTH)], piece_recv.at[side])


def scatter(o, dq, dkv, z_size, heads):
    group, tokens, wide = o.shape
    far = z_size // 2
    rows = jax.ShapeDtypeStruct((tokens, group * wide), o.dtype)
    pieces = jax.ShapeDtypeStruct((tokens, heads * WIDTH), o.dtype)
    block = dkv.shape[2:]
    here = pl.BlockSpec(memory_space=pltpu.VMEM)
    dma = pltpu.SemaphoreType.DMA
    return pl.pallas_call(
        functools.partial(scatter_kernel, z_size, heads),
        out_shape=(rows, rows, pieces, pieces),
        in_specs=[here] * 3,
        out_specs=(here,) * 4,
        scratch_shapes=[
            pltpu.VMEM((2 * z_size,) + block, dkv.dtype),
            pltpu.VMEM((2 * z_size,) + block, dkv.dtype),
            pltpu.VMEM((2, far) + block, dkv.dtype),
            pltpu.VMEM((2, far) + block, dkv.dtype),
            pltpu.VMEM((1,) + block, dkv.dtype),
            pltpu.VMEM((2, heads, tokens, WIDTH), dkv.dtype),
            dma((2,)), dma((2,)), dma, dma((2,)), dma((4 * far - 2 + 1,)), dma((2, far)), dma((2, far)),
            dma, dma, dma((2 * z_size,)), dma((5,)),
        ],
        compiler_params=pltpu.CompilerParams(
            collective_id=1, has_side_effects=True, vmem_limit_bytes=24 * 1024 * 1024
        ),
        name="scatter",
    )(o, dq, dkv)


def settle_kernel(*refs):
    count = len(refs) // 2
    sem = refs[-1]
    copies = [pltpu.make_async_copy(refs[i], refs[count + i], sem.at[i]) for i in range(count)]
    for copy in copies:
        copy.start()
    for copy in copies:
        copy.wait()


def settle(arrays):
    hbm = pl.BlockSpec(memory_space=pl.ANY)
    here = pl.BlockSpec(memory_space=pltpu.VMEM)
    return pl.pallas_call(
        settle_kernel,
        out_shape=tuple(jax.ShapeDtypeStruct(a.shape, a.dtype) for a in arrays),
        in_specs=[here] * len(arrays),
        out_specs=(hbm,) * len(arrays),
        scratch_shapes=[pltpu.SemaphoreType.DMA((len(arrays),))],
        compiler_params=pltpu.CompilerParams(vmem_limit_bytes=32 * 1024 * 1024),
        name="settle",
    )(*arrays)


def per_device(heads, z_size, queries, keys, values, output_gradient, doc_lengths, span_of):
    queries, output_gradient, keys, values, doc_lengths, span_of = (
        pltpu.with_memory_space_constraint(a, pltpu.HBM)
        for a in (queries, output_gradient, keys, values, doc_lengths, span_of)
    )
    q, do, kv = gather(queries, output_gradient, keys, values, z_size, heads)
    rows = (UNITS, SPAN, UNIT_HEADS * WIDTH)
    o, dq, dkv = attention(
        q.reshape(rows), do.reshape(rows), kv.reshape(N_CTX, 2, SPAN, WIDTH), span_of, doc_lengths
    )
    dkv = dkv.reshape((N_CTX // 2, 2) + dkv.shape[1:])
    return settle(scatter(o.reshape(q.shape), dq.reshape(q.shape), dkv, z_size, heads))


def solution(mesh):
    shard = P(("ctx", "head"), None)
    return jax.shard_map(
        functools.partial(per_device, mesh.shape["head"], N_CTX // 4),
        mesh=mesh,
        in_specs=(shard, shard, shard, shard, P(), P()),
        out_specs=(shard, shard, shard, shard),
        check_vma=False,
    )
```

```python
import functools
import math

import jax
import jax.numpy as jnp
from jax import lax
from jax.experimental import pallas as pl
from jax.experimental.pallas import tpu as pltpu
from jax.sharding import PartitionSpec as P

N_CTX = 32
SPAN = 256
WIDTH = 128
UNIT_HEADS = 4
UNITS = 2
MAX_BLOCKS = 18
COLS = UNIT_HEADS * SPAN
LIMIT = 2.0**60
SCALE = WIDTH**-0.5
LOG2_SCALE = SCALE * math.log2(math.e)
NEG = -1e30


NT = (((1,), (1,)), ((), ()))


def attention_kernel(
    span_hbm, len_hbm, rows_v, kv_v,
    out_v, dkv_v,
    holder, slots, acc, probs, grads, wide_buf,
    q_t, do_t, q_s, do_s, o_acc, dq_acc, level_b, delta_b, starts,
    span_ref, len_ref, table_sem,
):
    load_span = pltpu.make_async_copy(span_hbm, span_ref, table_sem.at[0])
    load_len = pltpu.make_async_copy(len_hbm, len_ref, table_sem.at[1])
    load_span.start()
    load_len.start()
    ctx = lax.axis_index("ctx")
    first_unit = ctx - ctx % UNITS

    def clear(c, _):
        acc[c] = jnp.zeros((2, WIDTH, SPAN), jnp.float32)
        return 0

    lax.fori_loop(0, N_CTX, clear, 0)

    load_span.wait()
    load_len.wait()

    def note(c, _):
        holder[span_ref[c]] = c
        return 0

    lax.fori_loop(0, N_CTX, note, 0)

    ends = []
    running = jnp.int32(0)
    for j in range(4):
        running = running + len_ref[j]
        ends.append(running)

    def doc_start(pos):
        start = jnp.zeros_like(pos)
        for end in ends:
            start = jnp.where(pos >= end, end, start)
        return start

    def rows_of(h):
        return pl.ds(h * SPAN, SPAN)

    def lanes_of(h):
        return pl.ds(h * WIDTH, WIDTH)

    def both(x):
        return jnp.concatenate([x, x], axis=1)

    def beside(parts):
        return parts[0] if len(parts) == 1 else jnp.concatenate(parts, axis=1)

    def below(parts):
        return parts[0] if len(parts) == 1 else jnp.concatenate(parts, axis=0)

    ones = jnp.ones((SPAN, WIDTH), jnp.bfloat16)

    def unit(u, _):
        group = rows_v.shape[0] // UNITS
        own = pl.ds(pl.multiple_of(u * group, group), group)

        def head_rows(side, h):
            return rows_v[own, side, :, lanes_of(h)].reshape(SPAN, WIDTH)

        def put_rows(side, h, value):
            out_v[own, side, :, lanes_of(h)] = value.astype(jnp.bfloat16).reshape(group, SPAN // group, WIDTH)

        span = span_ref[first_unit + u]
        first_pos = span * SPAN
        first_block = doc_start(first_pos) // SPAN
        last_start = doc_start(first_pos + (SPAN - 1))
        blocks = span - first_block + 1
        edges = jnp.maximum(jnp.minimum((last_start + (SPAN - 1)) // SPAN, span) - first_block, 0)
        starts[...] = doc_start(first_pos + lax.broadcasted_iota(jnp.int32, (SPAN, WIDTH), 0))

        for h in range(UNIT_HEADS):
            q_h = head_rows(0, h)
            q_s[rows_of(h)] = q_h
            q_t[:, rows_of(h)] = q_h.T

        def allowed_at(t):
            k_pos = t * SPAN + lax.broadcasted_iota(jnp.int32, (SPAN, SPAN), 1)
            q_pos = first_pos + lax.broadcasted_iota(jnp.int32, (SPAN, SPAN), 0)
            return (k_pos <= q_pos) & (k_pos >= both(starts[...]))

        def halves_max(s):
            return jnp.maximum(s[:, :WIDTH], s[:, WIDTH:])

        def row_max(x):
            return jnp.broadcast_to(jnp.max(x, axis=1, keepdims=True), x.shape)

        def score(slot, count):
            for n in range(count):
                wide_buf[n] = lax.dot_general(
                    q_s[...], kv_v[slots[slot + n], 0], NT, preferred_element_type=jnp.float32
                )

        def weigh(slot, count, allowed=None, take_top=False):
            for n in range(count):
                for h in range(UNIT_HEADS):
                    s = wide_buf[n, rows_of(h)]
                    if allowed is not None:
                        s = jnp.where(allowed, s, NEG)
                    if take_top:
                        level = row_max(halves_max(s))
                        level_b[rows_of(h)] = level
                    else:
                        level = level_b[rows_of(h)]
                    p = jnp.exp2((s - both(level)) * LOG2_SCALE)
                    probs[slot + n, rows_of(h)] = p.astype(jnp.bfloat16)

        def attend(slot, count):
            values = below([beside([kv_v[slots[slot + n], 1], ones]) for n in range(count)])
            o_acc[...] += jnp.dot(
                beside([probs[slot + n] for n in range(count)]), values, preferred_element_type=jnp.float32
            )

        def masked_step(i, _):
            score(i, 1)
            weigh(i, 1, allowed_at(first_block + i - 2))
            return 0

        def attend_step(i, _):
            attend(i, 1)
            return 0

        inner_from = edges + 2
        inner = blocks - 1 - edges
        slots[0] = first_unit
        slots[1] = holder[span]

        def place_slot(i, _):
            slots[i + 2] = holder[first_block + i]
            return 0

        lax.fori_loop(0, blocks - 1, place_slot, 0)
        probs[0] = jnp.zeros((COLS, SPAN), jnp.bfloat16)
        o_acc[...] = jnp.zeros_like(o_acc)
        score(1, 1)
        weigh(1, 1, allowed_at(span), take_top=True)
        lax.fori_loop(2, inner_from, masked_step, 0)
        lax.fori_loop(1, edges, attend_step, 0)

        def pair_step(j, _):
            slot = inner_from + 2 * j
            score(slot, 2)
            attend(slot - 2, 2)
            weigh(slot, 2)
            return 0

        lax.fori_loop(0, inner // 2, pair_step, 0)
        last = inner_from + inner - inner % 2

        @pl.when(inner % 2 == 1)
        def _():
            score(last, 1)
            attend(last - 2, 2)
            weigh(last, 1)
            attend(last, 1)

        @pl.when(inner % 2 == 0)
        def _():
            attend(last - 2, 2)

        worst = jnp.max(jnp.where(o_acc[:, WIDTH:] < LIMIT, 0.0, 1.0))

        @pl.when(worst > 0.0)
        def _():
            o_acc[...] = jnp.zeros_like(o_acc)
            level_b[...] = jnp.full_like(level_b, NEG)

            def top_step(i, _):
                k = kv_v[slots[i], 0]
                allowed = allowed_at(jnp.where(i == 1, span, first_block + i - 2))
                for h in range(UNIT_HEADS):
                    s = lax.dot_general(q_s[rows_of(h)], k, NT, preferred_element_type=jnp.float32)
                    s = jnp.where(allowed, s, NEG)
                    level_b[rows_of(h)] = jnp.maximum(level_b[rows_of(h)], halves_max(s))
                return 0

            lax.fori_loop(1, blocks + 1, top_step, 0)
            for h in range(UNIT_HEADS):
                level_b[rows_of(h)] = row_max(level_b[rows_of(h)])
            score(1, 1)
            weigh(1, 1, allowed_at(span))
            lax.fori_loop(2, blocks + 1, masked_step, 0)
            lax.fori_loop(1, blocks + 1, attend_step, 0)

        for h in range(UNIT_HEADS):
            inverse = 1.0 / o_acc[rows_of(h), WIDTH:]
            out = (o_acc[rows_of(h), :WIDTH] * inverse).astype(jnp.bfloat16)
            put_rows(0, h, out)
            scaled = (head_rows(1, h).astype(jnp.float32) * inverse).astype(jnp.bfloat16)
            do_s[rows_of(h)] = scaled
            do_t[:, rows_of(h)] = scaled.T
            delta = jnp.sum(scaled.astype(jnp.float32) * out.astype(jnp.float32), axis=1, keepdims=True)
            delta_b[rows_of(h)] = jnp.broadcast_to(delta, (SPAN, WIDTH))
        dq_acc[...] = jnp.zeros_like(dq_acc)

        def backward(i, count):
            places = [slots[i + n] for n in range(count)]
            for n, c in enumerate(places):
                wide_buf[n] = lax.dot_general(
                    do_s[...], kv_v[c, 1], NT, preferred_element_type=jnp.float32
                )
            for n in range(count):
                for h in range(UNIT_HEADS):
                    p = probs[i + n, rows_of(h)].astype(jnp.float32)
                    ds = p * (wide_buf[n, rows_of(h)] - both(delta_b[rows_of(h)]))
                    grads[n, rows_of(h)] = ds.astype(jnp.bfloat16)
            dv = jnp.dot(
                do_t[...], beside([probs[i + n] for n in range(count)]), preferred_element_type=jnp.float32
            )
            ds = beside([grads[n] for n in range(count)])
            dk = jnp.dot(q_t[...], ds, preferred_element_type=jnp.float32)
            dq_acc[...] += jnp.dot(
                ds, below([kv_v[c, 0] for c in places]), preferred_element_type=jnp.float32
            )
            for n, c in enumerate(places):
                part = slice(n * SPAN, (n + 1) * SPAN)
                acc[c, 0] += dk[:, part]
                acc[c, 1] += dv[:, part]

        def grad_step(j, _):
            backward(2 * j + 1, 2)
            return 0

        lax.fori_loop(0, blocks // 2, grad_step, 0)

        @pl.when(blocks % 2 == 1)
        def _():
            backward(blocks, 1)

        for h in range(UNIT_HEADS):
            put_rows(1, h, dq_acc[rows_of(h)] * SCALE)
        return 0

    lax.fori_loop(0, UNITS, unit, 0)

    def pack(c, _):
        dkv_v[c, 0] = (acc[c, 0] * SCALE).astype(jnp.bfloat16)
        dkv_v[c, 1] = acc[c, 1].astype(jnp.bfloat16)
        return 0

    lax.fori_loop(0, N_CTX, pack, 0)


def attention(rows, kv, span_of, doc_lengths):
    blocks = jax.ShapeDtypeStruct((N_CTX, 2, WIDTH, SPAN), jnp.bfloat16)
    table = pl.BlockSpec(memory_space=pltpu.HBM)
    here = pl.BlockSpec(memory_space=pltpu.VMEM)
    vmem = pltpu.VMEM
    return pl.pallas_call(
        attention_kernel,
        out_shape=(jax.ShapeDtypeStruct(rows.shape, rows.dtype), blocks),
        in_specs=[table, table, here, here],
        out_specs=(here, here),
        scratch_shapes=[
            pltpu.SMEM((N_CTX,), jnp.int32),
            pltpu.SMEM((MAX_BLOCKS,), jnp.int32),
            vmem(blocks.shape, jnp.float32),
            vmem((MAX_BLOCKS, COLS, SPAN), jnp.bfloat16),
            vmem((2, COLS, SPAN), jnp.bfloat16),
            vmem((2, COLS, SPAN), jnp.float32),
            vmem((WIDTH, COLS), jnp.bfloat16),
            vmem((WIDTH, COLS), jnp.bfloat16),
            vmem((COLS, WIDTH), jnp.bfloat16),
            vmem((COLS, WIDTH), jnp.bfloat16),
            vmem((COLS, 2 * WIDTH), jnp.float32),
            vmem((COLS, WIDTH), jnp.float32),
            vmem((COLS, WIDTH), jnp.float32),
            vmem((COLS, WIDTH), jnp.float32),
            vmem((SPAN, WIDTH), jnp.int32),
            pltpu.SMEM((N_CTX,), jnp.int32),
            pltpu.SMEM((4,), jnp.int32),
            pltpu.SemaphoreType.DMA((2,)),
        ],
        compiler_params=pltpu.CompilerParams(vmem_limit_bytes=40 * 1024 * 1024),
        name="attention",
    )(span_of, doc_lengths, rows, kv)


MESH_IDS = pl.DeviceIdType.MESH


def place(z_size):
    ctx, head = lax.axis_index("ctx"), lax.axis_index("head")
    return ctx, head, ctx // (2 * z_size), (ctx // 2) % z_size, ctx % 2


def meet(group, ctx, head, core, heads, others):
    barrier = pltpu.get_barrier_semaphore()
    base = ctx - core

    def greet(step, _):
        peer = (core * heads + head + step) % group
        pl.semaphore_signal(
            barrier, inc=1, device_id=(base + peer // heads, peer % heads), device_id_type=MESH_IDS
        )
        return 0

    lax.fori_loop(1, group, greet, 0)
    for other in others:
        pl.semaphore_signal(barrier, inc=1, device_id=(other, head), device_id_type=MESH_IDS)
    pl.semaphore_wait(barrier, group - 1 + len(others))


def arrived(ref, sem):
    pltpu.make_async_copy(ref, ref, sem).wait()


def send(src, dst, send_sem, recv_sem, ctx, head):
    pltpu.make_async_remote_copy(
        src_ref=src, dst_ref=dst, send_sem=send_sem, recv_sem=recv_sem,
        device_id=(ctx, head), device_id_type=MESH_IDS,
    ).start()


def gather_kernel(
    z_size, heads,
    q_hbm, do_hbm, k_hbm, v_hbm, rows_out, kv_out, rows_in, pieces_in,
    row_send, row_recv, piece_send, piece_recv, ring_send, right_recv, left_recv,
    cross_recv, twin_send, twin_recv, local_sem, load_sem,
):
    loads = []
    for n, (src, dst) in enumerate((
        (k_hbm, pieces_in.at[0]), (v_hbm, pieces_in.at[1]), (q_hbm, rows_in.at[0]), (do_hbm, rows_in.at[1])
    )):
        loads.append(pltpu.make_async_copy(src, dst, load_sem.at[n]))
        loads[-1].start()
    ctx, head, x, z, core = place(z_size)
    group = 2 * heads
    base = ctx - core
    mine = core * heads + head
    wide = rows_in.shape[2] // group

    def index(x_at, z_at):
        return (x_at * z_size + z_at) * 2 + core

    def block(x_at, z_at):
        return kv_out.at[x_at, z_at * 2 + core]

    right_z, left_z = (z + 1) % z_size, (z + z_size - 1) % z_size
    right, left = index(x, right_z), index(x, left_z)
    cross, twin = index(1 - x, z), base + 1 - core
    meet(group, ctx, head, core, heads, (right, left, cross))

    def piece_cols(at):
        return pl.ds(pl.multiple_of(at * WIDTH, WIDTH), WIDTH)

    def row_cols(at):
        peer_core, peer_head = at // heads, at % heads
        return pl.ds(pl.multiple_of((peer_head * 2 + peer_core) * wide, WIDTH), wide)

    mine_block = block(x, z)

    def send_pieces(step, _):
        peer = (head + step) % heads
        send(pieces_in.at[:, :, piece_cols(peer)], mine_block.at[:, head], piece_send, piece_recv, ctx, peer)
        return 0

    loads[0].wait()
    loads[1].wait()
    lax.fori_loop(1, heads, send_pieces, 0)
    own_piece = pltpu.make_async_copy(
        pieces_in.at[:, :, piece_cols(head)], mine_block.at[:, head], local_sem.at[0]
    )
    own_piece.start()
    loads[2].wait()
    loads[3].wait()
    own_rows = pltpu.make_async_copy(rows_in.at[:, :, row_cols(mine)], rows_out.at[mine], local_sem.at[1])
    own_rows.start()

    def send_row(step, _):
        peer = (mine + step) % group
        send(
            rows_in.at[:, :, row_cols(peer)], rows_out.at[mine], row_send, row_recv,
            base + peer // heads, peer % heads,
        )
        return 0

    rows_sent = [1]

    def send_rows(count):
        stop = min(rows_sent[0] + count, group)
        lax.fori_loop(rows_sent[0], stop, send_row, 0)
        rows_sent[0] = stop

    send_rows(2)
    own_piece.wait()
    pieces = mine_block.at[:, pl.ds(0, heads - 1)]
    arrived(pieces, piece_recv)

    sent = []

    def forward(what, to, recv):
        sem = ring_send.at[len(sent)]
        send(what, what, sem, recv, to, head)
        sent.append((what, sem))

    def share(z_at):
        both_x = kv_out.at[:, z_at * 2 + core]
        send(both_x, both_x, twin_send, twin_recv, twin, head)

    far = z_size // 2
    reach = ((far, far - 1), (far - 1, far))
    forward(mine_block, cross, cross_recv)
    forward(mine_block, right, right_recv.at[0, 0])
    forward(mine_block, left, left_recv.at[0, 0])
    send_rows(2)
    cross_block = block(1 - x, z)
    arrived(cross_block, cross_recv)
    forward(cross_block, right, right_recv.at[1, 0])
    forward(cross_block, left, left_recv.at[1, 0])
    share(z)
    for d in range(1, far + 1):
        for plane in range(2):
            at_x = x if plane == 0 else 1 - x
            for way in range(2):
                if d > reach[plane][way]:
                    continue
                recv, to = ((right_recv, right), (left_recv, left))[way]
                origin = (z + z_size - d) % z_size if way == 0 else (z + d) % z_size
                what = block(at_x, origin)
                arrived(what, recv.at[plane, d - 1])
                if d < reach[plane][way]:
                    forward(what, to, recv.at[plane, d])
                if plane == 1:
                    share(origin)
                send_rows(1)

    send_rows(group)
    arrived(pieces, piece_send)
    for what, sem in sent:
        arrived(what, sem)
    arrived(kv_out.at[0], twin_send)
    arrived(kv_out.at[0], twin_recv)
    own_rows.wait()
    rows = rows_out.at[pl.ds(0, group - 1)]
    arrived(rows, row_send)
    arrived(rows, row_recv)


def gather(q, do, k, v, z_size, heads):
    tokens = q.shape[0]
    group = 2 * heads
    far = z_size // 2
    rows = jax.ShapeDtypeStruct((group, 2, tokens, q.shape[1] // group), q.dtype)
    kv = jax.ShapeDtypeStruct((2, 2 * z_size, 2, heads, tokens, WIDTH), q.dtype)
    hbm = pl.BlockSpec(memory_space=pltpu.HBM)
    here = pl.BlockSpec(memory_space=pltpu.VMEM)
    dma = pltpu.SemaphoreType.DMA
    return pl.pallas_call(
        functools.partial(gather_kernel, z_size, heads),
        out_shape=(rows, kv),
        in_specs=[hbm] * 4,
        out_specs=(here, here),
        scratch_shapes=[
            pltpu.VMEM((2,) + q.shape, q.dtype), pltpu.VMEM((2,) + k.shape, k.dtype),
            dma, dma, dma, dma, dma((4 * far - 2 + 1,)), dma((2, far)), dma((2, far)),
            dma, dma, dma, dma((2,)), dma((4,)),
        ],
        compiler_params=pltpu.CompilerParams(
            collective_id=0, has_side_effects=True, vmem_limit_bytes=32 * 1024 * 1024
        ),
        name="gather",
    )(q, do, k, v)


def scatter_kernel(
    z_size, heads,
    rows_in, dkv_in, rows_out, pieces_out,
    part, twin_part, right_part, left_part, cross_part, final,
    row_send, row_recv, piece_send, piece_recv, ring_send, right_recv, left_recv,
    cross_recv, twin_send, twin_recv, local_sem,
):
    ctx, head, x, z, core = place(z_size)
    group = 2 * heads
    base = ctx - core
    mine = core * heads + head
    wide = rows_in.shape[3]

    def index(x_at, z_at):
        return (x_at * z_size + z_at) * 2 + core

    right, left = index(x, (z + 1) % z_size), index(x, (z + z_size - 1) % z_size)
    cross, twin = index(1 - x, z), base + 1 - core
    meet(group, ctx, head, core, heads, (right, left, cross))

    far = z_size // 2
    reach = ((far, far - 1), (far - 1, far))
    steps = []
    for back in range(far):
        for plane, way in ((0, 0), (1, 1), (1, 0), (0, 1)):
            d = reach[plane][way] - back
            if d > 0:
                steps.append((plane, way, d, back))

    to_twin = [far] + [s * d for d in range(far - 1, 0, -1) for s in (1, -1)] + [0]
    place_of = {offset: n for n, offset in enumerate(to_twin)}
    fed, had = [0], [0]

    def z_of(offset):
        return (z + z_size + offset) % z_size

    def feed_twin(count):
        for n in range(fed[0], min(fed[0] + count, len(to_twin))):
            at = z_of(to_twin[n])
            send(dkv_in.at[:, at, 1 - core], twin_part.at[:, at], twin_send, twin_recv.at[n], twin, head)
        fed[0] = min(fed[0] + count, len(to_twin))

    def need_twin(offset):
        n = place_of[far if abs(offset) == far else offset]
        while had[0] <= n:
            arrived(twin_part.at[:, z_of(to_twin[had[0]])], twin_recv.at[had[0]])
            had[0] += 1

    feed_twin(3)
    my_rows = pl.ds(pl.multiple_of((head * 2 + core) * wide, WIDTH), wide)

    def send_row(step, _):
        peer = (mine + step) % group
        send(
            rows_in.at[peer], rows_out.at[:, :, my_rows], row_send, row_recv,
            base + peer // heads, peer % heads,
        )
        return 0

    rows_sent = [1]

    def send_rows(count):
        stop = min(rows_sent[0] + count, group)
        lax.fori_loop(rows_sent[0], stop, send_row, 0)
        rows_sent[0] = stop

    own_rows = pltpu.make_async_copy(rows_in.at[mine], rows_out.at[:, :, my_rows], local_sem.at[0])
    own_rows.start()

    def combine(at_x, at_z, extras, last=False):
        def add_half(side, _):
            total = dkv_in[at_x, at_z, core, side].astype(jnp.float32)
            total = total + twin_part[at_x, at_z, side].astype(jnp.float32)
            for ref, at in extras:
                total = total + ref[at + (side,)].astype(jnp.float32)
            if last:
                final[side] = total.T.astype(final.dtype).reshape(final.shape[1:])
            else:
                part[at_x, at_z, side] = total.astype(part.dtype)
            return 0

        lax.fori_loop(0, 2, add_half, 0)

    sent = []
    for n, (plane, way, d, back) in enumerate(steps):
        offset = d if way == 0 else -d
        at_x, at_z = (x if plane == 0 else 1 - x), z_of(offset)
        recv, buf, to = ((right_recv, right_part, right), (left_recv, left_part, left))[way]
        need_twin(offset)
        extras = []
        if back > 0:
            arrived(buf.at[plane, back - 1], recv.at[plane, back - 1])
            extras = [(buf, (plane, back - 1))]
        combine(at_x, at_z, extras)
        send(part.at[at_x, at_z], buf.at[plane, back], ring_send.at[n], recv.at[plane, back], to, head)
        sent.append((part.at[at_x, at_z], ring_send.at[n]))
        if n % 2 == 0:
            feed_twin(1)
        send_rows(1)
    feed_twin(len(to_twin))
    send_rows(group)
    need_twin(0)
    for plane in (1, 0):
        at_x = x if plane == 0 else 1 - x
        last_right, last_left = reach[plane][0] - 1, reach[plane][1] - 1
        arrived(right_part.at[plane, last_right], right_recv.at[plane, last_right])
        arrived(left_part.at[plane, last_left], left_recv.at[plane, last_left])
        extras = [(right_part, (plane, last_right)), (left_part, (plane, last_left))]
        if plane == 0:
            arrived(cross_part.at[0], cross_recv)
            extras.append((cross_part, (0,)))
        combine(at_x, z, extras, last=plane == 0)
        if plane == 1:
            sem = ring_send.at[len(steps)]
            send(part.at[at_x, z], cross_part.at[0], sem, cross_recv, cross, head)
            sent.append((part.at[at_x, z], sem))

    my_cols = pl.ds(pl.multiple_of(head * WIDTH, WIDTH), WIDTH)

    def send_pieces(step, _):
        peer = (head + step) % heads
        send(final.at[:, peer], pieces_out.at[:, :, my_cols], piece_send, piece_recv, ctx, peer)
        return 0

    lax.fori_loop(1, heads, send_pieces, 0)
    own_piece = pltpu.make_async_copy(final.at[:, head], pieces_out.at[:, :, my_cols], local_sem.at[1])
    own_piece.start()
    own_piece.wait()
    own_rows.wait()
    for what, sem in sent:
        arrived(what, sem)
    arrived(part, twin_send)
    rows = rows_out.at[:, :, pl.ds(0, (group - 1) * wide)]
    arrived(rows, row_send)
    arrived(rows, row_recv)
    arrived(final.at[:, pl.ds(0, heads - 1)], piece_send)
    arrived(pieces_out.at[:, :, pl.ds(0, (heads - 1) * WIDTH)], piece_recv)


def scatter(rows, dkv, z_size, heads):
    group, _, tokens, wide = rows.shape
    far = z_size // 2
    block = dkv.shape[3:]
    here = pl.BlockSpec(memory_space=pltpu.VMEM)
    dma = pltpu.SemaphoreType.DMA
    return pl.pallas_call(
        functools.partial(scatter_kernel, z_size, heads),
        out_shape=(
            jax.ShapeDtypeStruct((2, tokens, group * wide), rows.dtype),
            jax.ShapeDtypeStruct((2, tokens, heads * WIDTH), rows.dtype),
        ),
        in_specs=[here] * 2,
        out_specs=(here, here),
        scratch_shapes=[
            pltpu.VMEM((2, z_size) + block, dkv.dtype),
            pltpu.VMEM((2, z_size) + block, dkv.dtype),
            pltpu.VMEM((2, far) + block, dkv.dtype),
            pltpu.VMEM((2, far) + block, dkv.dtype),
            pltpu.VMEM((1,) + block, dkv.dtype),
            pltpu.VMEM((2, heads, tokens, WIDTH), dkv.dtype),
            dma, dma, dma, dma, dma((4 * far - 2 + 1,)), dma((2, far)), dma((2, far)),
            dma, dma, dma((z_size,)), dma((2,)),
        ],
        compiler_params=pltpu.CompilerParams(
            collective_id=1, has_side_effects=True, vmem_limit_bytes=24 * 1024 * 1024
        ),
        name="scatter",
    )(rows, dkv)


def settle_kernel(rows, pieces, o, dq, dk, dv, sem):
    copies = []
    for src, outs in ((rows, (o, dq)), (pieces, (dk, dv))):
        for n, out in enumerate(outs):
            copies.append(pltpu.make_async_copy(src.at[n], out, sem.at[len(copies)]))
            copies[-1].start()
    for copy in copies:
        copy.wait()


def settle(arrays):
    hbm = pl.BlockSpec(memory_space=pl.ANY)
    here = pl.BlockSpec(memory_space=pltpu.VMEM)
    return pl.pallas_call(
        settle_kernel,
        out_shape=tuple(jax.ShapeDtypeStruct(a.shape[1:], a.dtype) for a in arrays for _ in range(2)),
        in_specs=[here] * len(arrays),
        out_specs=(hbm,) * 4,
        scratch_shapes=[pltpu.SemaphoreType.DMA((4,))],
        compiler_params=pltpu.CompilerParams(vmem_limit_bytes=32 * 1024 * 1024),
        name="settle",
    )(*arrays)


def per_device(heads, z_size, queries, keys, values, output_gradient, doc_lengths, span_of):
    queries, output_gradient, keys, values, doc_lengths, span_of = (
        pltpu.with_memory_space_constraint(a, pltpu.HBM)
        for a in (queries, output_gradient, keys, values, doc_lengths, span_of)
    )
    rows, kv = gather(queries, output_gradient, keys, values, z_size, heads)
    outs, dkv = attention(rows, kv.reshape(N_CTX, 2, SPAN, WIDTH), span_of, doc_lengths)
    return settle(scatter(outs, dkv.reshape((2, z_size, 2) + dkv.shape[1:]), z_size, heads))


def solution(mesh):
    shard = P(("ctx", "head"), None)
    return jax.shard_map(
        functools.partial(per_device, mesh.shape["head"], N_CTX // 4),
        mesh=mesh,
        in_specs=(shard, shard, shard, shard, P(), P()),
        out_specs=(shard, shard, shard, shard),
        check_vma=False,
    )
```

```python
import functools
import math

import jax
import jax.numpy as jnp
from jax import lax
from jax.experimental import pallas as pl
from jax.experimental.pallas import tpu as pltpu
from jax.sharding import PartitionSpec as P

N_CTX = 32
SPAN = 256
WIDTH = 128
UNIT_HEADS = 4
UNITS = 2
MAX_BLOCKS = 18
COLS = UNIT_HEADS * SPAN
LIMIT = 2.0**60
SCALE = WIDTH**-0.5
LOG2_SCALE = SCALE * math.log2(math.e)
NEG = -1e30


NT = (((1,), (1,)), ((), ()))


def attention_kernel(
    span_hbm, len_hbm, rows_v, kv_v,
    out_v, dkv_v,
    holder, slots, acc, probs, grads, wide_buf,
    q_t, do_t, q_s, do_s, o_acc, dq_acc, level_b, delta_b, starts,
    span_ref, len_ref, table_sem,
):
    load_span = pltpu.make_async_copy(span_hbm, span_ref, table_sem.at[0])
    load_len = pltpu.make_async_copy(len_hbm, len_ref, table_sem.at[1])
    load_span.start()
    load_len.start()
    ctx = lax.axis_index("ctx")
    first_unit = ctx - ctx % UNITS

    def clear(c, _):
        acc[c] = jnp.zeros((2, WIDTH, SPAN), jnp.float32)
        return 0

    lax.fori_loop(0, N_CTX, clear, 0)

    load_span.wait()
    load_len.wait()

    def note(c, _):
        holder[span_ref[c]] = c
        return 0

    lax.fori_loop(0, N_CTX, note, 0)

    ends = []
    running = jnp.int32(0)
    for j in range(4):
        running = running + len_ref[j]
        ends.append(running)

    def doc_start(pos):
        start = jnp.zeros_like(pos)
        for end in ends:
            start = jnp.where(pos >= end, end, start)
        return start

    def rows_of(h):
        return pl.ds(h * SPAN, SPAN)

    def lanes_of(h):
        return pl.ds(h * WIDTH, WIDTH)

    def both(x):
        return jnp.concatenate([x, x], axis=1)

    def beside(parts):
        return parts[0] if len(parts) == 1 else jnp.concatenate(parts, axis=1)

    def below(parts):
        return parts[0] if len(parts) == 1 else jnp.concatenate(parts, axis=0)

    ones = jnp.ones((SPAN, WIDTH), jnp.bfloat16)

    def unit(u, _):
        group = rows_v.shape[0] // UNITS
        own = pl.ds(pl.multiple_of(u * group, group), group)

        def head_rows(side, h):
            return rows_v[own, side, :, lanes_of(h)].reshape(SPAN, WIDTH)

        def put_rows(side, h, value):
            out_v[own, side, :, lanes_of(h)] = value.astype(jnp.bfloat16).reshape(group, SPAN // group, WIDTH)

        span = span_ref[first_unit + u]
        first_pos = span * SPAN
        first_block = doc_start(first_pos) // SPAN
        last_start = doc_start(first_pos + (SPAN - 1))
        blocks = span - first_block + 1
        edges = jnp.maximum(jnp.minimum((last_start + (SPAN - 1)) // SPAN, span) - first_block, 0)
        starts[...] = doc_start(first_pos + lax.broadcasted_iota(jnp.int32, (SPAN, WIDTH), 0))

        for h in range(UNIT_HEADS):
            q_h = head_rows(0, h)
            q_s[rows_of(h)] = q_h
            q_t[:, rows_of(h)] = q_h.T

        def allowed_at(t):
            k_pos = t * SPAN + lax.broadcasted_iota(jnp.int32, (SPAN, SPAN), 1)
            q_pos = first_pos + lax.broadcasted_iota(jnp.int32, (SPAN, SPAN), 0)
            return (k_pos <= q_pos) & (k_pos >= both(starts[...]))

        def halves_max(s):
            return jnp.maximum(s[:, :WIDTH], s[:, WIDTH:])

        def row_max(x):
            return jnp.broadcast_to(jnp.max(x, axis=1, keepdims=True), x.shape)

        def score(slot, count):
            for n in range(count):
                wide_buf[n] = lax.dot_general(
                    q_s[...], kv_v[slots[slot + n], 0], NT, preferred_element_type=jnp.float32
                )

        def weigh(slot, count, allowed=None, take_top=False):
            for n in range(count):
                for h in range(UNIT_HEADS):
                    s = wide_buf[n, rows_of(h)]
                    if allowed is not None:
                        s = jnp.where(allowed, s, NEG)
                    if take_top:
                        level = row_max(halves_max(s))
                        level_b[rows_of(h)] = level
                    else:
                        level = level_b[rows_of(h)]
                    p = jnp.exp2((s - both(level)) * LOG2_SCALE)
                    probs[slot + n, rows_of(h)] = p.astype(jnp.bfloat16)

        def attend(slot, count):
            values = below([beside([kv_v[slots[slot + n], 1], ones]) for n in range(count)])
            o_acc[...] += jnp.dot(
                beside([probs[slot + n] for n in range(count)]), values, preferred_element_type=jnp.float32
            )

        def masked_step(i, _):
            score(i, 1)
            weigh(i, 1, allowed_at(first_block + i - 2))
            return 0

        def attend_step(i, _):
            attend(i, 1)
            return 0

        inner_from = edges + 2
        inner = blocks - 1 - edges
        slots[0] = first_unit
        slots[1] = holder[span]

        def place_slot(i, _):
            slots[i + 2] = holder[first_block + i]
            return 0

        lax.fori_loop(0, blocks - 1, place_slot, 0)
        probs[0] = jnp.zeros((COLS, SPAN), jnp.bfloat16)
        o_acc[...] = jnp.zeros_like(o_acc)
        score(1, 1)
        weigh(1, 1, allowed_at(span), take_top=True)
        lax.fori_loop(2, inner_from, masked_step, 0)
        lax.fori_loop(1, edges, attend_step, 0)

        def pair_step(j, _):
            slot = inner_from + 2 * j
            score(slot, 2)
            attend(slot - 2, 2)
            weigh(slot, 2)
            return 0

        lax.fori_loop(0, inner // 2, pair_step, 0)
        last = inner_from + inner - inner % 2

        @pl.when(inner % 2 == 1)
        def _():
            score(last, 1)
            attend(last - 2, 2)
            weigh(last, 1)
            attend(last, 1)

        @pl.when(inner % 2 == 0)
        def _():
            attend(last - 2, 2)

        worst = jnp.max(jnp.where(o_acc[:, WIDTH:] < LIMIT, 0.0, 1.0))

        @pl.when(worst > 0.0)
        def _():
            o_acc[...] = jnp.zeros_like(o_acc)
            level_b[...] = jnp.full_like(level_b, NEG)

            def top_step(i, _):
                k = kv_v[slots[i], 0]
                allowed = allowed_at(jnp.where(i == 1, span, first_block + i - 2))
                for h in range(UNIT_HEADS):
                    s = lax.dot_general(q_s[rows_of(h)], k, NT, preferred_element_type=jnp.float32)
                    s = jnp.where(allowed, s, NEG)
                    level_b[rows_of(h)] = jnp.maximum(level_b[rows_of(h)], halves_max(s))
                return 0

            lax.fori_loop(1, blocks + 1, top_step, 0)
            for h in range(UNIT_HEADS):
                level_b[rows_of(h)] = row_max(level_b[rows_of(h)])
            score(1, 1)
            weigh(1, 1, allowed_at(span))
            lax.fori_loop(2, blocks + 1, masked_step, 0)
            lax.fori_loop(1, blocks + 1, attend_step, 0)

        for h in range(UNIT_HEADS):
            inverse = 1.0 / o_acc[rows_of(h), WIDTH:]
            out = (o_acc[rows_of(h), :WIDTH] * inverse).astype(jnp.bfloat16)
            put_rows(0, h, out)
            scaled = (head_rows(1, h).astype(jnp.float32) * inverse).astype(jnp.bfloat16)
            do_s[rows_of(h)] = scaled
            do_t[:, rows_of(h)] = scaled.T
            delta = jnp.sum(scaled.astype(jnp.float32) * out.astype(jnp.float32), axis=1, keepdims=True)
            delta_b[rows_of(h)] = jnp.broadcast_to(delta, (SPAN, WIDTH))
        dq_acc[...] = jnp.zeros_like(dq_acc)

        def backward(i, count):
            places = [slots[i + n] for n in range(count)]
            for n, c in enumerate(places):
                wide_buf[n] = lax.dot_general(
                    do_s[...], kv_v[c, 1], NT, preferred_element_type=jnp.float32
                )
            for n in range(count):
                for h in range(UNIT_HEADS):
                    p = probs[i + n, rows_of(h)].astype(jnp.float32)
                    ds = p * (wide_buf[n, rows_of(h)] - both(delta_b[rows_of(h)]))
                    grads[n, rows_of(h)] = ds.astype(jnp.bfloat16)
            dv = jnp.dot(
                do_t[...], beside([probs[i + n] for n in range(count)]), preferred_element_type=jnp.float32
            )
            ds = beside([grads[n] for n in range(count)])
            dk = jnp.dot(q_t[...], ds, preferred_element_type=jnp.float32)
            dq_acc[...] += jnp.dot(
                ds, below([kv_v[c, 0] for c in places]), preferred_element_type=jnp.float32
            )
            for n, c in enumerate(places):
                part = slice(n * SPAN, (n + 1) * SPAN)
                acc[c, 0] += dk[:, part]
                acc[c, 1] += dv[:, part]

        def grad_step(j, _):
            backward(2 * j + 1, 2)
            return 0

        lax.fori_loop(0, blocks // 2, grad_step, 0)

        @pl.when(blocks % 2 == 1)
        def _():
            backward(blocks, 1)

        for h in range(UNIT_HEADS):
            put_rows(1, h, dq_acc[rows_of(h)] * SCALE)
        return 0

    lax.fori_loop(0, UNITS, unit, 0)

    def pack(c, _):
        dkv_v[c, 0] = (acc[c, 0] * SCALE).astype(jnp.bfloat16)
        dkv_v[c, 1] = acc[c, 1].astype(jnp.bfloat16)
        return 0

    lax.fori_loop(0, N_CTX, pack, 0)


def attention(rows, kv, span_of, doc_lengths):
    blocks = jax.ShapeDtypeStruct((N_CTX, 2, WIDTH, SPAN), jnp.bfloat16)
    table = pl.BlockSpec(memory_space=pltpu.HBM)
    here = pl.BlockSpec(memory_space=pltpu.VMEM)
    vmem = pltpu.VMEM
    return pl.pallas_call(
        attention_kernel,
        out_shape=(jax.ShapeDtypeStruct(rows.shape, rows.dtype), blocks),
        in_specs=[table, table, here, here],
        out_specs=(here, here),
        scratch_shapes=[
            pltpu.SMEM((N_CTX,), jnp.int32),
            pltpu.SMEM((MAX_BLOCKS,), jnp.int32),
            vmem(blocks.shape, jnp.float32),
            vmem((MAX_BLOCKS, COLS, SPAN), jnp.bfloat16),
            vmem((2, COLS, SPAN), jnp.bfloat16),
            vmem((2, COLS, SPAN), jnp.float32),
            vmem((WIDTH, COLS), jnp.bfloat16),
            vmem((WIDTH, COLS), jnp.bfloat16),
            vmem((COLS, WIDTH), jnp.bfloat16),
            vmem((COLS, WIDTH), jnp.bfloat16),
            vmem((COLS, 2 * WIDTH), jnp.float32),
            vmem((COLS, WIDTH), jnp.float32),
            vmem((COLS, WIDTH), jnp.float32),
            vmem((COLS, WIDTH), jnp.float32),
            vmem((SPAN, WIDTH), jnp.int32),
            pltpu.SMEM((N_CTX,), jnp.int32),
            pltpu.SMEM((4,), jnp.int32),
            pltpu.SemaphoreType.DMA((2,)),
        ],
        compiler_params=pltpu.CompilerParams(vmem_limit_bytes=40 * 1024 * 1024),
        name="attention",
    )(span_of, doc_lengths, rows, kv)


MESH_IDS = pl.DeviceIdType.MESH


def place(z_size):
    ctx, head = lax.axis_index("ctx"), lax.axis_index("head")
    return ctx, head, ctx // (2 * z_size), (ctx // 2) % z_size, ctx % 2


def meet(group, ctx, head, core, heads, others):
    barrier = pltpu.get_barrier_semaphore()
    base = ctx - core

    def greet(step, _):
        peer = (core * heads + head + step) % group
        pl.semaphore_signal(
            barrier, inc=1, device_id=(base + peer // heads, peer % heads), device_id_type=MESH_IDS
        )
        return 0

    lax.fori_loop(1, group, greet, 0)
    for other in others:
        pl.semaphore_signal(barrier, inc=1, device_id=(other, head), device_id_type=MESH_IDS)
    pl.semaphore_wait(barrier, group - 1 + len(others))


def arrived(ref, sem):
    pltpu.make_async_copy(ref, ref, sem).wait()


def send(src, dst, send_sem, recv_sem, ctx, head):
    pltpu.make_async_remote_copy(
        src_ref=src, dst_ref=dst, send_sem=send_sem, recv_sem=recv_sem,
        device_id=(ctx, head), device_id_type=MESH_IDS,
    ).start()


def gather_kernel(
    z_size, heads,
    q_hbm, do_hbm, k_hbm, v_hbm, rows_out, kv_out, rows_in, pieces_in,
    row_send, row_recv, piece_send, piece_recv, ring_send, right_recv, left_recv,
    cross_recv, twin_send, twin_recv, local_sem, load_sem,
):
    loads = []
    for n, (src, dst) in enumerate((
        (k_hbm, pieces_in.at[0]), (v_hbm, pieces_in.at[1]), (q_hbm, rows_in.at[0]), (do_hbm, rows_in.at[1])
    )):
        loads.append(pltpu.make_async_copy(src, dst, load_sem.at[n]))
        loads[-1].start()
    ctx, head, x, z, core = place(z_size)
    group = 2 * heads
    base = ctx - core
    mine = core * heads + head
    wide = rows_in.shape[2] // group

    def index(x_at, z_at):
        return (x_at * z_size + z_at) * 2 + core

    def block(x_at, z_at):
        return kv_out.at[x_at, z_at * 2 + core]

    right_z, left_z = (z + 1) % z_size, (z + z_size - 1) % z_size
    right, left = index(x, right_z), index(x, left_z)
    cross, twin = index(1 - x, z), base + 1 - core
    meet(group, ctx, head, core, heads, (right, left, cross))

    def piece_cols(at):
        return pl.ds(pl.multiple_of(at * WIDTH, WIDTH), WIDTH)

    def row_cols(at):
        peer_core, peer_head = at // heads, at % heads
        return pl.ds(pl.multiple_of((peer_head * 2 + peer_core) * wide, WIDTH), wide)

    mine_block = block(x, z)

    def send_pieces(step, _):
        peer = (head + step) % heads
        send(pieces_in.at[:, :, piece_cols(peer)], mine_block.at[:, head], piece_send, piece_recv, ctx, peer)
        return 0

    loads[0].wait()
    loads[1].wait()
    lax.fori_loop(1, heads, send_pieces, 0)
    own_piece = pltpu.make_async_copy(
        pieces_in.at[:, :, piece_cols(head)], mine_block.at[:, head], local_sem.at[0]
    )
    own_piece.start()
    loads[2].wait()
    loads[3].wait()
    own_rows = pltpu.make_async_copy(rows_in.at[:, :, row_cols(mine)], rows_out.at[mine], local_sem.at[1])
    own_rows.start()

    def send_row(step, _):
        peer = (mine + step) % group
        send(
            rows_in.at[:, :, row_cols(peer)], rows_out.at[mine], row_send, row_recv,
            base + peer // heads, peer % heads,
        )
        return 0

    rows_sent = [1]

    def send_rows(count):
        stop = min(rows_sent[0] + count, group)
        lax.fori_loop(rows_sent[0], stop, send_row, 0)
        rows_sent[0] = stop

    send_rows(2)
    own_piece.wait()
    pieces = mine_block.at[:, pl.ds(0, heads - 1)]
    arrived(pieces, piece_recv)

    sent = []

    def forward(what, to, recv):
        sem = ring_send.at[len(sent)]
        send(what, what, sem, recv, to, head)
        sent.append((what, sem))

    def share(z_at):
        both_x = kv_out.at[:, z_at * 2 + core]
        send(both_x, both_x, twin_send, twin_recv, twin, head)

    far = z_size // 2
    reach = ((far, far - 1), (far - 1, far))
    forward(mine_block, cross, cross_recv)
    forward(mine_block, right, right_recv.at[0, 0])
    forward(mine_block, left, left_recv.at[0, 0])
    send_rows(2)
    cross_block = block(1 - x, z)
    arrived(cross_block, cross_recv)
    forward(cross_block, right, right_recv.at[1, 0])
    forward(cross_block, left, left_recv.at[1, 0])
    share(z)
    for d in range(1, far + 1):
        for plane in range(2):
            at_x = x if plane == 0 else 1 - x
            for way in range(2):
                if d > reach[plane][way]:
                    continue
                recv, to = ((right_recv, right), (left_recv, left))[way]
                origin = (z + z_size - d) % z_size if way == 0 else (z + d) % z_size
                what = block(at_x, origin)
                arrived(what, recv.at[plane, d - 1])
                if d < reach[plane][way]:
                    forward(what, to, recv.at[plane, d])
                if plane == 1:
                    share(origin)
                send_rows(1)

    send_rows(group)
    arrived(pieces, piece_send)
    for what, sem in sent:
        arrived(what, sem)
    arrived(kv_out.at[0], twin_send)
    arrived(kv_out.at[0], twin_recv)
    own_rows.wait()
    rows = rows_out.at[pl.ds(0, group - 1)]
    arrived(rows, row_send)
    arrived(rows, row_recv)


def gather(q, do, k, v, z_size, heads):
    tokens = q.shape[0]
    group = 2 * heads
    far = z_size // 2
    rows = jax.ShapeDtypeStruct((group, 2, tokens, q.shape[1] // group), q.dtype)
    kv = jax.ShapeDtypeStruct((2, 2 * z_size, 2, heads, tokens, WIDTH), q.dtype)
    hbm = pl.BlockSpec(memory_space=pltpu.HBM)
    here = pl.BlockSpec(memory_space=pltpu.VMEM)
    dma = pltpu.SemaphoreType.DMA
    return pl.pallas_call(
        functools.partial(gather_kernel, z_size, heads),
        out_shape=(rows, kv),
        in_specs=[hbm] * 4,
        out_specs=(here, here),
        scratch_shapes=[
            pltpu.VMEM((2,) + q.shape, q.dtype), pltpu.VMEM((2,) + k.shape, k.dtype),
            dma, dma, dma, dma, dma((4 * far - 2 + 1,)), dma((2, far)), dma((2, far)),
            dma, dma, dma, dma((2,)), dma((4,)),
        ],
        compiler_params=pltpu.CompilerParams(
            collective_id=0, has_side_effects=True, vmem_limit_bytes=32 * 1024 * 1024
        ),
        name="gather",
    )(q, do, k, v)


def scatter_kernel(
    z_size, heads,
    rows_in, dkv_in, rows_out, pieces_out,
    part, twin_part, right_part, left_part, cross_part, final,
    row_send, row_recv, piece_send, piece_recv, ring_send, right_recv, left_recv,
    cross_recv, twin_send, twin_recv, local_sem,
):
    ctx, head, x, z, core = place(z_size)
    group = 2 * heads
    base = ctx - core
    mine = core * heads + head
    wide = rows_in.shape[3]

    def index(x_at, z_at):
        return (x_at * z_size + z_at) * 2 + core

    right, left = index(x, (z + 1) % z_size), index(x, (z + z_size - 1) % z_size)
    over_right, over_left = index(1 - x, (z + 1) % z_size), index(1 - x, (z + z_size - 1) % z_size)
    cross, twin = index(1 - x, z), base + 1 - core
    meet(group, ctx, head, core, heads, (right, left, cross, over_right, over_left))

    far = z_size // 2
    reach = ((far, far - 1), (far - 1, far))
    steps = []
    for back in range(far):
        for plane, way in ((0, 0), (1, 1), (1, 0), (0, 1)):
            d = reach[plane][way] - back
            if d > 0:
                steps.append((plane, way, d, back))

    to_twin = [far] + [s * d for d in range(far - 1, 0, -1) for s in (1, -1)]
    to_twin.insert(3, 0)
    place_of = {offset: n for n, offset in enumerate(to_twin)}
    fed, had = [0], [0]

    def z_of(offset):
        return (z + z_size + offset) % z_size

    def feed_twin(count):
        for n in range(fed[0], min(fed[0] + count, len(to_twin))):
            at = z_of(to_twin[n])
            send(dkv_in.at[:, at, 1 - core], twin_part.at[:, at], twin_send, twin_recv.at[n], twin, head)
        fed[0] = min(fed[0] + count, len(to_twin))

    def need_twin(offset):
        n = place_of[far if abs(offset) == far else offset]
        while had[0] <= n:
            arrived(twin_part.at[:, z_of(to_twin[had[0]])], twin_recv.at[had[0]])
            had[0] += 1

    feed_twin(3)
    my_rows = pl.ds(pl.multiple_of((head * 2 + core) * wide, WIDTH), wide)

    def send_row(step, _):
        peer = (mine + step) % group
        send(
            rows_in.at[peer], rows_out.at[:, :, my_rows], row_send, row_recv,
            base + peer // heads, peer % heads,
        )
        return 0

    rows_sent = [1]

    def send_rows(count):
        stop = min(rows_sent[0] + count, group)
        lax.fori_loop(rows_sent[0], stop, send_row, 0)
        rows_sent[0] = stop

    own_rows = pltpu.make_async_copy(rows_in.at[mine], rows_out.at[:, :, my_rows], local_sem.at[0])
    own_rows.start()

    def combine(at_x, at_z, extras, last=False):
        def add_half(side, _):
            total = dkv_in[at_x, at_z, core, side].astype(jnp.float32)
            total = total + twin_part[at_x, at_z, side].astype(jnp.float32)
            for ref, at in extras:
                total = total + ref[at + (side,)].astype(jnp.float32)
            if last:
                final[side] = total.T.astype(final.dtype).reshape(final.shape[1:])
            else:
                part[at_x, at_z, side] = total.astype(part.dtype)
            return 0

        lax.fori_loop(0, 2, add_half, 0)

    sent = []
    for n, (plane, way, d, back) in enumerate(steps):
        offset = d if way == 0 else -d
        at_x, at_z = (x if plane == 0 else 1 - x), z_of(offset)
        recv, buf, to, over = (
            (right_recv, right_part, right, over_right), (left_recv, left_part, left, over_left)
        )[way]
        if plane == 1 and d == 1:
            to = over
        need_twin(offset)
        extras = []
        if back > 0:
            arrived(buf.at[plane, back - 1], recv.at[plane, back - 1])
            extras = [(buf, (plane, back - 1))]
        combine(at_x, at_z, extras)
        send(part.at[at_x, at_z], buf.at[plane, back], ring_send.at[n], recv.at[plane, back], to, head)
        sent.append((part.at[at_x, at_z], ring_send.at[n]))
        if n % 2 == 0:
            feed_twin(1)
        send_rows(1)
        if n == min(5, len(steps) - 1):
            need_twin(0)
            combine(1 - x, z, [])
            sem = ring_send.at[len(steps)]
            send(part.at[1 - x, z], cross_part.at[0], sem, cross_recv, cross, head)
            sent.append((part.at[1 - x, z], sem))
    feed_twin(len(to_twin))
    send_rows(group)
    extras = [(cross_part, (0,))]
    arrived(cross_part.at[0], cross_recv)
    for plane in range(2):
        for way, (buf, recv) in enumerate(((right_part, right_recv), (left_part, left_recv))):
            at = reach[plane][way] - 1
            arrived(buf.at[plane, at], recv.at[plane, at])
            extras.append((buf, (plane, at)))
    combine(x, z, extras, last=True)

    my_cols = pl.ds(pl.multiple_of(head * WIDTH, WIDTH), WIDTH)

    def send_pieces(step, _):
        peer = (head + step) % heads
        send(final.at[:, peer], pieces_out.at[:, :, my_cols], piece_send, piece_recv, ctx, peer)
        return 0

    lax.fori_loop(1, heads, send_pieces, 0)
    own_piece = pltpu.make_async_copy(final.at[:, head], pieces_out.at[:, :, my_cols], local_sem.at[1])
    own_piece.start()
    own_piece.wait()
    own_rows.wait()
    for what, sem in sent:
        arrived(what, sem)
    arrived(part, twin_send)
    rows = rows_out.at[:, :, pl.ds(0, (group - 1) * wide)]
    arrived(rows, row_send)
    arrived(rows, row_recv)
    arrived(final.at[:, pl.ds(0, heads - 1)], piece_send)
    arrived(pieces_out.at[:, :, pl.ds(0, (heads - 1) * WIDTH)], piece_recv)


def scatter(rows, dkv, z_size, heads):
    group, _, tokens, wide = rows.shape
    far = z_size // 2
    block = dkv.shape[3:]
    here = pl.BlockSpec(memory_space=pltpu.VMEM)
    dma = pltpu.SemaphoreType.DMA
    return pl.pallas_call(
        functools.partial(scatter_kernel, z_size, heads),
        out_shape=(
            jax.ShapeDtypeStruct((2, tokens, group * wide), rows.dtype),
            jax.ShapeDtypeStruct((2, tokens, heads * WIDTH), rows.dtype),
        ),
        in_specs=[here] * 2,
        out_specs=(here, here),
        scratch_shapes=[
            pltpu.VMEM((2, z_size) + block, dkv.dtype),
            pltpu.VMEM((2, z_size) + block, dkv.dtype),
            pltpu.VMEM((2, far) + block, dkv.dtype),
            pltpu.VMEM((2, far) + block, dkv.dtype),
            pltpu.VMEM((1,) + block, dkv.dtype),
            pltpu.VMEM((2, heads, tokens, WIDTH), dkv.dtype),
            dma, dma, dma, dma, dma((4 * far - 2 + 1,)), dma((2, far)), dma((2, far)),
            dma, dma, dma((z_size,)), dma((2,)),
        ],
        compiler_params=pltpu.CompilerParams(
            collective_id=1, has_side_effects=True, vmem_limit_bytes=24 * 1024 * 1024
        ),
        name="scatter",
    )(rows, dkv)


def settle_kernel(rows, pieces, o, dq, dk, dv, sem):
    copies = []
    for src, outs in ((rows, (o, dq)), (pieces, (dk, dv))):
        for n, out in enumerate(outs):
            copies.append(pltpu.make_async_copy(src.at[n], out, sem.at[len(copies)]))
            copies[-1].start()
    for copy in copies:
        copy.wait()


def settle(arrays):
    hbm = pl.BlockSpec(memory_space=pl.ANY)
    here = pl.BlockSpec(memory_space=pltpu.VMEM)
    return pl.pallas_call(
        settle_kernel,
        out_shape=tuple(jax.ShapeDtypeStruct(a.shape[1:], a.dtype) for a in arrays for _ in range(2)),
        in_specs=[here] * len(arrays),
        out_specs=(hbm,) * 4,
        scratch_shapes=[pltpu.SemaphoreType.DMA((4,))],
        compiler_params=pltpu.CompilerParams(vmem_limit_bytes=32 * 1024 * 1024),
        name="settle",
    )(*arrays)


def per_device(heads, z_size, queries, keys, values, output_gradient, doc_lengths, span_of):
    queries, output_gradient, keys, values, doc_lengths, span_of = (
        pltpu.with_memory_space_constraint(a, pltpu.HBM)
        for a in (queries, output_gradient, keys, values, doc_lengths, span_of)
    )
    rows, kv = gather(queries, output_gradient, keys, values, z_size, heads)
    outs, dkv = attention(rows, kv.reshape(N_CTX, 2, SPAN, WIDTH), span_of, doc_lengths)
    return settle(scatter(outs, dkv.reshape((2, z_size, 2) + dkv.shape[1:]), z_size, heads))


def solution(mesh):
    shard = P(("ctx", "head"), None)
    return jax.shard_map(
        functools.partial(per_device, mesh.shape["head"], N_CTX // 4),
        mesh=mesh,
        in_specs=(shard, shard, shard, shard, P(), P()),
        out_specs=(shard, shard, shard, shard),
        check_vma=False,
    )
```

```python
import functools
import math

import jax
import jax.numpy as jnp
from jax import lax
from jax.experimental import pallas as pl
from jax.experimental.pallas import tpu as pltpu
from jax.sharding import PartitionSpec as P

N_CTX = 32
SPAN = 256
WIDTH = 128
UNIT_HEADS = 4
UNITS = 2
MAX_BLOCKS = 18
COLS = UNIT_HEADS * SPAN
LIMIT = 2.0**60
SCALE = WIDTH**-0.5
LOG2_SCALE = SCALE * math.log2(math.e)
NEG = -1e30


NT = (((1,), (1,)), ((), ()))


def attention_kernel(
    span_hbm, len_hbm, rows_v, kv_v,
    out_v, dkv_v,
    holder, slots, acc, probs, grads, wide_buf,
    q_t, do_t, q_s, do_s, o_acc, dq_acc, level_b, delta_b, starts,
    span_ref, len_ref, table_sem,
):
    load_span = pltpu.make_async_copy(span_hbm, span_ref, table_sem.at[0])
    load_len = pltpu.make_async_copy(len_hbm, len_ref, table_sem.at[1])
    load_span.start()
    load_len.start()
    ctx = lax.axis_index("ctx")
    first_unit = ctx - ctx % UNITS

    def clear(c, _):
        acc[c] = jnp.zeros((2, WIDTH, SPAN), jnp.float32)
        return 0

    lax.fori_loop(0, N_CTX, clear, 0)

    load_span.wait()
    load_len.wait()

    def note(c, _):
        holder[span_ref[c]] = c
        return 0

    lax.fori_loop(0, N_CTX, note, 0)

    ends = []
    running = jnp.int32(0)
    for j in range(4):
        running = running + len_ref[j]
        ends.append(running)

    def doc_start(pos):
        start = jnp.zeros_like(pos)
        for end in ends:
            start = jnp.where(pos >= end, end, start)
        return start

    def rows_of(h):
        return pl.ds(h * SPAN, SPAN)

    def lanes_of(h):
        return pl.ds(h * WIDTH, WIDTH)

    def both(x):
        return jnp.concatenate([x, x], axis=1)

    def beside(parts):
        return parts[0] if len(parts) == 1 else jnp.concatenate(parts, axis=1)

    def below(parts):
        return parts[0] if len(parts) == 1 else jnp.concatenate(parts, axis=0)

    ones = jnp.ones((SPAN, WIDTH), jnp.bfloat16)

    def unit(u, _):
        group = rows_v.shape[0] // UNITS
        own = pl.ds(pl.multiple_of(u * group, group), group)

        def head_rows(side, h):
            return rows_v[own, side, :, lanes_of(h)].reshape(SPAN, WIDTH)

        def put_rows(side, h, value):
            out_v[own, side, :, lanes_of(h)] = value.astype(jnp.bfloat16).reshape(group, SPAN // group, WIDTH)

        span = span_ref[first_unit + u]
        first_pos = span * SPAN
        first_block = doc_start(first_pos) // SPAN
        last_start = doc_start(first_pos + (SPAN - 1))
        blocks = span - first_block + 1
        edges = jnp.maximum(jnp.minimum((last_start + (SPAN - 1)) // SPAN, span) - first_block, 0)
        starts[...] = doc_start(first_pos + lax.broadcasted_iota(jnp.int32, (SPAN, WIDTH), 0))

        for h in range(UNIT_HEADS):
            q_h = head_rows(0, h)
            q_s[rows_of(h)] = q_h
            q_t[:, rows_of(h)] = q_h.T

        def allowed_at(t):
            k_pos = t * SPAN + lax.broadcasted_iota(jnp.int32, (SPAN, SPAN), 1)
            q_pos = first_pos + lax.broadcasted_iota(jnp.int32, (SPAN, SPAN), 0)
            return (k_pos <= q_pos) & (k_pos >= both(starts[...]))

        def halves_max(s):
            return jnp.maximum(s[:, :WIDTH], s[:, WIDTH:])

        def row_max(x):
            return jnp.broadcast_to(jnp.max(x, axis=1, keepdims=True), x.shape)

        def score(slot, count):
            for n in range(count):
                wide_buf[n] = lax.dot_general(
                    q_s[...], kv_v[slots[slot + n], 0], NT, preferred_element_type=jnp.float32
                )

        def weigh(slot, count, allowed=None, take_top=False):
            for n in range(count):
                for h in range(UNIT_HEADS):
                    s = wide_buf[n, rows_of(h)]
                    if allowed is not None:
                        s = jnp.where(allowed, s, NEG)
                    if take_top:
                        level = row_max(halves_max(s))
                        level_b[rows_of(h)] = level
                    else:
                        level = level_b[rows_of(h)]
                    p = jnp.exp2((s - both(level)) * LOG2_SCALE)
                    probs[slot + n, rows_of(h)] = p.astype(jnp.bfloat16)

        def attend(slot, count):
            values = below([beside([kv_v[slots[slot + n], 1], ones]) for n in range(count)])
            o_acc[...] += jnp.dot(
                beside([probs[slot + n] for n in range(count)]), values, preferred_element_type=jnp.float32
            )

        def masked_step(i, _):
            score(i, 1)
            weigh(i, 1, allowed_at(first_block + i - 2))
            return 0

        def attend_step(i, _):
            attend(i, 1)
            return 0

        inner_from = edges + 2
        inner = blocks - 1 - edges
        slots[0] = first_unit
        slots[1] = holder[span]

        def place_slot(i, _):
            slots[i + 2] = holder[first_block + i]
            return 0

        lax.fori_loop(0, blocks - 1, place_slot, 0)
        probs[0] = jnp.zeros((COLS, SPAN), jnp.bfloat16)
        o_acc[...] = jnp.zeros_like(o_acc)
        score(1, 1)
        weigh(1, 1, allowed_at(span), take_top=True)
        lax.fori_loop(2, inner_from, masked_step, 0)
        lax.fori_loop(1, edges, attend_step, 0)

        def pair_step(j, _):
            slot = inner_from + 2 * j
            score(slot, 2)
            attend(slot - 2, 2)
            weigh(slot, 2)
            return 0

        lax.fori_loop(0, inner // 2, pair_step, 0)
        last = inner_from + inner - inner % 2

        @pl.when(inner % 2 == 1)
        def _():
            score(last, 1)
            attend(last - 2, 2)
            weigh(last, 1)
            attend(last, 1)

        @pl.when(inner % 2 == 0)
        def _():
            attend(last - 2, 2)

        worst = jnp.max(jnp.where(o_acc[:, WIDTH:] < LIMIT, 0.0, 1.0))

        @pl.when(worst > 0.0)
        def _():
            o_acc[...] = jnp.zeros_like(o_acc)
            level_b[...] = jnp.full_like(level_b, NEG)

            def top_step(i, _):
                k = kv_v[slots[i], 0]
                allowed = allowed_at(jnp.where(i == 1, span, first_block + i - 2))
                for h in range(UNIT_HEADS):
                    s = lax.dot_general(q_s[rows_of(h)], k, NT, preferred_element_type=jnp.float32)
                    s = jnp.where(allowed, s, NEG)
                    level_b[rows_of(h)] = jnp.maximum(level_b[rows_of(h)], halves_max(s))
                return 0

            lax.fori_loop(1, blocks + 1, top_step, 0)
            for h in range(UNIT_HEADS):
                level_b[rows_of(h)] = row_max(level_b[rows_of(h)])
            score(1, 1)
            weigh(1, 1, allowed_at(span))
            lax.fori_loop(2, blocks + 1, masked_step, 0)
            lax.fori_loop(1, blocks + 1, attend_step, 0)

        for h in range(UNIT_HEADS):
            inverse = 1.0 / o_acc[rows_of(h), WIDTH:]
            out = (o_acc[rows_of(h), :WIDTH] * inverse).astype(jnp.bfloat16)
            put_rows(0, h, out)
            scaled = (head_rows(1, h).astype(jnp.float32) * inverse).astype(jnp.bfloat16)
            do_s[rows_of(h)] = scaled
            do_t[:, rows_of(h)] = scaled.T
            delta = jnp.sum(scaled.astype(jnp.float32) * out.astype(jnp.float32), axis=1, keepdims=True)
            delta_b[rows_of(h)] = jnp.broadcast_to(delta, (SPAN, WIDTH))
        dq_acc[...] = jnp.zeros_like(dq_acc)

        def backward(i, count):
            places = [slots[i + n] for n in range(count)]
            for n, c in enumerate(places):
                wide_buf[n] = lax.dot_general(
                    do_s[...], kv_v[c, 1], NT, preferred_element_type=jnp.float32
                )
            for n in range(count):
                for h in range(UNIT_HEADS):
                    p = probs[i + n, rows_of(h)].astype(jnp.float32)
                    ds = p * (wide_buf[n, rows_of(h)] - both(delta_b[rows_of(h)]))
                    grads[n, rows_of(h)] = ds.astype(jnp.bfloat16)
            dv = jnp.dot(
                do_t[...], beside([probs[i + n] for n in range(count)]), preferred_element_type=jnp.float32
            )
            ds = beside([grads[n] for n in range(count)])
            dk = jnp.dot(q_t[...], ds, preferred_element_type=jnp.float32)
            dq_acc[...] += jnp.dot(
                ds, below([kv_v[c, 0] for c in places]), preferred_element_type=jnp.float32
            )
            for n, c in enumerate(places):
                part = slice(n * SPAN, (n + 1) * SPAN)
                acc[c, 0] += dk[:, part]
                acc[c, 1] += dv[:, part]

        def grad_step(j, _):
            backward(2 * j + 1, 2)
            return 0

        lax.fori_loop(0, blocks // 2, grad_step, 0)

        @pl.when(blocks % 2 == 1)
        def _():
            backward(blocks, 1)

        for h in range(UNIT_HEADS):
            put_rows(1, h, dq_acc[rows_of(h)] * SCALE)
        return 0

    lax.fori_loop(0, UNITS, unit, 0)

    def pack(c, _):
        dkv_v[c, 0] = (acc[c, 0] * SCALE).astype(jnp.bfloat16)
        dkv_v[c, 1] = acc[c, 1].astype(jnp.bfloat16)
        return 0

    lax.fori_loop(0, N_CTX, pack, 0)


def attention(rows, kv, span_of, doc_lengths):
    blocks = jax.ShapeDtypeStruct((N_CTX, 2, WIDTH, SPAN), jnp.bfloat16)
    table = pl.BlockSpec(memory_space=pltpu.HBM)
    here = pl.BlockSpec(memory_space=pltpu.VMEM)
    vmem = pltpu.VMEM
    return pl.pallas_call(
        attention_kernel,
        out_shape=(jax.ShapeDtypeStruct(rows.shape, rows.dtype), blocks),
        in_specs=[table, table, here, here],
        out_specs=(here, here),
        scratch_shapes=[
            pltpu.SMEM((N_CTX,), jnp.int32),
            pltpu.SMEM((MAX_BLOCKS,), jnp.int32),
            vmem(blocks.shape, jnp.float32),
            vmem((MAX_BLOCKS, COLS, SPAN), jnp.bfloat16),
            vmem((2, COLS, SPAN), jnp.bfloat16),
            vmem((2, COLS, SPAN), jnp.float32),
            vmem((WIDTH, COLS), jnp.bfloat16),
            vmem((WIDTH, COLS), jnp.bfloat16),
            vmem((COLS, WIDTH), jnp.bfloat16),
            vmem((COLS, WIDTH), jnp.bfloat16),
            vmem((COLS, 2 * WIDTH), jnp.float32),
            vmem((COLS, WIDTH), jnp.float32),
            vmem((COLS, WIDTH), jnp.float32),
            vmem((COLS, WIDTH), jnp.float32),
            vmem((SPAN, WIDTH), jnp.int32),
            pltpu.SMEM((N_CTX,), jnp.int32),
            pltpu.SMEM((4,), jnp.int32),
            pltpu.SemaphoreType.DMA((2,)),
        ],
        compiler_params=pltpu.CompilerParams(vmem_limit_bytes=40 * 1024 * 1024),
        name="attention",
    )(span_of, doc_lengths, rows, kv)


MESH_IDS = pl.DeviceIdType.MESH


def place(z_size):
    ctx, head = lax.axis_index("ctx"), lax.axis_index("head")
    return ctx, head, ctx // (2 * z_size), (ctx // 2) % z_size, ctx % 2


def meet(group, ctx, head, core, heads, others):
    barrier = pltpu.get_barrier_semaphore()
    base = ctx - core

    def greet(step, _):
        peer = (core * heads + head + step) % group
        pl.semaphore_signal(
            barrier, inc=1, device_id=(base + peer // heads, peer % heads), device_id_type=MESH_IDS
        )
        return 0

    lax.fori_loop(1, group, greet, 0)
    for other in others:
        pl.semaphore_signal(barrier, inc=1, device_id=(other, head), device_id_type=MESH_IDS)
    pl.semaphore_wait(barrier, group - 1 + len(others))


def arrived(ref, sem):
    pltpu.make_async_copy(ref, ref, sem).wait()


def send(src, dst, send_sem, recv_sem, ctx, head):
    pltpu.make_async_remote_copy(
        src_ref=src, dst_ref=dst, send_sem=send_sem, recv_sem=recv_sem,
        device_id=(ctx, head), device_id_type=MESH_IDS,
    ).start()


def gather_kernel(
    z_size, heads,
    q_hbm, do_hbm, k_hbm, v_hbm, rows_out, kv_out, rows_in, pieces_in,
    row_send, row_recv, piece_send, piece_recv, ring_send, right_recv, left_recv,
    cross_recv, twin_send, twin_recv, local_sem, load_sem,
):
    loads = []
    for n, (src, dst) in enumerate((
        (k_hbm, pieces_in.at[0]), (v_hbm, pieces_in.at[1]), (q_hbm, rows_in.at[0]), (do_hbm, rows_in.at[1])
    )):
        loads.append(pltpu.make_async_copy(src, dst, load_sem.at[n]))
        loads[-1].start()
    ctx, head, x, z, core = place(z_size)
    group = 2 * heads
    base = ctx - core
    mine = core * heads + head
    wide = rows_in.shape[2] // group

    def index(x_at, z_at):
        return (x_at * z_size + z_at) * 2 + core

    def block(x_at, z_at):
        return kv_out.at[x_at, z_at * 2 + core]

    right_z, left_z = (z + 1) % z_size, (z + z_size - 1) % z_size
    right, left = index(x, right_z), index(x, left_z)
    over_right, over_left = index(1 - x, right_z), index(1 - x, left_z)
    cross, twin = index(1 - x, z), base + 1 - core
    meet(group, ctx, head, core, heads, (right, left, cross, over_right, over_left))

    def piece_cols(at):
        return pl.ds(pl.multiple_of(at * WIDTH, WIDTH), WIDTH)

    def row_cols(at):
        peer_core, peer_head = at // heads, at % heads
        return pl.ds(pl.multiple_of((peer_head * 2 + peer_core) * wide, WIDTH), wide)

    mine_block = block(x, z)

    def send_pieces(step, _):
        peer = (head + step) % heads
        send(pieces_in.at[:, :, piece_cols(peer)], mine_block.at[:, head], piece_send, piece_recv, ctx, peer)
        return 0

    loads[0].wait()
    loads[1].wait()
    lax.fori_loop(1, heads, send_pieces, 0)
    own_piece = pltpu.make_async_copy(
        pieces_in.at[:, :, piece_cols(head)], mine_block.at[:, head], local_sem.at[0]
    )
    own_piece.start()
    loads[2].wait()
    loads[3].wait()
    own_rows = pltpu.make_async_copy(rows_in.at[:, :, row_cols(mine)], rows_out.at[mine], local_sem.at[1])
    own_rows.start()

    def send_row(step, _):
        peer = (mine + step) % group
        send(
            rows_in.at[:, :, row_cols(peer)], rows_out.at[mine], row_send, row_recv,
            base + peer // heads, peer % heads,
        )
        return 0

    rows_sent = [1]

    def send_rows(count):
        stop = min(rows_sent[0] + count, group)
        lax.fori_loop(rows_sent[0], stop, send_row, 0)
        rows_sent[0] = stop

    send_rows(2)
    own_piece.wait()
    pieces = mine_block.at[:, pl.ds(0, heads - 1)]
    arrived(pieces, piece_recv)

    sent = []

    def forward(what, to, recv):
        sem = ring_send.at[len(sent)]
        send(what, what, sem, recv, to, head)
        sent.append((what, sem))

    def share(z_at):
        both_x = kv_out.at[:, z_at * 2 + core]
        send(both_x, both_x, twin_send, twin_recv, twin, head)

    far = z_size // 2
    reach = ((far, far - 1), (far - 1, far))
    forward(mine_block, right, right_recv.at[0, 0])
    forward(mine_block, left, left_recv.at[0, 0])
    forward(mine_block, over_right, right_recv.at[1, 0])
    forward(mine_block, over_left, left_recv.at[1, 0])
    forward(mine_block, cross, cross_recv)
    send_rows(2)
    arrived(block(1 - x, z), cross_recv)
    share(z)
    for d in range(1, far + 1):
        for plane in range(2):
            at_x = x if plane == 0 else 1 - x
            for way in range(2):
                if d > reach[plane][way]:
                    continue
                recv, to = ((right_recv, right), (left_recv, left))[way]
                origin = (z + z_size - d) % z_size if way == 0 else (z + d) % z_size
                what = block(at_x, origin)
                arrived(what, recv.at[plane, d - 1])
                if d < reach[plane][way]:
                    forward(what, to, recv.at[plane, d])
                if d == far:
                    send(what, what, twin_send, twin_recv, twin, head)
                elif plane == 1:
                    share(origin)
                send_rows(1)

    send_rows(group)
    arrived(pieces, piece_send)
    for what, sem in sent:
        arrived(what, sem)
    arrived(kv_out.at[0], twin_send)
    arrived(kv_out.at[0], twin_recv)
    own_rows.wait()
    rows = rows_out.at[pl.ds(0, group - 1)]
    arrived(rows, row_send)
    arrived(rows, row_recv)


def gather(q, do, k, v, z_size, heads):
    tokens = q.shape[0]
    group = 2 * heads
    far = z_size // 2
    rows = jax.ShapeDtypeStruct((group, 2, tokens, q.shape[1] // group), q.dtype)
    kv = jax.ShapeDtypeStruct((2, 2 * z_size, 2, heads, tokens, WIDTH), q.dtype)
    hbm = pl.BlockSpec(memory_space=pltpu.HBM)
    here = pl.BlockSpec(memory_space=pltpu.VMEM)
    dma = pltpu.SemaphoreType.DMA
    return pl.pallas_call(
        functools.partial(gather_kernel, z_size, heads),
        out_shape=(rows, kv),
        in_specs=[hbm] * 4,
        out_specs=(here, here),
        scratch_shapes=[
            pltpu.VMEM((2,) + q.shape, q.dtype), pltpu.VMEM((2,) + k.shape, k.dtype),
            dma, dma, dma, dma, dma((4 * far - 2 + 1,)), dma((2, far)), dma((2, far)),
            dma, dma, dma, dma((2,)), dma((4,)),
        ],
        compiler_params=pltpu.CompilerParams(
            collective_id=0, has_side_effects=True, vmem_limit_bytes=32 * 1024 * 1024
        ),
        name="gather",
    )(q, do, k, v)


def scatter_kernel(
    z_size, heads,
    rows_in, dkv_in, rows_out, pieces_out,
    part, twin_part, right_part, left_part, cross_part, final,
    row_send, row_recv, piece_send, piece_recv, ring_send, right_recv, left_recv,
    cross_recv, twin_send, twin_recv, local_sem,
):
    ctx, head, x, z, core = place(z_size)
    group = 2 * heads
    base = ctx - core
    mine = core * heads + head
    wide = rows_in.shape[3]

    def index(x_at, z_at):
        return (x_at * z_size + z_at) * 2 + core

    right, left = index(x, (z + 1) % z_size), index(x, (z + z_size - 1) % z_size)
    over_right, over_left = index(1 - x, (z + 1) % z_size), index(1 - x, (z + z_size - 1) % z_size)
    cross, twin = index(1 - x, z), base + 1 - core
    meet(group, ctx, head, core, heads, (right, left, cross, over_right, over_left))

    far = z_size // 2
    reach = ((far, far - 1), (far - 1, far))
    steps = []
    for back in range(far):
        for plane, way in ((0, 0), (1, 1), (1, 0), (0, 1)):
            d = reach[plane][way] - back
            if d > 0:
                steps.append((plane, way, d, back))

    to_twin = [far] + [s * d for d in range(far - 1, 0, -1) for s in (1, -1)]
    to_twin.insert(3, 0)
    place_of = {offset: n for n, offset in enumerate(to_twin)}
    fed, had = [0], [0]

    def z_of(offset):
        return (z + z_size + offset) % z_size

    def feed_twin(count):
        for n in range(fed[0], min(fed[0] + count, len(to_twin))):
            at = z_of(to_twin[n])
            send(dkv_in.at[:, at, 1 - core], twin_part.at[:, at], twin_send, twin_recv.at[n], twin, head)
        fed[0] = min(fed[0] + count, len(to_twin))

    def need_twin(offset):
        n = place_of[far if abs(offset) == far else offset]
        while had[0] <= n:
            arrived(twin_part.at[:, z_of(to_twin[had[0]])], twin_recv.at[had[0]])
            had[0] += 1

    feed_twin(3)
    my_rows = pl.ds(pl.multiple_of((head * 2 + core) * wide, WIDTH), wide)

    def send_row(step, _):
        peer = (mine + step) % group
        send(
            rows_in.at[peer], rows_out.at[:, :, my_rows], row_send, row_recv,
            base + peer // heads, peer % heads,
        )
        return 0

    rows_sent = [1]

    def send_rows(count):
        stop = min(rows_sent[0] + count, group)
        lax.fori_loop(rows_sent[0], stop, send_row, 0)
        rows_sent[0] = stop

    own_rows = pltpu.make_async_copy(rows_in.at[mine], rows_out.at[:, :, my_rows], local_sem.at[0])
    own_rows.start()

    def combine(at_x, at_z, extras, last=False):
        def add_half(side, _):
            total = dkv_in[at_x, at_z, core, side].astype(jnp.float32)
            total = total + twin_part[at_x, at_z, side].astype(jnp.float32)
            for ref, at in extras:
                total = total + ref[at + (side,)].astype(jnp.float32)
            if last:
                final[side] = total.T.astype(final.dtype).reshape(final.shape[1:])
            else:
                part[at_x, at_z, side] = total.astype(part.dtype)
            return 0

        lax.fori_loop(0, 2, add_half, 0)

    sent = []
    for n, (plane, way, d, back) in enumerate(steps):
        offset = d if way == 0 else -d
        at_x, at_z = (x if plane == 0 else 1 - x), z_of(offset)
        recv, buf, to, over = (
            (right_recv, right_part, right, over_right), (left_recv, left_part, left, over_left)
        )[way]
        if plane == 1 and d == 1:
            to = over
        need_twin(offset)
        extras = []
        if back > 0:
            arrived(buf.at[plane, back - 1], recv.at[plane, back - 1])
            extras = [(buf, (plane, back - 1))]
        combine(at_x, at_z, extras)
        send(part.at[at_x, at_z], buf.at[plane, back], ring_send.at[n], recv.at[plane, back], to, head)
        sent.append((part.at[at_x, at_z], ring_send.at[n]))
        if n % 2 == 0:
            feed_twin(1)
        send_rows(1)
        if n == min(5, len(steps) - 1):
            need_twin(0)
            combine(1 - x, z, [])
            sem = ring_send.at[len(steps)]
            send(part.at[1 - x, z], cross_part.at[0], sem, cross_recv, cross, head)
            sent.append((part.at[1 - x, z], sem))
    feed_twin(len(to_twin))
    send_rows(group)
    extras = [(cross_part, (0,))]
    arrived(cross_part.at[0], cross_recv)
    for plane in range(2):
        for way, (buf, recv) in enumerate(((right_part, right_recv), (left_part, left_recv))):
            at = reach[plane][way] - 1
            arrived(buf.at[plane, at], recv.at[plane, at])
            extras.append((buf, (plane, at)))
    combine(x, z, extras, last=True)

    my_cols = pl.ds(pl.multiple_of(head * WIDTH, WIDTH), WIDTH)

    def send_pieces(step, _):
        peer = (head + step) % heads
        send(final.at[:, peer], pieces_out.at[:, :, my_cols], piece_send, piece_recv, ctx, peer)
        return 0

    lax.fori_loop(1, heads, send_pieces, 0)
    own_piece = pltpu.make_async_copy(final.at[:, head], pieces_out.at[:, :, my_cols], local_sem.at[1])
    own_piece.start()
    own_piece.wait()
    own_rows.wait()
    for what, sem in sent:
        arrived(what, sem)
    arrived(part, twin_send)
    rows = rows_out.at[:, :, pl.ds(0, (group - 1) * wide)]
    arrived(rows, row_send)
    arrived(rows, row_recv)
    arrived(final.at[:, pl.ds(0, heads - 1)], piece_send)
    arrived(pieces_out.at[:, :, pl.ds(0, (heads - 1) * WIDTH)], piece_recv)


def scatter(rows, dkv, z_size, heads):
    group, _, tokens, wide = rows.shape
    far = z_size // 2
    block = dkv.shape[3:]
    here = pl.BlockSpec(memory_space=pltpu.VMEM)
    dma = pltpu.SemaphoreType.DMA
    return pl.pallas_call(
        functools.partial(scatter_kernel, z_size, heads),
        out_shape=(
            jax.ShapeDtypeStruct((2, tokens, group * wide), rows.dtype),
            jax.ShapeDtypeStruct((2, tokens, heads * WIDTH), rows.dtype),
        ),
        in_specs=[here] * 2,
        out_specs=(here, here),
        scratch_shapes=[
            pltpu.VMEM((2, z_size) + block, dkv.dtype),
            pltpu.VMEM((2, z_size) + block, dkv.dtype),
            pltpu.VMEM((2, far) + block, dkv.dtype),
            pltpu.VMEM((2, far) + block, dkv.dtype),
            pltpu.VMEM((1,) + block, dkv.dtype),
            pltpu.VMEM((2, heads, tokens, WIDTH), dkv.dtype),
            dma, dma, dma, dma, dma((4 * far - 2 + 1,)), dma((2, far)), dma((2, far)),
            dma, dma, dma((z_size,)), dma((2,)),
        ],
        compiler_params=pltpu.CompilerParams(
            collective_id=1, has_side_effects=True, vmem_limit_bytes=24 * 1024 * 1024
        ),
        name="scatter",
    )(rows, dkv)


def settle_kernel(rows, pieces, o, dq, dk, dv, sem):
    copies = []
    for src, outs in ((rows, (o, dq)), (pieces, (dk, dv))):
        for n, out in enumerate(outs):
            copies.append(pltpu.make_async_copy(src.at[n], out, sem.at[len(copies)]))
            copies[-1].start()
    for copy in copies:
        copy.wait()


def settle(arrays):
    hbm = pl.BlockSpec(memory_space=pl.ANY)
    here = pl.BlockSpec(memory_space=pltpu.VMEM)
    return pl.pallas_call(
        settle_kernel,
        out_shape=tuple(jax.ShapeDtypeStruct(a.shape[1:], a.dtype) for a in arrays for _ in range(2)),
        in_specs=[here] * len(arrays),
        out_specs=(hbm,) * 4,
        scratch_shapes=[pltpu.SemaphoreType.DMA((4,))],
        compiler_params=pltpu.CompilerParams(vmem_limit_bytes=32 * 1024 * 1024),
        name="settle",
    )(*arrays)


def per_device(heads, z_size, queries, keys, values, output_gradient, doc_lengths, span_of):
    queries, output_gradient, keys, values, doc_lengths, span_of = (
        pltpu.with_memory_space_constraint(a, pltpu.HBM)
        for a in (queries, output_gradient, keys, values, doc_lengths, span_of)
    )
    rows, kv = gather(queries, output_gradient, keys, values, z_size, heads)
    outs, dkv = attention(rows, kv.reshape(N_CTX, 2, SPAN, WIDTH), span_of, doc_lengths)
    return settle(scatter(outs, dkv.reshape((2, z_size, 2) + dkv.shape[1:]), z_size, heads))


def solution(mesh):
    shard = P(("ctx", "head"), None)
    return jax.shard_map(
        functools.partial(per_device, mesh.shape["head"], N_CTX // 4),
        mesh=mesh,
        in_specs=(shard, shard, shard, shard, P(), P()),
        out_specs=(shard, shard, shard, shard),
        check_vma=False,
    )
```

```python
import functools
import math

import jax
import jax.numpy as jnp
from jax import lax
from jax.experimental import pallas as pl
from jax.experimental.pallas import tpu as pltpu
from jax.sharding import PartitionSpec as P

N_CTX = 32
SPAN = 256
WIDTH = 128
UNIT_HEADS = 4
UNITS = 2
MAX_BLOCKS = 18
COLS = UNIT_HEADS * SPAN
LIMIT = 2.0**60
SCALE = WIDTH**-0.5
LOG2_SCALE = SCALE * math.log2(math.e)
NEG = -1e30


NT = (((1,), (1,)), ((), ()))


def attention_kernel(
    span_hbm, len_hbm, rows_v, kv_v,
    out_v, dkv_v,
    holder, slots, acc, probs, grads, wide_buf,
    q_t, do_t, q_s, do_s, o_acc, dq_acc, level_b, delta_b, starts,
    span_ref, len_ref, table_sem,
):
    load_span = pltpu.make_async_copy(span_hbm, span_ref, table_sem.at[0])
    load_len = pltpu.make_async_copy(len_hbm, len_ref, table_sem.at[1])
    load_span.start()
    load_len.start()
    ctx = lax.axis_index("ctx")
    first_unit = ctx - ctx % UNITS

    def clear(c, _):
        acc[c] = jnp.zeros((2, WIDTH, SPAN), jnp.float32)
        return 0

    lax.fori_loop(0, N_CTX, clear, 0)

    load_span.wait()
    load_len.wait()

    def note(c, _):
        holder[span_ref[c]] = c
        return 0

    lax.fori_loop(0, N_CTX, note, 0)

    ends = []
    running = jnp.int32(0)
    for j in range(4):
        running = running + len_ref[j]
        ends.append(running)

    def doc_start(pos):
        start = jnp.zeros_like(pos)
        for end in ends:
            start = jnp.where(pos >= end, end, start)
        return start

    def rows_of(h):
        return pl.ds(h * SPAN, SPAN)

    def lanes_of(h):
        return pl.ds(h * WIDTH, WIDTH)

    def both(x):
        return jnp.concatenate([x, x], axis=1)

    def beside(parts):
        return parts[0] if len(parts) == 1 else jnp.concatenate(parts, axis=1)

    def below(parts):
        return parts[0] if len(parts) == 1 else jnp.concatenate(parts, axis=0)

    ones = jnp.ones((SPAN, WIDTH), jnp.bfloat16)

    def unit(u, _):
        group = rows_v.shape[0] // UNITS
        own = pl.ds(pl.multiple_of(u * group, group), group)

        def head_rows(side, h):
            return rows_v[own, side, :, lanes_of(h)].reshape(SPAN, WIDTH)

        def put_rows(side, h, value):
            out_v[own, side, :, lanes_of(h)] = value.astype(jnp.bfloat16).reshape(group, SPAN // group, WIDTH)

        span = span_ref[first_unit + u]
        first_pos = span * SPAN
        first_block = doc_start(first_pos) // SPAN
        last_start = doc_start(first_pos + (SPAN - 1))
        blocks = span - first_block + 1
        edges = jnp.maximum(jnp.minimum((last_start + (SPAN - 1)) // SPAN, span) - first_block, 0)
        starts[...] = doc_start(first_pos + lax.broadcasted_iota(jnp.int32, (SPAN, WIDTH), 0))

        for h in range(UNIT_HEADS):
            q_h = head_rows(0, h)
            q_s[rows_of(h)] = q_h
            q_t[:, rows_of(h)] = q_h.T

        def allowed_at(t):
            k_pos = t * SPAN + lax.broadcasted_iota(jnp.int32, (SPAN, SPAN), 1)
            q_pos = first_pos + lax.broadcasted_iota(jnp.int32, (SPAN, SPAN), 0)
            return (k_pos <= q_pos) & (k_pos >= both(starts[...]))

        def halves_max(s):
            return jnp.maximum(s[:, :WIDTH], s[:, WIDTH:])

        def row_max(x):
            return jnp.broadcast_to(jnp.max(x, axis=1, keepdims=True), x.shape)

        def score(slot, count):
            for n in range(count):
                wide_buf[n] = lax.dot_general(
                    q_s[...], kv_v[slots[slot + n], 0], NT, preferred_element_type=jnp.float32
                )

        def weigh(slot, count, allowed=None, take_top=False):
            for n in range(count):
                for h in range(UNIT_HEADS):
                    s = wide_buf[n, rows_of(h)]
                    if allowed is not None:
                        s = jnp.where(allowed, s, NEG)
                    if take_top:
                        level = row_max(halves_max(s))
                        level_b[rows_of(h)] = level
                    else:
                        level = level_b[rows_of(h)]
                    p = jnp.exp2((s - both(level)) * LOG2_SCALE)
                    probs[slot + n, rows_of(h)] = p.astype(jnp.bfloat16)

        def attend(slot, count):
            values = below([beside([kv_v[slots[slot + n], 1], ones]) for n in range(count)])
            o_acc[...] += jnp.dot(
                beside([probs[slot + n] for n in range(count)]), values, preferred_element_type=jnp.float32
            )

        def masked_step(i, _):
            score(i, 1)
            weigh(i, 1, allowed_at(first_block + i - 2))
            return 0

        def attend_step(i, _):
            attend(i, 1)
            return 0

        inner_from = edges + 2
        inner = blocks - 1 - edges
        slots[0] = first_unit
        slots[1] = holder[span]

        def place_slot(i, _):
            slots[i + 2] = holder[first_block + i]
            return 0

        lax.fori_loop(0, blocks - 1, place_slot, 0)
        probs[0] = jnp.zeros((COLS, SPAN), jnp.bfloat16)
        o_acc[...] = jnp.zeros_like(o_acc)
        score(1, 1)
        weigh(1, 1, allowed_at(span), take_top=True)
        lax.fori_loop(2, inner_from, masked_step, 0)
        lax.fori_loop(1, edges, attend_step, 0)

        def pair_step(j, _):
            slot = inner_from + 2 * j
            score(slot, 2)
            attend(slot - 2, 2)
            weigh(slot, 2)
            return 0

        lax.fori_loop(0, inner // 2, pair_step, 0)
        last = inner_from + inner - inner % 2

        @pl.when(inner % 2 == 1)
        def _():
            score(last, 1)
            attend(last - 2, 2)
            weigh(last, 1)
            attend(last, 1)

        @pl.when(inner % 2 == 0)
        def _():
            attend(last - 2, 2)

        worst = jnp.max(jnp.where(o_acc[:, WIDTH:] < LIMIT, 0.0, 1.0))

        @pl.when(worst > 0.0)
        def _():
            o_acc[...] = jnp.zeros_like(o_acc)
            level_b[...] = jnp.full_like(level_b, NEG)

            def top_step(i, _):
                k = kv_v[slots[i], 0]
                allowed = allowed_at(jnp.where(i == 1, span, first_block + i - 2))
                for h in range(UNIT_HEADS):
                    s = lax.dot_general(q_s[rows_of(h)], k, NT, preferred_element_type=jnp.float32)
                    s = jnp.where(allowed, s, NEG)
                    level_b[rows_of(h)] = jnp.maximum(level_b[rows_of(h)], halves_max(s))
                return 0

            lax.fori_loop(1, blocks + 1, top_step, 0)
            for h in range(UNIT_HEADS):
                level_b[rows_of(h)] = row_max(level_b[rows_of(h)])
            score(1, 1)
            weigh(1, 1, allowed_at(span))
            lax.fori_loop(2, blocks + 1, masked_step, 0)
            lax.fori_loop(1, blocks + 1, attend_step, 0)

        for h in range(UNIT_HEADS):
            inverse = 1.0 / o_acc[rows_of(h), WIDTH:]
            out = (o_acc[rows_of(h), :WIDTH] * inverse).astype(jnp.bfloat16)
            put_rows(0, h, out)
            scaled = (head_rows(1, h).astype(jnp.float32) * inverse).astype(jnp.bfloat16)
            do_s[rows_of(h)] = scaled
            do_t[:, rows_of(h)] = scaled.T
            delta = jnp.sum(scaled.astype(jnp.float32) * out.astype(jnp.float32), axis=1, keepdims=True)
            delta_b[rows_of(h)] = jnp.broadcast_to(delta, (SPAN, WIDTH))
        dq_acc[...] = jnp.zeros_like(dq_acc)

        def backward(i, count):
            places = [slots[i + n] for n in range(count)]
            for n, c in enumerate(places):
                wide_buf[n] = lax.dot_general(
                    do_s[...], kv_v[c, 1], NT, preferred_element_type=jnp.float32
                )
            dv = jnp.dot(
                do_t[...], beside([probs[i + n] for n in range(count)]), preferred_element_type=jnp.float32
            )
            for n, c in enumerate(places):
                acc[c, 1] += dv[:, n * SPAN : (n + 1) * SPAN]
            for n in range(count):
                for h in range(UNIT_HEADS):
                    p = probs[i + n, rows_of(h)].astype(jnp.float32)
                    ds = p * (wide_buf[n, rows_of(h)] - both(delta_b[rows_of(h)]))
                    grads[n, rows_of(h)] = ds.astype(jnp.bfloat16)
            ds = beside([grads[n] for n in range(count)])
            dk = jnp.dot(q_t[...], ds, preferred_element_type=jnp.float32)
            dq_acc[...] += jnp.dot(
                ds, below([kv_v[c, 0] for c in places]), preferred_element_type=jnp.float32
            )
            for n, c in enumerate(places):
                acc[c, 0] += dk[:, n * SPAN : (n + 1) * SPAN]

        def grad_step(j, _):
            backward(2 * j + 1, 2)
            return 0

        lax.fori_loop(0, blocks // 2, grad_step, 0)

        @pl.when(blocks % 2 == 1)
        def _():
            backward(blocks, 1)

        for h in range(UNIT_HEADS):
            put_rows(1, h, dq_acc[rows_of(h)] * SCALE)
        return 0

    lax.fori_loop(0, UNITS, unit, 0)

    def pack(c, _):
        dkv_v[c, 0] = (acc[c, 0] * SCALE).astype(jnp.bfloat16)
        dkv_v[c, 1] = acc[c, 1].astype(jnp.bfloat16)
        return 0

    lax.fori_loop(0, N_CTX, pack, 0)


def attention(rows, kv, span_of, doc_lengths):
    blocks = jax.ShapeDtypeStruct((N_CTX, 2, WIDTH, SPAN), jnp.bfloat16)
    table = pl.BlockSpec(memory_space=pltpu.HBM)
    here = pl.BlockSpec(memory_space=pltpu.VMEM)
    vmem = pltpu.VMEM
    return pl.pallas_call(
        attention_kernel,
        out_shape=(jax.ShapeDtypeStruct(rows.shape, rows.dtype), blocks),
        in_specs=[table, table, here, here],
        out_specs=(here, here),
        scratch_shapes=[
            pltpu.SMEM((N_CTX,), jnp.int32),
            pltpu.SMEM((MAX_BLOCKS,), jnp.int32),
            vmem(blocks.shape, jnp.float32),
            vmem((MAX_BLOCKS, COLS, SPAN), jnp.bfloat16),
            vmem((2, COLS, SPAN), jnp.bfloat16),
            vmem((2, COLS, SPAN), jnp.float32),
            vmem((WIDTH, COLS), jnp.bfloat16),
            vmem((WIDTH, COLS), jnp.bfloat16),
            vmem((COLS, WIDTH), jnp.bfloat16),
            vmem((COLS, WIDTH), jnp.bfloat16),
            vmem((COLS, 2 * WIDTH), jnp.float32),
            vmem((COLS, WIDTH), jnp.float32),
            vmem((COLS, WIDTH), jnp.float32),
            vmem((COLS, WIDTH), jnp.float32),
            vmem((SPAN, WIDTH), jnp.int32),
            pltpu.SMEM((N_CTX,), jnp.int32),
            pltpu.SMEM((4,), jnp.int32),
            pltpu.SemaphoreType.DMA((2,)),
        ],
        compiler_params=pltpu.CompilerParams(vmem_limit_bytes=40 * 1024 * 1024),
        name="attention",
    )(span_of, doc_lengths, rows, kv)


MESH_IDS = pl.DeviceIdType.MESH


def place(z_size):
    ctx, head = lax.axis_index("ctx"), lax.axis_index("head")
    return ctx, head, ctx // (2 * z_size), (ctx // 2) % z_size, ctx % 2


def meet(group, ctx, head, core, heads, others):
    barrier = pltpu.get_barrier_semaphore()
    base = ctx - core

    def greet(step, _):
        peer = (core * heads + head + step) % group
        pl.semaphore_signal(
            barrier, inc=1, device_id=(base + peer // heads, peer % heads), device_id_type=MESH_IDS
        )
        return 0

    lax.fori_loop(1, group, greet, 0)
    for other in others:
        pl.semaphore_signal(barrier, inc=1, device_id=(other, head), device_id_type=MESH_IDS)
    pl.semaphore_wait(barrier, group - 1 + len(others))


def arrived(ref, sem):
    pltpu.make_async_copy(ref, ref, sem).wait()


def send(src, dst, send_sem, recv_sem, ctx, head):
    pltpu.make_async_remote_copy(
        src_ref=src, dst_ref=dst, send_sem=send_sem, recv_sem=recv_sem,
        device_id=(ctx, head), device_id_type=MESH_IDS,
    ).start()


def gather_kernel(
    z_size, heads,
    q_hbm, do_hbm, k_hbm, v_hbm, rows_out, kv_out, rows_in, pieces_in,
    row_send, row_recv, piece_send, piece_recv, ring_send, right_recv, left_recv,
    cross_recv, twin_send, twin_recv, local_sem, load_sem,
):
    loads = []
    for n, (src, dst) in enumerate((
        (k_hbm, pieces_in.at[0]), (v_hbm, pieces_in.at[1]), (q_hbm, rows_in.at[0]), (do_hbm, rows_in.at[1])
    )):
        loads.append(pltpu.make_async_copy(src, dst, load_sem.at[n]))
        loads[-1].start()
    ctx, head, x, z, core = place(z_size)
    group = 2 * heads
    base = ctx - core
    mine = core * heads + head
    wide = rows_in.shape[2] // group

    def index(x_at, z_at):
        return (x_at * z_size + z_at) * 2 + core

    def block(x_at, z_at):
        return kv_out.at[x_at, z_at * 2 + core]

    right_z, left_z = (z + 1) % z_size, (z + z_size - 1) % z_size
    right, left = index(x, right_z), index(x, left_z)
    cross, twin = index(1 - x, z), base + 1 - core
    meet(group, ctx, head, core, heads, (right, left, cross))

    def piece_cols(at):
        return pl.ds(pl.multiple_of(at * WIDTH, WIDTH), WIDTH)

    def row_cols(at):
        peer_core, peer_head = at // heads, at % heads
        return pl.ds(pl.multiple_of((peer_head * 2 + peer_core) * wide, WIDTH), wide)

    mine_block = block(x, z)

    def send_pieces(step, _):
        peer = (head + step) % heads
        send(pieces_in.at[:, :, piece_cols(peer)], mine_block.at[:, head], piece_send, piece_recv, ctx, peer)
        return 0

    loads[0].wait()
    loads[1].wait()
    lax.fori_loop(1, heads, send_pieces, 0)
    own_piece = pltpu.make_async_copy(
        pieces_in.at[:, :, piece_cols(head)], mine_block.at[:, head], local_sem.at[0]
    )
    own_piece.start()
    loads[2].wait()
    loads[3].wait()
    own_rows = pltpu.make_async_copy(rows_in.at[:, :, row_cols(mine)], rows_out.at[mine], local_sem.at[1])
    own_rows.start()

    def send_row(step, _):
        peer = (mine + step) % group
        send(
            rows_in.at[:, :, row_cols(peer)], rows_out.at[mine], row_send, row_recv,
            base + peer // heads, peer % heads,
        )
        return 0

    rows_sent = [1]

    def send_rows(count):
        stop = min(rows_sent[0] + count, group)
        lax.fori_loop(rows_sent[0], stop, send_row, 0)
        rows_sent[0] = stop

    send_rows(2)
    own_piece.wait()
    pieces = mine_block.at[:, pl.ds(0, heads - 1)]
    arrived(pieces, piece_recv)

    sent = []

    def forward(what, to, recv):
        sem = ring_send.at[len(sent)]
        send(what, what, sem, recv, to, head)
        sent.append((what, sem))

    def share(z_at):
        both_x = kv_out.at[:, z_at * 2 + core]
        send(both_x, both_x, twin_send, twin_recv, twin, head)

    far = z_size // 2
    reach = ((far, far - 1), (far - 1, far))
    forward(mine_block, cross, cross_recv)
    forward(mine_block, right, right_recv.at[0, 0])
    forward(mine_block, left, left_recv.at[0, 0])
    send_rows(2)
    cross_block = block(1 - x, z)
    arrived(cross_block, cross_recv)
    forward(cross_block, right, right_recv.at[1, 0])
    forward(cross_block, left, left_recv.at[1, 0])
    share(z)
    for d in range(1, far + 1):
        for plane in range(2):
            at_x = x if plane == 0 else 1 - x
            for way in range(2):
                if d > reach[plane][way]:
                    continue
                recv, to = ((right_recv, right), (left_recv, left))[way]
                origin = (z + z_size - d) % z_size if way == 0 else (z + d) % z_size
                what = block(at_x, origin)
                arrived(what, recv.at[plane, d - 1])
                if d < reach[plane][way]:
                    forward(what, to, recv.at[plane, d])
                if d == far:
                    send(what, what, twin_send, twin_recv, twin, head)
                elif plane == 1:
                    share(origin)
                send_rows(1)

    send_rows(group)
    arrived(pieces, piece_send)
    for what, sem in sent:
        arrived(what, sem)
    arrived(kv_out.at[0], twin_send)
    arrived(kv_out.at[0], twin_recv)
    own_rows.wait()
    rows = rows_out.at[pl.ds(0, group - 1)]
    arrived(rows, row_send)
    arrived(rows, row_recv)


def gather(q, do, k, v, z_size, heads):
    tokens = q.shape[0]
    group = 2 * heads
    far = z_size // 2
    rows = jax.ShapeDtypeStruct((group, 2, tokens, q.shape[1] // group), q.dtype)
    kv = jax.ShapeDtypeStruct((2, 2 * z_size, 2, heads, tokens, WIDTH), q.dtype)
    hbm = pl.BlockSpec(memory_space=pltpu.HBM)
    here = pl.BlockSpec(memory_space=pltpu.VMEM)
    dma = pltpu.SemaphoreType.DMA
    return pl.pallas_call(
        functools.partial(gather_kernel, z_size, heads),
        out_shape=(rows, kv),
        in_specs=[hbm] * 4,
        out_specs=(here, here),
        scratch_shapes=[
            pltpu.VMEM((2,) + q.shape, q.dtype), pltpu.VMEM((2,) + k.shape, k.dtype),
            dma, dma, dma, dma, dma((4 * far - 2 + 1,)), dma((2, far)), dma((2, far)),
            dma, dma, dma, dma((2,)), dma((4,)),
        ],
        compiler_params=pltpu.CompilerParams(
            collective_id=0, has_side_effects=True, vmem_limit_bytes=32 * 1024 * 1024
        ),
        name="gather",
    )(q, do, k, v)


def scatter_kernel(
    z_size, heads,
    rows_in, dkv_in, rows_out, pieces_out,
    part, twin_part, right_part, left_part, cross_part, final,
    row_send, row_recv, piece_send, piece_recv, ring_send, right_recv, left_recv,
    cross_recv, twin_send, twin_recv, local_sem,
):
    ctx, head, x, z, core = place(z_size)
    group = 2 * heads
    base = ctx - core
    mine = core * heads + head
    wide = rows_in.shape[3]

    def index(x_at, z_at):
        return (x_at * z_size + z_at) * 2 + core

    right, left = index(x, (z + 1) % z_size), index(x, (z + z_size - 1) % z_size)
    over_right, over_left = index(1 - x, (z + 1) % z_size), index(1 - x, (z + z_size - 1) % z_size)
    cross, twin = index(1 - x, z), base + 1 - core
    meet(group, ctx, head, core, heads, (right, left, cross, over_right, over_left))

    far = z_size // 2
    reach = ((far, far - 1), (far - 1, far))
    steps = []
    for back in range(far):
        for plane, way in ((0, 0), (1, 1), (1, 0), (0, 1)):
            d = reach[plane][way] - back
            if d > 0:
                steps.append((plane, way, d, back))

    to_twin = [far] + [s * d for d in range(far - 1, 0, -1) for s in (1, -1)]
    to_twin.insert(3, 0)
    place_of = {offset: n for n, offset in enumerate(to_twin)}
    fed, had = [0], [0]

    def z_of(offset):
        return (z + z_size + offset) % z_size

    def feed_twin(count):
        for n in range(fed[0], min(fed[0] + count, len(to_twin))):
            at = z_of(to_twin[n])
            send(dkv_in.at[:, at, 1 - core], twin_part.at[:, at], twin_send, twin_recv.at[n], twin, head)
        fed[0] = min(fed[0] + count, len(to_twin))

    def need_twin(offset):
        n = place_of[far if abs(offset) == far else offset]
        while had[0] <= n:
            arrived(twin_part.at[:, z_of(to_twin[had[0]])], twin_recv.at[had[0]])
            had[0] += 1

    feed_twin(3)
    my_rows = pl.ds(pl.multiple_of((head * 2 + core) * wide, WIDTH), wide)

    def send_row(step, _):
        peer = (mine + step) % group
        send(
            rows_in.at[peer], rows_out.at[:, :, my_rows], row_send, row_recv,
            base + peer // heads, peer % heads,
        )
        return 0

    rows_sent = [1]

    def send_rows(count):
        stop = min(rows_sent[0] + count, group)
        lax.fori_loop(rows_sent[0], stop, send_row, 0)
        rows_sent[0] = stop

    own_rows = pltpu.make_async_copy(rows_in.at[mine], rows_out.at[:, :, my_rows], local_sem.at[0])
    own_rows.start()

    def combine(at_x, at_z, extras, last=False):
        def add_half(side, _):
            total = dkv_in[at_x, at_z, core, side].astype(jnp.float32)
            total = total + twin_part[at_x, at_z, side].astype(jnp.float32)
            for ref, at in extras:
                total = total + ref[at + (side,)].astype(jnp.float32)
            if last:
                final[side] = total.T.astype(final.dtype).reshape(final.shape[1:])
            else:
                part[at_x, at_z, side] = total.astype(part.dtype)
            return 0

        lax.fori_loop(0, 2, add_half, 0)

    sent = []
    for n, (plane, way, d, back) in enumerate(steps):
        offset = d if way == 0 else -d
        at_x, at_z = (x if plane == 0 else 1 - x), z_of(offset)
        recv, buf, to, over = (
            (right_recv, right_part, right, over_right), (left_recv, left_part, left, over_left)
        )[way]
        if plane == 1 and d == 1:
            to = over
        need_twin(offset)
        extras = []
        if back > 0:
            arrived(buf.at[plane, back - 1], recv.at[plane, back - 1])
            extras = [(buf, (plane, back - 1))]
        combine(at_x, at_z, extras)
        send(part.at[at_x, at_z], buf.at[plane, back], ring_send.at[n], recv.at[plane, back], to, head)
        sent.append((part.at[at_x, at_z], ring_send.at[n]))
        if n % 2 == 0:
            feed_twin(1)
        send_rows(1)
        if n == min(5, len(steps) - 1):
            need_twin(0)
            combine(1 - x, z, [])
            sem = ring_send.at[len(steps)]
            send(part.at[1 - x, z], cross_part.at[0], sem, cross_recv, cross, head)
            sent.append((part.at[1 - x, z], sem))
    feed_twin(len(to_twin))
    send_rows(group)
    extras = [(cross_part, (0,))]
    arrived(cross_part.at[0], cross_recv)
    for plane in range(2):
        for way, (buf, recv) in enumerate(((right_part, right_recv), (left_part, left_recv))):
            at = reach[plane][way] - 1
            arrived(buf.at[plane, at], recv.at[plane, at])
            extras.append((buf, (plane, at)))
    combine(x, z, extras, last=True)

    my_cols = pl.ds(pl.multiple_of(head * WIDTH, WIDTH), WIDTH)

    def send_pieces(step, _):
        peer = (head + step) % heads
        send(final.at[:, peer], pieces_out.at[:, :, my_cols], piece_send, piece_recv, ctx, peer)
        return 0

    lax.fori_loop(1, heads, send_pieces, 0)
    own_piece = pltpu.make_async_copy(final.at[:, head], pieces_out.at[:, :, my_cols], local_sem.at[1])
    own_piece.start()
    own_piece.wait()
    own_rows.wait()
    for what, sem in sent:
        arrived(what, sem)
    arrived(part, twin_send)
    rows = rows_out.at[:, :, pl.ds(0, (group - 1) * wide)]
    arrived(rows, row_send)
    arrived(rows, row_recv)
    arrived(final.at[:, pl.ds(0, heads - 1)], piece_send)
    arrived(pieces_out.at[:, :, pl.ds(0, (heads - 1) * WIDTH)], piece_recv)


def scatter(rows, dkv, z_size, heads):
    group, _, tokens, wide = rows.shape
    far = z_size // 2
    block = dkv.shape[3:]
    here = pl.BlockSpec(memory_space=pltpu.VMEM)
    dma = pltpu.SemaphoreType.DMA
    return pl.pallas_call(
        functools.partial(scatter_kernel, z_size, heads),
        out_shape=(
            jax.ShapeDtypeStruct((2, tokens, group * wide), rows.dtype),
            jax.ShapeDtypeStruct((2, tokens, heads * WIDTH), rows.dtype),
        ),
        in_specs=[here] * 2,
        out_specs=(here, here),
        scratch_shapes=[
            pltpu.VMEM((2, z_size) + block, dkv.dtype),
            pltpu.VMEM((2, z_size) + block, dkv.dtype),
            pltpu.VMEM((2, far) + block, dkv.dtype),
            pltpu.VMEM((2, far) + block, dkv.dtype),
            pltpu.VMEM((1,) + block, dkv.dtype),
            pltpu.VMEM((2, heads, tokens, WIDTH), dkv.dtype),
            dma, dma, dma, dma, dma((4 * far - 2 + 1,)), dma((2, far)), dma((2, far)),
            dma, dma, dma((z_size,)), dma((2,)),
        ],
        compiler_params=pltpu.CompilerParams(
            collective_id=1, has_side_effects=True, vmem_limit_bytes=24 * 1024 * 1024
        ),
        name="scatter",
    )(rows, dkv)


def settle_kernel(rows, pieces, o, dq, dk, dv, sem):
    copies = []
    for src, outs in ((rows, (o, dq)), (pieces, (dk, dv))):
        for n, out in enumerate(outs):
            copies.append(pltpu.make_async_copy(src.at[n], out, sem.at[len(copies)]))
            copies[-1].start()
    for copy in copies:
        copy.wait()


def settle(arrays):
    hbm = pl.BlockSpec(memory_space=pl.ANY)
    here = pl.BlockSpec(memory_space=pltpu.VMEM)
    return pl.pallas_call(
        settle_kernel,
        out_shape=tuple(jax.ShapeDtypeStruct(a.shape[1:], a.dtype) for a in arrays for _ in range(2)),
        in_specs=[here] * len(arrays),
        out_specs=(hbm,) * 4,
        scratch_shapes=[pltpu.SemaphoreType.DMA((4,))],
        compiler_params=pltpu.CompilerParams(vmem_limit_bytes=32 * 1024 * 1024),
        name="settle",
    )(*arrays)


def per_device(heads, z_size, queries, keys, values, output_gradient, doc_lengths, span_of):
    queries, output_gradient, keys, values, doc_lengths, span_of = (
        pltpu.with_memory_space_constraint(a, pltpu.HBM)
        for a in (queries, output_gradient, keys, values, doc_lengths, span_of)
    )
    rows, kv = gather(queries, output_gradient, keys, values, z_size, heads)
    outs, dkv = attention(rows, kv.reshape(N_CTX, 2, SPAN, WIDTH), span_of, doc_lengths)
    return settle(scatter(outs, dkv.reshape((2, z_size, 2) + dkv.shape[1:]), z_size, heads))


def solution(mesh):
    shard = P(("ctx", "head"), None)
    return jax.shard_map(
        functools.partial(per_device, mesh.shape["head"], N_CTX // 4),
        mesh=mesh,
        in_specs=(shard, shard, shard, shard, P(), P()),
        out_specs=(shard, shard, shard, shard),
        check_vma=False,
    )
```
